32 devices in a mesh: ctx: 32 (over z, y, x, core).
Axes of the slice: x: 2, y: 2, z: 4, core: 2. Of those that a mesh axis runs over, the one named last changes fastest.
Arguments:
- query: bfloat16 [8192, 1280], P('ctx'), may hold values from -16 to 16
- key: bfloat16 [8192, 1280], P('ctx'), may hold values from -16 to 16
- value: bfloat16 [8192, 1280], P('ctx'), may hold values from -6 to 6
- grad_out: bfloat16 [8192, 1280], P('ctx'), may hold values from -16 to 16
- offsets: int32 [2, 10], replicated, may hold values from 0 to 255, as said below
Outputs:
- grad_query: bfloat16 [8192, 1280], P('ctx')
- grad_key: bfloat16 [8192, 1280], P('ctx')
- grad_value: bfloat16 [8192, 1280], P('ctx')
The draws below stay inside these ranges and needn't reach their ends.
Inputs may be any that keep to these rules, and one draw needn't show every extreme that they name: Row 0 holds 0 or 1 for each head, half of the heads taking each; row 1 holds distinct offsets below 256, one of them 256 - 1.
All inputs are finite; a program needn't handle non-finite values.
Results may differ from the reference program's by a relative error of at most 0.007.
Values may be sent and summed in bfloat16 or wider, within the bound.
No kernel may reach another device: no remote copies, remote signals or barrier semaphores. Data moves between devices by JAX's collectives and lax.ppermute only.
A program may use at most 64 MiB of HBM per device.

```python
import math
import jax
import jax.numpy as jnp
from jax import lax

HEADS = 10
DH = 128
TOK_DEV = 256
TOPG = 32
TOKENS = 8192


def draw_query(key, part):
    extent = (TOKENS, HEADS * DH)
    return jnp.clip(jax.random.normal(jax.random.fold_in(key, 11), extent, jnp.float32), -6.0, 6.0).astype(jnp.bfloat16)


def draw_key(key, part):
    extent = (TOKENS, HEADS * DH)
    return jnp.clip(jax.random.normal(jax.random.fold_in(key, 12), extent, jnp.float32), -6.0, 6.0).astype(jnp.bfloat16)


def draw_offsets(key, part):
    pair_offsets = jax.random.permutation(jax.random.fold_in(key, 41), HEADS).astype(jnp.int32) % 2
    far_offsets = jax.random.permutation(jax.random.fold_in(key, 42), TOK_DEV - 1)[:HEADS - 1].astype(jnp.int32)
    far_offsets = jnp.concatenate([far_offsets, jnp.full((1,), TOK_DEV - 1, jnp.int32)])
    far_offsets = jax.random.permutation(jax.random.fold_in(key, 43), far_offsets)
    return jnp.stack([pair_offsets, far_offsets]).astype(jnp.int32)


def level_of(key, shape, cuts, least, top_value):
    gain, own = 1.0, jax.random.fold_in(key, 6)
    for dim, parts in cuts:
        steps = jnp.exp(jax.random.uniform(jax.random.fold_in(own, dim), (parts,), jnp.float32, least / len(cuts), top_value / len(cuts)))
        gain = gain * jnp.repeat(steps, shape[dim] // parts).reshape([-1 if axis == dim else 1 for axis in range(len(shape))])
    return gain


def normal_values(own_key, shape, deviation, limit, shards=(), held_as=jnp.bfloat16):
    level = level_of(own_key, shape, shards, -0.22, 0.18) if shards else 1.0
    drawn = jax.random.normal(own_key, shape, jnp.float32) * deviation * level
    return jnp.minimum(jnp.maximum(drawn, -limit), limit).astype(held_as)


def setup_inputs(seed: int = 0) -> dict:
    arg_keys = jax.random.split(jax.random.key(seed), 6)
    return {
        "query": draw_query(jax.random.fold_in(arg_keys[5], 71), 0),
        "key": draw_key(jax.random.fold_in(arg_keys[5], 71), 0),
        "value": normal_values(arg_keys[2], (TOKENS, HEADS * DH), 1.0, 6.0, ((0, 32),)),
        "grad_out": normal_values(arg_keys[3], (TOKENS, HEADS * DH), 4.0, 16.0, ((0, 32),)),
        "offsets": draw_offsets(jax.random.fold_in(arg_keys[5], 71), 0),
    }


def onehot_table(dilation, offset_row, dtype):
    return (jnp.arange(dilation, dtype=jnp.int32)[:, None] == offset_row[None, :].astype(jnp.int32)).astype(dtype)


def level_select(source, segment_width, dilation, offset_row):
    length, head_count, head_size = source.shape
    selector = onehot_table(dilation, offset_row, source.dtype)
    grouped = source.reshape(length // segment_width, segment_width // dilation, dilation, head_count, head_size)
    return jnp.sum(grouped * selector[None, None, :, :, None], axis=2)


def level_place(source, dilation, offset_row):
    segments, members, head_count, head_size = source.shape
    selector = onehot_table(dilation, offset_row, source.dtype)
    spread = source[:, :, None] * selector[None, None, :, :, None]
    return spread.reshape(segments * members * dilation, head_count, head_size)


def stat_select(source, segment_width, dilation, offset_row):
    head_count, length = source.shape
    selector = onehot_table(dilation, offset_row, source.dtype)
    grouped = source.reshape(head_count, length // segment_width, segment_width // dilation, dilation)
    return jnp.transpose(jnp.sum(grouped * selector.T[:, None, None, :], axis=3), (1, 0, 2))


def stat_place(source, dilation, offset_row):
    segments, head_count, members = source.shape
    selector = onehot_table(dilation, offset_row, source.dtype)
    spread = jnp.transpose(source, (1, 0, 2))[:, :, :, None] * selector.T[:, None, None, :]
    return spread.reshape(head_count, segments * members * dilation)


def segment_map(kernel, operands):
    segments = operands[0].shape[0]
    per_batch = math.gcd(segments, 8)
    batched = tuple(operand.reshape((segments // per_batch, per_batch) + operand.shape[1:]) for operand in operands)
    results = lax.map(lambda member: kernel(*member), batched)
    return tuple(result.reshape((segments,) + result.shape[2:]) for result in results)


def forward_block(queries, keys_in, values_in):
    factor = queries.shape[-1] ** -0.5
    scores = jnp.einsum("gmhc,gnhc->ghmn", queries.astype(jnp.float32), keys_in.astype(jnp.float32)) * factor
    row_peak = jnp.max(scores, axis=-1)
    powered = jnp.exp(scores - row_peak[..., None])
    row_total = jnp.sum(powered, axis=-1)
    rounded = lax.optimization_barrier(powered.astype(jnp.bfloat16)).astype(jnp.float32)
    blended = jnp.einsum("ghmn,gnhc->gmhc", rounded, values_in.astype(jnp.float32))
    return row_peak, row_total, blended


def backward_block(queries, keys_in, values_in, out_grads, log_total, row_delta):
    factor = queries.shape[-1] ** -0.5
    queries_wide = queries.astype(jnp.float32)
    keys_wide = keys_in.astype(jnp.float32)
    values_wide = values_in.astype(jnp.float32)
    grads_wide = out_grads.astype(jnp.float32)
    scores = jnp.einsum("gmhc,gnhc->ghmn", queries_wide, keys_wide) * factor
    chances = jnp.exp(scores - log_total[..., None])
    rounded = lax.optimization_barrier(chances.astype(jnp.bfloat16)).astype(jnp.float32)
    value_grad = jnp.einsum("ghmn,gmhc->gnhc", rounded, grads_wide)
    product_grad = jnp.einsum("gmhc,gnhc->ghmn", grads_wide, values_wide)
    score_grad = (factor * chances * (product_grad - row_delta[..., None])).astype(jnp.bfloat16)
    score_grad = lax.optimization_barrier(score_grad).astype(jnp.float32)
    query_grad = jnp.einsum("ghmn,gnhc->gmhc", score_grad, keys_wide)
    key_grad = jnp.einsum("ghmn,gmhc->gnhc", score_grad, queries_wide)
    return query_grad, key_grad, value_grad


def reference(query, key, value, grad_out, offsets):
    head_count = offsets.shape[1]
    length = query.shape[0]
    head_size = query.shape[1] // head_count
    operands = [operand.reshape(length, head_count, head_size) for operand in (query, key, value, grad_out)]
    plan = ((TOK_DEV, 1, jnp.zeros((head_count,), jnp.int32)), (2 * TOK_DEV, 2, offsets[0]), (TOPG * TOK_DEV, TOK_DEV, offsets[1]))
    picked = []
    peaks = []
    totals = []
    blends = []
    masks = []
    for segment_width, dilation, offset_row in plan:
        selected = [level_select(operand, segment_width, dilation, offset_row) for operand in operands]
        level_peak, level_total, level_blend = segment_map(forward_block, tuple(selected[:3]))
        picked.append(selected)
        peaks.append(stat_place(level_peak, dilation, offset_row))
        totals.append(stat_place(level_total, dilation, offset_row))
        blends.append(level_place(level_blend, dilation, offset_row))
        masks.append(stat_place(jnp.ones_like(level_peak), dilation, offset_row))
    row_peak = peaks[0]
    for level in (1, 2):
        row_peak = jnp.maximum(row_peak, jnp.where(masks[level] > 0, peaks[level], peaks[0]))
    weights = [jnp.exp(peaks[0] - row_peak)]
    for level in (1, 2):
        weights.append(masks[level] * jnp.exp(jnp.where(masks[level] > 0, peaks[level], row_peak) - row_peak))
    row_total = totals[0] * weights[0] + totals[1] * weights[1] + totals[2] * weights[2]
    blended = blends[0] * weights[0].T[:, :, None] + blends[1] * weights[1].T[:, :, None] + blends[2] * weights[2].T[:, :, None]
    attended = blended / row_total.T[:, :, None]
    log_total = row_peak + jnp.log(row_total)
    row_delta = jnp.sum(operands[3].astype(jnp.float32) * attended, axis=-1).T
    gradients = []
    for (segment_width, dilation, offset_row), selected in zip(plan, picked):
        level_log = stat_select(log_total, segment_width, dilation, offset_row)
        level_delta = stat_select(row_delta, segment_width, dilation, offset_row)
        results = segment_map(backward_block, (selected[0], selected[1], selected[2], selected[3], level_log, level_delta))
        gradients.append([level_place(result, dilation, offset_row) for result in results])
    finals = []
    for which in range(3):
        summed = gradients[0][which] + gradients[1][which] + gradients[2][which]
        finals.append(summed.astype(jnp.bfloat16).reshape(length, head_count * head_size))
    return (finals[0], finals[1], finals[2])
```

```python
import functools

import jax
import jax.numpy as jnp
from jax import lax
from jax.experimental import pallas as pl
from jax.experimental.pallas import tpu as pltpu
from jax.sharding import PartitionSpec as P

NEG = -1e30
F32 = jnp.float32
BF16 = jnp.bfloat16
STAT_ROWS = 8
VMEM_LIMIT = 40 * 1024 * 1024


def iota(shape, dim):
    return lax.broadcasted_iota(jnp.int32, shape, dim)


def dot_nt(a, b):
    return lax.dot_general(a, b, (((1,), (1,)), ((), ())), preferred_element_type=F32)


def dot_tn(a, b):
    return lax.dot_general(a, b, (((0,), (0,)), ((), ())), preferred_element_type=F32)


def dot_nn(a, b):
    return lax.dot_general(a, b, (((1,), (0,)), ((), ())), preferred_element_type=F32)


def two_rows(first, second):
    row = iota((8, first.shape[1]), 0)
    return jnp.where(row == 0, first, jnp.where(row == 1, second, 0.0)).astype(BF16)


def pair_chosen(wide_offset, pair_offset):
    return jnp.bitwise_and(wide_offset, 1) == pair_offset


def pack_kernel(heads, off_ref, k_ref, v_ref, q_ref, g_ref, out_ref, buf, acc, sems):
    dh = out_ref.shape[1]
    copies = []
    for s, ref in enumerate((k_ref, v_ref, q_ref, g_ref)):
        for h in range(heads):
            base = pl.multiple_of(jnp.bitwise_and(off_ref[1, h], ~15), 16)
            slot = s * heads + h
            copy = pltpu.make_async_copy(
                ref.at[pl.ds(base, 16), pl.ds(h * dh, dh)], buf.at[slot], sems.at[slot]
            )
            copy.start()
            copies.append(copy)
    acc[...] = jnp.zeros_like(acc)
    row = iota((16, dh), 0)
    for s in range(4):
        for h in range(heads):
            slot = s * heads + h
            copies[slot].wait()
            own = row == jnp.bitwise_and(off_ref[1, h], 15)
            block = jnp.where(own, buf[slot].astype(F32), 0.0)
            acc[slot : slot + 1, :] = jnp.sum(block, axis=0, keepdims=True)
    out_ref[...] = acc[...].astype(BF16)


def stats_kernel(heads, off_ref, own_ref, far_ref, k_ref, v_ref, load_ref, s_ref, dp_ref, acc, far):
    dh = own_ref.shape[1]
    length = k_ref.shape[0]
    scale = dh**-0.5
    acc[...] = own_ref[...].astype(F32)
    far[...] = far_ref[...].astype(F32)
    row = iota((8, length), 0)
    lane = iota((8, length), 1)
    row8 = iota((8, dh), 0)
    lane8 = iota((8, dh), 1)
    table = jnp.zeros((8, dh), F32)
    for h in range(heads):
        cols = slice(h * dh, (h + 1) * dh)
        nq, ng = 2 * heads + h, 3 * heads + h
        s = dot_nt(two_rows(acc[nq : nq + 1, :], far[nq : nq + 1, :]), k_ref[:, cols]) * scale
        dp = dot_nt(two_rows(acc[ng : ng + 1, :], far[ng : ng + 1, :]), v_ref[:, cols])
        s_ref[h * 8 : h * 8 + 8, :] = s
        dp_ref[h * 8 : h * 8 + 8, :] = dp
        weight, valid = row_weights(off_ref, h, row, lane)
        masked = jnp.where(valid, s, NEG)
        m = jnp.max(masked, axis=1, keepdims=True)
        e = jnp.exp(masked - m) * weight
        t = jnp.sum(e, axis=1, keepdims=True)
        d = jnp.sum(e * dp, axis=1, keepdims=True)
        column = jnp.zeros((8, dh), F32)
        for index, value in enumerate((m[0:1], t[0:1], d[0:1], m[1:2], t[1:2], d[1:2])):
            column = jnp.where(row8 == index, value, column)
        table = jnp.where(lane8 == h, column, table)
    high = table.astype(BF16).astype(F32)
    rest = table - high
    middle = rest.astype(BF16).astype(F32)
    low = (rest - middle).astype(BF16).astype(F32)
    acc[4 * heads : 4 * heads + 8, :] = high + pltpu.roll(middle, 16, 1) + pltpu.roll(low, 32, 1)
    load = acc[...].astype(BF16)
    load_ref[...] = jnp.broadcast_to(load[None], load_ref.shape)


def row_weights(off_ref, h, row, lane):
    chosen = pair_chosen(off_ref[1, h], off_ref[0, h])
    both = jnp.logical_and(jnp.bitwise_and(lane, 1) == off_ref[0, h], chosen)
    both = both.astype(F32)
    weight = jnp.where(row == 0, 1.0 + both, jnp.where(row == 1, both, 0.0))
    return weight, weight > 0.0


def main_kernel(
    off_ref, q_ref, k_ref, v_ref, g_ref, kf_ref, vf_ref, dq_ref, dk_ref, dv_ref, ret_ref
):
    h = pl.program_id(0)
    length, dh = q_ref.shape
    half = length // 2
    scale = dh**-0.5
    pair, wide = off_ref[0, h], off_ref[1, h]
    pick = (iota((length, half), 0) == 2 * iota((length, half), 1) + pair).astype(BF16)
    q, k, v, g = q_ref[...], k_ref[...], v_ref[...], g_ref[...]
    kc = dot_tn(pick, kf_ref[...]).astype(BF16)
    vc = dot_tn(pick, vf_ref[...]).astype(BF16)
    rows = iota((length, 1), 0)
    chosen = jnp.bitwise_and(rows, 1) == pair
    a_t = chosen.astype(F32)
    a_u = (jnp.bitwise_and(iota((1, length), 1), 1) == pair).astype(F32)
    s1 = dot_nt(q, k) * scale
    s2 = dot_nt(q, kc) * scale + jnp.where(chosen, 0.0, NEG)
    m = jnp.maximum(jnp.max(s1, axis=1, keepdims=True), jnp.max(s2, axis=1, keepdims=True))
    e1 = jnp.exp(s1 - m) * (1.0 + a_t * a_u)
    e2 = jnp.exp(s2 - m)
    total = jnp.sum(e1, axis=1, keepdims=True) + jnp.sum(e2, axis=1, keepdims=True)
    inverse = jnp.where(rows == wide, 0.0, 1.0 / total)
    p1 = e1 * inverse
    p2 = e2 * inverse
    dp1 = dot_nt(g, v)
    dp2 = dot_nt(g, vc)
    delta = jnp.sum(p1 * dp1, axis=1, keepdims=True) + jnp.sum(p2 * dp2, axis=1, keepdims=True)
    ds1 = (scale * p1 * (dp1 - delta)).astype(BF16)
    ds2 = (scale * p2 * (dp2 - delta)).astype(BF16)
    dq_ref[...] = (dot_nn(ds1, k) + dot_nn(ds2, kc)).astype(BF16)
    dk_ref[...] = dot_tn(ds1, q)
    dv_ref[...] = dot_tn(p1.astype(BF16), g)
    ret_ref[:half, :] = dot_tn(ds2, q).astype(BF16)
    ret_ref[half:, :] = dot_tn(p2.astype(BF16), g).astype(BF16)


def join_kernel(off_ref, own_ref, dk_ref, dv_ref, ret_ref, kf_ref, vf_ref, dko, dvo, sc, dpc, rows):
    h = pl.program_id(0)
    heads = pl.num_programs(0)
    length, dh = dk_ref.shape
    half = length // 2
    pair = off_ref[0, h]
    pick = (iota((length, half), 0) == 2 * iota((length, half), 1) + pair).astype(BF16)
    dko[...] = dk_ref[...] + dot_nn(pick, ret_ref[:half, :])
    dvo[...] = dv_ref[...] + dot_nn(pick, ret_ref[half:, :])
    rows[...] = own_ref[...].astype(F32)
    query = rows[pl.ds(2 * heads + h, 1), :]
    grad = rows[pl.ds(3 * heads + h, 1), :]
    sc[...] = dot_nt(two_rows(query, query), kf_ref[...]) * dh**-0.5
    dpc[...] = dot_nt(two_rows(grad, grad), vf_ref[...])


def final_kernel(
    heads, span, off_ref, me_ref, recv_ref, s_ref, dp_ref, sc_ref, dpc_ref, k_ref, kf_ref,
    dqi, dki, dvi, dqo, dko, dvo, flat,
):
    length = k_ref.shape[0]
    dh = k_ref.shape[1] // heads
    slots = recv_ref.shape[1]
    scale = dh**-0.5
    me = me_ref[0]
    mate = jnp.bitwise_xor(me, 1)
    flat[...] = recv_ref[...].astype(F32).reshape(span * slots, dh)

    def gathered(slot):
        return flat[pl.ds(slot, span, stride=slots), :]

    def stat(index):
        x = gathered(4 * heads + index)
        return x + pltpu.roll(x, dh - 16, 1) + pltpu.roll(x, dh - 32, 1)

    even = jnp.bitwise_and(iota((span, dh), 0), 1) == 0

    def exchanged(x):
        return jnp.where(even, pltpu.roll(x, span - 1, 0), pltpu.roll(x, 1, 0))

    m_a, t_a, d_a = stat(0), stat(1), stat(2)
    m_b, t_b, d_b = exchanged(stat(3)), exchanged(stat(4)), exchanged(stat(5))
    m_ab = jnp.maximum(m_a, m_b)
    w_a, w_b = jnp.exp(m_a - m_ab), jnp.exp(m_b - m_ab)
    t_ab = t_a * w_a + t_b * w_b
    d_ab = d_a * w_a + d_b * w_b
    device = iota((span, 1), 0)
    is_me, is_mate = device == me, device == mate
    row = iota((8, length), 0)
    lane = iota((8, length), 1)
    row1 = iota((8, 1), 0)
    row8 = iota((8, dh), 0)

    def one(mask, x):
        return jnp.sum(jnp.where(mask, x, 0.0), axis=0, keepdims=True)

    for h in range(heads):
        cols = slice(h * dh, (h + 1) * dh)
        wide, pair = off_ref[1, h], off_ref[0, h]
        k_w, v_w, q_w, g_w = [gathered(i * heads + h) for i in range(4)]
        k_b = k_w.astype(BF16)
        s_w = dot_nt(q_w.astype(BF16), k_b) * scale
        dp_w = dot_nt(g_w.astype(BF16), v_w.astype(BF16))
        m_h = m_ab[:, h : h + 1]
        m = jnp.maximum(m_h, jnp.max(s_w, axis=1, keepdims=True))
        e = jnp.exp(s_w - m)
        shift = jnp.exp(m_h - m)
        total = t_ab[:, h : h + 1] * shift + jnp.sum(e, axis=1, keepdims=True)
        part = d_ab[:, h : h + 1] * shift + jnp.sum(e * dp_w, axis=1, keepdims=True)
        inverse = 1.0 / total
        delta = part * inverse
        p_w = e * inverse
        ds_w = (scale * p_w * (dp_w - delta)).astype(BF16).astype(F32)
        p_w = p_w.astype(BF16).astype(F32)
        mine = iota((1, span), 1) == me
        ds_column = jnp.sum(jnp.where(mine, ds_w, 0.0), axis=1, keepdims=True)
        p_column = jnp.sum(jnp.where(mine, p_w, 0.0), axis=1, keepdims=True)
        dk_w = jnp.sum(ds_column * q_w, axis=0, keepdims=True)
        dv_w = jnp.sum(p_column * g_w, axis=0, keepdims=True)
        ds_row = jnp.broadcast_to(one(is_me, ds_w), (8, span)).astype(BF16)

        def two(x):
            return jnp.where(row1 == 0, one(is_me, x), one(is_mate, x))

        m_r, inverse_r, delta_r = two(m), two(inverse), two(delta)
        weight, valid = row_weights(off_ref, h, row, lane)
        s_r = s_ref[h * 8 : h * 8 + 8, :]
        p_r = jnp.exp(jnp.where(valid, s_r - m_r, NEG)) * weight * inverse_r
        ds_r = scale * p_r * (dp_ref[h * 8 : h * 8 + 8, :] - delta_r)
        both = jnp.logical_and(jnp.bitwise_and(lane, 1) == pair, pair_chosen(wide, pair))
        s_c = sc_ref[h * 8 : h * 8 + 8, :]
        p_c = jnp.exp(jnp.where(both, s_c - m_r[0:1], NEG)) * inverse_r[0:1]
        ds_c = scale * p_c * (dpc_ref[h * 8 : h * 8 + 8, :] - delta_r[0:1])
        dq_row = (
            dot_nn(ds_r.astype(BF16), k_ref[:, cols])
            + dot_nn(ds_c.astype(BF16), kf_ref[:, cols])
            + dot_nn(ds_row, k_b)
        )[0:1, :]
        here = iota((length, dh), 0) == wide
        dqo[:, cols] = jnp.where(here, dq_row, dqi[:, cols].astype(F32)).astype(BF16)
        spot = (lane == wide).astype(F32)

        def added(base, left, first, second, own):
            high = own.astype(BF16).astype(F32)
            right = jnp.where(row8 == 2, high, jnp.where(row8 == 3, own - high, 0.0))
            right = jnp.where(row8 == 0, first, jnp.where(row8 == 1, second, right))
            left = jnp.where(row < 2, left, jnp.where(row < 4, spot, 0.0))
            return (base + dot_tn(left.astype(BF16), right.astype(BF16))).astype(BF16)

        dko[:, cols] = added(dki[:, cols], ds_r, one(is_me, q_w), one(is_mate, q_w), dk_w)
        dvo[:, cols] = added(dvi[:, cols], p_r, one(is_me, g_w), one(is_mate, g_w), dv_w)


def on_device(query, key, value, grad_out, offsets):
    length, width = query.shape
    heads = offsets.shape[1]
    dh = width // heads
    size = lax.axis_size("ctx")
    span = min(size, 128)
    slots = 4 * heads + STAT_ROWS
    half = length // 2
    mates = [(i, i ^ 1) for i in range(size)]
    vmem = pl.BlockSpec(memory_space=pltpu.VMEM)
    smem = pl.BlockSpec(memory_space=pltpu.SMEM)
    anywhere = pl.BlockSpec(memory_space=pl.ANY)
    params = pltpu.CompilerParams(vmem_limit_bytes=VMEM_LIMIT)
    small = pl.CostEstimate(flops=1000, bytes_accessed=1000, transcendentals=0)

    def shape(rows, columns, dtype):
        return jax.ShapeDtypeStruct((rows, columns), dtype)

    own = pl.pallas_call(
        functools.partial(pack_kernel, heads),
        out_shape=shape(slots, dh, BF16),
        in_specs=[smem] + [anywhere] * 4,
        out_specs=vmem,
        scratch_shapes=[
            pltpu.VMEM((4 * heads, 16, dh), BF16),
            pltpu.VMEM((slots, dh), F32),
            pltpu.SemaphoreType.DMA((4 * heads,)),
        ],
        compiler_params=params,
        cost_estimate=small,
        name="pack_rows",
    )(offsets, key, value, query, grad_out)
    far = lax.ppermute(own, "ctx", mates)
    key_far = lax.ppermute(key, "ctx", mates)
    value_far = lax.ppermute(value, "ctx", mates)
    load, s_rows, dp_rows = pl.pallas_call(
        functools.partial(stats_kernel, heads),
        out_shape=(
            jax.ShapeDtypeStruct((span, slots, dh), BF16),
            shape(heads * 8, length, F32),
            shape(heads * 8, length, F32),
        ),
        in_specs=[smem] + [vmem] * 4,
        out_specs=(vmem,) * 3,
        scratch_shapes=[pltpu.VMEM((slots, dh), F32), pltpu.VMEM((slots, dh), F32)],
        compiler_params=params,
        cost_estimate=small,
        name="row_stats",
    )(offsets, own, far, key, value)
    groups = None
    if size > span:
        groups = [list(range(base, base + span)) for base in range(0, size, span)]
    received = lax.all_to_all(load, "ctx", 0, 0, axis_index_groups=groups, tiled=True)
    block = pl.BlockSpec((length, dh), lambda h: (0, h))
    dq, dk, dv, partial = pl.pallas_call(
        main_kernel,
        grid=(heads,),
        out_shape=(
            shape(length, width, BF16),
            shape(length, width, F32),
            shape(length, width, F32),
            shape(length, width, BF16),
        ),
        in_specs=[smem] + [block] * 6,
        out_specs=(block,) * 4,
        compiler_params=params,
        cost_estimate=small,
        name="near_levels",
    )(offsets, query, key, value, grad_out, key_far, value_far)
    returned = lax.ppermute(partial, "ctx", mates)
    thin = pl.BlockSpec((8, length), lambda h: (h, 0))
    dk, dv, s_far, dp_far = pl.pallas_call(
        join_kernel,
        grid=(heads,),
        out_shape=(
            shape(length, width, F32),
            shape(length, width, F32),
            shape(heads * 8, length, F32),
            shape(heads * 8, length, F32),
        ),
        in_specs=[smem, vmem] + [block] * 5,
        out_specs=(block, block, thin, thin),
        scratch_shapes=[pltpu.VMEM((slots, dh), F32)],
        compiler_params=params,
        cost_estimate=small,
        name="join_pair",
    )(offsets, own, dk, dv, returned, key_far, value_far)
    me = lax.rem(lax.axis_index("ctx"), span).astype(jnp.int32).reshape(1)
    return pl.pallas_call(
        functools.partial(final_kernel, heads, span),
        out_shape=(shape(length, width, BF16),) * 3,
        in_specs=[smem, smem] + [vmem] * 10,
        out_specs=(vmem,) * 3,
        scratch_shapes=[pltpu.VMEM((span * slots, dh), F32)],
        compiler_params=params,
        cost_estimate=small,
        name="third_level",
    )(offsets, me, received, s_rows, dp_rows, s_far, dp_far, key, key_far, dq, dk, dv)


def solution(mesh):
    placed = (P("ctx", None), P("ctx", None), P("ctx", None), P("ctx", None), P())
    return jax.shard_map(
        on_device,
        mesh=mesh,
        in_specs=placed,
        out_specs=(P("ctx", None), P("ctx", None), P("ctx", None)),
        check_vma=False,
    )
```

```python
import functools

import jax
import jax.numpy as jnp
from jax import lax
from jax.experimental import pallas as pl
from jax.experimental.pallas import tpu as pltpu
from jax.sharding import PartitionSpec as P

NEG = -1e30
F32 = jnp.float32
BF16 = jnp.bfloat16
STAT_ROWS = 8
VMEM_LIMIT = 16 * 1024 * 1024
LOG2E = 1.4426950408889634


def iota(shape, dim):
    return lax.broadcasted_iota(jnp.int32, shape, dim)


def dot_nt(a, b):
    return lax.dot_general(a, b, (((1,), (1,)), ((), ())), preferred_element_type=F32)


def dot_tn(a, b):
    return lax.dot_general(a, b, (((0,), (0,)), ((), ())), preferred_element_type=F32)


def dot_nn(a, b):
    return lax.dot_general(a, b, (((1,), (0,)), ((), ())), preferred_element_type=F32)


def block_rows(rows, heads):
    row = iota(rows.shape, 0)
    return jnp.concatenate(
        [jnp.where(row == h, rows, 0.0).astype(BF16) for h in range(heads)], axis=1
    )


def own_columns(wide_rows, heads):
    dh = wide_rows.shape[1] // heads
    row = iota((16, dh), 0)
    return sum(
        jnp.where(row == h, wide_rows[:, h * dh : (h + 1) * dh], 0.0) for h in range(heads)
    )


def offset_column(off_ref, level, heads, rows):
    row = jnp.bitwise_and(iota((rows, 1), 0), 15)
    column = jnp.zeros((rows, 1), jnp.int32)
    for h in range(heads):
        column = jnp.where(row == h, off_ref[level, h], column)
    return column


def level_one_keys(off_ref, heads, rows, length):
    pair = offset_column(off_ref, 0, heads, rows)
    wide = offset_column(off_ref, 1, heads, rows)
    lane = iota((rows, length), 1)
    chosen = jnp.bitwise_and(wide, 1) == pair
    return jnp.logical_and(jnp.bitwise_and(lane, 1) == pair, chosen)


def row_weights(off_ref, heads, length):
    both = level_one_keys(off_ref, heads, 32, length).astype(F32)
    return jnp.where(iota((32, length), 0) < 16, 1.0 + both, both)


def pack_kernel(heads, off_ref, q_ref, g_ref, out_ref, buf, acc, sems):
    dh = out_ref.shape[1]
    copies = []
    for s, ref in enumerate((q_ref, g_ref)):
        for h in range(heads):
            base = pl.multiple_of(jnp.bitwise_and(off_ref[1, h], ~15), 16)
            slot = s * heads + h
            copy = pltpu.make_async_copy(
                ref.at[pl.ds(base, 16), pl.ds(h * dh, dh)], buf.at[slot], sems.at[slot]
            )
            copy.start()
            copies.append(copy)
    acc[...] = jnp.zeros_like(acc)
    row = iota((16, dh), 0)
    for s in range(2):
        for h in range(heads):
            slot = s * heads + h
            copies[slot].wait()
            own = row == jnp.bitwise_and(off_ref[1, h], 15)
            block = jnp.where(own, buf[slot].astype(F32), 0.0)
            acc[16 * s + h : 16 * s + h + 1, :] = jnp.sum(block, axis=0, keepdims=True)
    out_ref[...] = acc[...].astype(BF16)


def stats_kernel(
    heads, span, off_ref, own_ref, far_ref, k_ref, v_ref, load_ref, s_ref, dp_ref, acc, load, sems
):
    dh = own_ref.shape[1]
    length = k_ref.shape[0]
    own, far = own_ref[...].astype(F32), far_ref[...].astype(F32)

    def both_rows(first):
        return jnp.concatenate(
            [block_rows(rows[first : first + 16, :], heads) for rows in (own, far)], axis=0
        )

    s = dot_nt(both_rows(0), k_ref[...]) * (dh**-0.5 * LOG2E)
    dp = dot_nt(both_rows(16), v_ref[...])
    s_ref[...] = s
    dp_ref[...] = dp
    place = iota((16, dh), 0)
    for i, ref in enumerate((k_ref, v_ref)):
        for h in range(heads):
            base = pl.multiple_of(jnp.bitwise_and(off_ref[1, h], ~15), 16)
            block = ref[pl.ds(base, 16), h * dh : (h + 1) * dh].astype(F32)
            block = jnp.where(place == jnp.bitwise_and(off_ref[1, h], 15), block, 0.0)
            slot = i * heads + h
            acc[slot : slot + 1, :] = jnp.sum(block, axis=0, keepdims=True)
    acc[2 * heads : 3 * heads, :] = own[:heads, :]
    acc[3 * heads : 4 * heads, :] = own[16 : 16 + heads, :]
    weight = row_weights(off_ref, heads, length)
    masked = jnp.where(weight > 0.0, s, NEG)
    m = jnp.max(masked, axis=1, keepdims=True)
    e = jnp.exp2(masked - m) * weight
    t = jnp.sum(e, axis=1, keepdims=True)
    d = jnp.sum(e * dp, axis=1, keepdims=True)
    lane = iota((32, 128), 1)
    table = jnp.where(lane == 0, m, jnp.where(lane == 1, t, jnp.where(lane == 2, d, 0.0)))
    table = jnp.concatenate([table, jnp.zeros((96, 128), F32)], axis=0).T[0:STAT_ROWS, :]
    high = table.astype(BF16).astype(F32)
    rest = table - high
    middle = rest.astype(BF16).astype(F32)
    low = (rest - middle).astype(BF16).astype(F32)
    acc[4 * heads : 4 * heads + STAT_ROWS, :] = (
        high + pltpu.roll(middle, 32, 1) + pltpu.roll(low, 64, 1)
    )
    load[...] = acc[...].astype(BF16)
    copies = [pltpu.make_async_copy(load, load_ref.at[i], sems.at[i]) for i in range(span)]
    for copy in copies:
        copy.start()
    for copy in copies:
        copy.wait()


def near_head(off_ref, h, inputs, outputs, wait, send):
    q_ref, k_ref, v_ref, g_ref, kf_ref, vf_ref = inputs
    dq_ref, dk_ref, dv_ref, ret_ref = outputs
    length, dh = q_ref.shape[0], q_ref.shape[1] // off_ref.shape[1]
    half = length // 2
    scale = dh**-0.5
    cols = slice(h * dh, (h + 1) * dh)
    pair, wide = off_ref[0, h], off_ref[1, h]
    wait(h)
    q, k, v, g = q_ref[:, cols], k_ref[:, cols], v_ref[:, cols], g_ref[:, cols]
    pick = (iota((half, length), 1) == 2 * iota((half, length), 0) + pair).astype(BF16)
    kc = dot_nn(pick, kf_ref[:, cols]).astype(BF16)
    vc = dot_nn(pick, vf_ref[:, cols]).astype(BF16)
    yield
    lanes = iota((1, length), 1)
    chosen = jnp.bitwise_and(lanes, 1) == pair
    a_t = chosen.astype(F32)
    a_u = (jnp.bitwise_and(iota((length, 1), 0), 1) == pair).astype(F32)
    s1 = dot_nt(k, q)
    s2 = dot_nt(kc, q) + jnp.where(chosen, 0.0, NEG)
    yield
    m = jnp.maximum(jnp.max(s1, axis=0, keepdims=True), jnp.max(s2, axis=0, keepdims=True))
    m = m * (scale * LOG2E)
    dp1 = dot_nt(v, g)
    dp2 = dot_nt(vc, g)
    yield
    e1 = jnp.exp2(s1 * (scale * LOG2E) - m) * (1.0 + a_t * a_u)
    e2 = jnp.exp2(s2 * (scale * LOG2E) - m)
    total = jnp.sum(e1, axis=0, keepdims=True) + jnp.sum(e2, axis=0, keepdims=True)
    part = jnp.sum(e1 * dp1, axis=0, keepdims=True) + jnp.sum(e2 * dp2, axis=0, keepdims=True)
    yield
    inverse = jnp.where(lanes == wide, 0.0, 1.0 / total)
    delta = part * inverse
    p1 = e1 * inverse
    p2 = e2 * inverse
    ds1 = (scale * p1 * (dp1 - delta)).astype(BF16)
    ds2 = (scale * p2 * (dp2 - delta)).astype(BF16)
    p1 = p1.astype(BF16)
    p2 = p2.astype(BF16)
    yield
    dk_ref[:, cols] = dot_nn(ds1, q)
    dv_ref[:, cols] = dot_nn(p1, g)
    ret_ref[:half, cols] = dot_nn(ds2, q).astype(BF16)
    ret_ref[half:, cols] = dot_nn(p2, g).astype(BF16)
    dq_ref[:, cols] = (dot_tn(k, ds1) + dot_tn(kc, ds2)).T.astype(BF16)
    send(h)
    yield


def main_kernel(
    heads, off_ref, own_ref, q_ref, k_ref, v_ref, g_ref, kf_ref, vf_hbm,
    dq_hbm, dk_hbm, dv_hbm, ret_hbm, sc_ref, dpc_ref,
    vf_ref, dq_ref, dk_ref, dv_ref, ret_ref, in_sems, out_sems,
):
    dh = q_ref.shape[1] // heads
    near = (dq_ref, dk_ref, dv_ref, ret_ref)
    reads, writes = [], []
    for j in range(heads // 2):
        cols = slice(2 * j * dh, 2 * (j + 1) * dh)
        copy = pltpu.make_async_copy(vf_hbm.at[:, cols], vf_ref.at[:, cols], in_sems.at[j])
        copy.start()
        reads.append(copy)

    def wait(h):
        if h % 2 == 0:
            reads[h // 2].wait()

    def send(h):
        cols = slice(h * dh, (h + 1) * dh)
        for i, (a, b) in enumerate(zip(near, (dq_hbm, dk_hbm, dv_hbm, ret_hbm))):
            copy = pltpu.make_async_copy(a.at[:, cols], b.at[:, cols], out_sems.at[h, i])
            copy.start()
            writes.append(copy)

    own = own_ref[...].astype(F32)
    sc_ref[...] = dot_nt(block_rows(own[:16, :], heads), kf_ref[...]) * (dh**-0.5 * LOG2E)
    inputs = (q_ref, k_ref, v_ref, g_ref, kf_ref, vf_ref)
    work = [near_head(off_ref, h, inputs, near, wait, send) for h in range(heads)]
    steps, lag = 6, 2
    for turn in range(steps + lag * (heads - 1)):
        for h in reversed(range(heads)):
            if 0 <= turn - lag * h < steps:
                next(work[h])
    dpc_ref[...] = dot_nt(block_rows(own[16:, :], heads), vf_ref[...])
    for copy in writes:
        copy.wait()


def final_kernel(
    heads, span, off_ref, me_ref, recv_ref, own_ref, far_ref, s_ref, dp_ref, sc_ref, dpc_ref,
    k_ref, kf_ref, ret, dk_hbm, dv_hbm, dq_in, dq_ref, dk_ref, dv_ref,
    flat, dki, dvi, blocks, dko, dvo, read_sems, block_sems, write_sems,
):
    length, dh = k_ref.shape[0], own_ref.shape[1]
    half = length // 2
    slots = recv_ref.shape[1]
    scale = dh**-0.5
    me = me_ref[0]
    mate = jnp.bitwise_xor(me, 1)

    def place(ref, h):
        base = pl.multiple_of(jnp.bitwise_and(off_ref[1, h], ~15), 16)
        return ref.at[pl.ds(base, 16), pl.ds(h * dh, dh)]

    step = 2 * dh
    chunks = [slice(j * step, (j + 1) * step) for j in range(heads // 2)]
    reads = [
        pltpu.make_async_copy(place(dq_in, h), blocks.at[h], block_sems.at[h]) for h in range(heads)
    ]
    fetches = [
        [
            pltpu.make_async_copy(a.at[:, cols], b.at[:, cols], read_sems.at[i, j])
            for j, cols in enumerate(chunks)
        ]
        for i, (a, b) in enumerate(((dk_hbm, dki), (dv_hbm, dvi)))
    ]
    for group in [reads] + fetches:
        for copy in group:
            copy.start()
    flat[...] = recv_ref[...].astype(F32).reshape(span * slots, dh)
    own, far = own_ref[...].astype(F32), far_ref[...].astype(F32)

    def gathered(slot):
        return flat[pl.ds(slot, span, stride=slots), :]

    even = jnp.bitwise_and(iota((16, 128), 1), 1) == 0

    def stat(index):
        x = gathered(4 * heads + index)
        x = x + pltpu.roll(x, 96, 1) + pltpu.roll(x, 64, 1)
        if span < 128:
            x = jnp.concatenate([x, jnp.zeros((128 - span, 128), F32)], axis=0)
        x = x.T
        near, other = x[0:16, :], x[16:32, :]
        other = jnp.where(even, pltpu.roll(other, 127, 1), pltpu.roll(other, 1, 1))
        return near[:, :span], other[:, :span]

    (m_a, m_b), (t_a, t_b), (d_a, d_b) = stat(0), stat(1), stat(2)
    row = iota((16, span), 0)
    device = iota((span, 1), 0)
    k_w, v_w, q_w, g_w = [
        [gathered(i * heads + h).astype(BF16) for h in range(heads)] for i in range(4)
    ]
    m_c, t_c, d_c, s_key, dp_key = [jnp.zeros((16, span), F32) for _ in range(5)]
    for h in range(heads):
        s = dot_nt(k_w[h], q_w[h]) * (scale * LOG2E)
        dp = dot_nt(v_w[h], g_w[h])
        m = jnp.max(s, axis=0, keepdims=True)
        e = jnp.exp2(s - m)
        here = row == h
        m_c = jnp.where(here, m, m_c)
        t_c = jnp.where(here, jnp.sum(e, axis=0, keepdims=True), t_c)
        d_c = jnp.where(here, jnp.sum(e * dp, axis=0, keepdims=True), d_c)
        mine = device == me
        s_key = jnp.where(here, jnp.sum(jnp.where(mine, s, 0.0), axis=0, keepdims=True), s_key)
        dp_key = jnp.where(here, jnp.sum(jnp.where(mine, dp, 0.0), axis=0, keepdims=True), dp_key)
    m_all = jnp.maximum(jnp.maximum(m_a, m_b), m_c)
    w_a, w_b, w_c = jnp.exp2(m_a - m_all), jnp.exp2(m_b - m_all), jnp.exp2(m_c - m_all)
    inverse = 1.0 / (t_a * w_a + t_b * w_b + t_c * w_c)
    delta = (d_a * w_a + d_b * w_b + d_c * w_c) * inverse
    p_key = jnp.exp2(s_key - m_all) * inverse
    ds_key = scale * p_key * (dp_key - delta)

    def column(x, index):
        return jnp.sum(jnp.where(iota((16, span), 1) == index, x, 0.0), axis=1, keepdims=True)

    m_me, i_me, d_me = [column(x, me) for x in (m_all, inverse, delta)]
    m_two, i_two, d_two = [
        jnp.concatenate([a, column(x, mate)], axis=0)
        for a, x in ((m_me, m_all), (i_me, inverse), (d_me, delta))
    ]

    def one_head(rows, h):
        return jnp.where(iota(rows.shape, 0) == h, rows, 0.0).astype(BF16)

    q_own, g_own = own[:16, :], own[16:, :]
    s_row = sum(dot_nt(one_head(q_own, h), k_w[h]) for h in range(heads)) * (scale * LOG2E)
    dp_row = sum(dot_nt(one_head(g_own, h), v_w[h]) for h in range(heads))
    ds_row = scale * (jnp.exp2(s_row - m_me) * i_me) * (dp_row - d_me)
    weight = row_weights(off_ref, heads, length)
    p_two = jnp.exp2(jnp.where(weight > 0.0, s_ref[...] - m_two, NEG)) * weight * i_two
    ds_two = scale * p_two * (dp_ref[...] - d_two)
    met = level_one_keys(off_ref, heads, 16, length)
    p_far = jnp.exp2(jnp.where(met, sc_ref[...] - m_me, NEG)) * i_me
    ds_far = scale * p_far * (dpc_ref[...] - d_me)
    dq_rows = own_columns(
        dot_nn(ds_two[0:16, :].astype(BF16), k_ref[...]) + dot_nn(ds_far.astype(BF16), kf_ref[...]),
        heads,
    ) + sum(dot_nn(one_head(ds_row, h), k_w[h]) for h in range(heads))
    dk_rows = sum(dot_nn(one_head(ds_key, h), q_w[h]) for h in range(heads))
    dv_rows = sum(dot_nn(one_head(p_key, h), g_w[h]) for h in range(heads))
    wide = offset_column(off_ref, 1, heads, 32)
    spot = (iota((32, length), 1) == wide).astype(F32)

    def spread(left, first, rows):
        high = rows.astype(BF16).astype(F32)
        left = jnp.concatenate([left, spot], axis=0).T.astype(BF16)
        parts = (own[first : first + 16, :], far[first : first + 16, :], high, rows - high)
        return left, jnp.concatenate([block_rows(part, heads) for part in parts], axis=0)

    writes = []
    for index, (base, out, out_ref, left, right) in enumerate(
        (
            (dki, dko, dk_ref) + spread(ds_two, 0, dk_rows),
            (dvi, dvo, dv_ref) + spread(p_two, 16, dv_rows),
        )
    ):
        back = slice(index * half, (index + 1) * half)
        for j, chunk in enumerate(chunks):
            fetches[index][j].wait()
            for h in (2 * j, 2 * j + 1):
                cols = slice(h * dh, (h + 1) * dh)
                pair = off_ref[0, h]
                pick = iota((length, half), 0) == 2 * iota((length, half), 1) + pair
                added = dot_nn(left, right[:, cols]) + dot_nn(pick.astype(BF16), ret[back, cols])
                out[:, cols] = (base[:, cols] + added).astype(BF16)
            sem = write_sems.at[index, j]
            copy = pltpu.make_async_copy(out.at[:, chunk], out_ref.at[:, chunk], sem)
            copy.start()
            writes.append(copy)
    for h in range(heads):
        reads[h].wait()
        here = iota((16, dh), 0) == jnp.bitwise_and(off_ref[1, h], 15)
        blocks[h] = jnp.where(here, dq_rows[h : h + 1, :], blocks[h].astype(F32)).astype(BF16)
        copy = pltpu.make_async_copy(blocks.at[h], place(dq_ref, h), block_sems.at[h])
        copy.start()
        writes.append(copy)
    for copy in writes:
        copy.wait()


def on_device(query, key, value, grad_out, offsets):
    length, width = query.shape
    heads = offsets.shape[1]
    dh = width // heads
    size = lax.axis_size("ctx")
    span = min(size, 128)
    slots = 4 * heads + STAT_ROWS
    mates = [(i, i ^ 1) for i in range(size)]
    vmem = pl.BlockSpec(memory_space=pltpu.VMEM)
    smem = pl.BlockSpec(memory_space=pltpu.SMEM)
    hbm = pl.BlockSpec(memory_space=pltpu.HBM)
    params = pltpu.CompilerParams(vmem_limit_bytes=VMEM_LIMIT)
    small = pl.CostEstimate(flops=1000, bytes_accessed=1000, transcendentals=0)

    def call(kernel, name, out_shape, in_specs, out_specs, scratch, **kwargs):
        return pl.pallas_call(
            kernel,
            out_shape=out_shape,
            in_specs=in_specs,
            out_specs=out_specs,
            scratch_shapes=scratch,
            compiler_params=params,
            cost_estimate=small,
            name=name,
            **kwargs,
        )

    def far_memory(*arrays):
        return [pltpu.with_memory_space_constraint(array, pltpu.HBM) for array in arrays]

    def near_memory(*arrays):
        return [pltpu.with_memory_space_constraint(array, pltpu.VMEM) for array in arrays]

    own = call(
        functools.partial(pack_kernel, heads),
        "pack_rows",
        pltpu.VMEM((32, dh), BF16),
        [smem] + [hbm] * 2,
        vmem,
        [
            pltpu.VMEM((2 * heads, 16, dh), BF16),
            pltpu.VMEM((32, dh), F32),
            pltpu.SemaphoreType.DMA((2 * heads,)),
        ],
    )(*far_memory(offsets, query, grad_out))
    far = lax.ppermute(own, "ctx", mates)
    key_far = lax.ppermute(key, "ctx", mates)
    value_far = lax.ppermute(value, "ctx", mates)
    load, s_rows, dp_rows = call(
        functools.partial(stats_kernel, heads, span),
        "row_stats",
        (
            pltpu.HBM((span, slots, dh), BF16),
            pltpu.VMEM((32, length), F32),
            pltpu.VMEM((32, length), F32),
        ),
        [smem] + [vmem] * 4,
        (hbm, vmem, vmem),
        [
            pltpu.VMEM((slots, dh), F32),
            pltpu.VMEM((slots, dh), BF16),
            pltpu.SemaphoreType.DMA((span,)),
        ],
    )(*far_memory(offsets), *near_memory(own, far, key, value))
    groups = None
    if size > span:
        groups = [list(range(base, base + span)) for base in range(0, size, span)]
    received = lax.all_to_all(load, "ctx", 0, 0, axis_index_groups=groups, tiled=True)
    whole = pltpu.VMEM((length, width), BF16)
    wide = pltpu.VMEM((length, width), F32)
    thin = pltpu.VMEM((16, length), F32)
    dq, dk, dv, partial, s_far, dp_far = call(
        functools.partial(main_kernel, heads),
        "near_levels",
        (
            pltpu.HBM((length, width), BF16),
            pltpu.HBM((length, width), F32),
            pltpu.HBM((length, width), F32),
            pltpu.HBM((length, width), BF16),
            thin,
            thin,
        ),
        [smem] + [vmem] * 6 + [hbm],
        (hbm,) * 4 + (vmem,) * 2,
        [
            whole,
            whole,
            wide,
            wide,
            whole,
            pltpu.SemaphoreType.DMA((heads // 2,)),
            pltpu.SemaphoreType.DMA((heads, 4)),
        ],
    )(
        *far_memory(offsets),
        *near_memory(own, query, key, value, grad_out, key_far),
        *far_memory(value_far),
    )
    returned = lax.ppermute(partial, "ctx", mates)
    me = lax.rem(lax.axis_index("ctx"), span).astype(jnp.int32).reshape(1)
    return call(
        functools.partial(final_kernel, heads, span),
        "third_level",
        (pltpu.HBM((length, width), BF16),) * 3,
        [smem] * 2 + [vmem] * 10 + [hbm] * 3,
        (hbm,) * 3,
        [
            pltpu.VMEM((span * slots, dh), F32),
            wide,
            wide,
            pltpu.VMEM((heads, 16, dh), BF16),
            whole,
            whole,
            pltpu.SemaphoreType.DMA((2, heads // 2)),
            pltpu.SemaphoreType.DMA((heads,)),
            pltpu.SemaphoreType.DMA((2, heads // 2)),
        ],
        input_output_aliases={14: 0},
    )(
        *far_memory(offsets),
        me,
        *near_memory(received, own, far, s_rows, dp_rows, s_far, dp_far),
        *near_memory(key, key_far, returned),
        *far_memory(dk, dv, dq),
    )


def solution(mesh):
    placed = (P("ctx", None), P("ctx", None), P("ctx", None), P("ctx", None), P())
    return jax.shard_map(
        on_device,
        mesh=mesh,
        in_specs=placed,
        out_specs=(P("ctx", None), P("ctx", None), P("ctx", None)),
        check_vma=False,
    )
```

```python
import functools

import jax
import jax.numpy as jnp
from jax import lax
from jax.experimental import pallas as pl
from jax.experimental.pallas import tpu as pltpu
from jax.sharding import PartitionSpec as P

NEG = -1e30
F32 = jnp.float32
BF16 = jnp.bfloat16
STAT_ROWS = 4
VMEM_LIMIT = 16 * 1024 * 1024
LOG2E = 1.4426950408889634


def iota(shape, dim):
    return lax.broadcasted_iota(jnp.int32, shape, dim)


def dot_nt(a, b):
    return lax.dot_general(a, b, (((1,), (1,)), ((), ())), preferred_element_type=F32)


def dot_tn(a, b):
    return lax.dot_general(a, b, (((0,), (0,)), ((), ())), preferred_element_type=F32)


def dot_nn(a, b):
    return lax.dot_general(a, b, (((1,), (0,)), ((), ())), preferred_element_type=F32)


def block_rows(rows, heads):
    row = iota(rows.shape, 0)
    return jnp.concatenate(
        [jnp.where(row == h, rows, 0.0).astype(BF16) for h in range(heads)], axis=1
    )


def own_columns(wide_rows, heads):
    dh = wide_rows.shape[1] // heads
    row = iota((16, dh), 0)
    return sum(
        jnp.where(row == h, wide_rows[:, h * dh : (h + 1) * dh], 0.0) for h in range(heads)
    )


def offset_column(off_ref, level, heads, rows):
    row = jnp.bitwise_and(iota((rows, 1), 0), 15)
    column = jnp.zeros((rows, 1), jnp.int32)
    for h in range(heads):
        column = jnp.where(row == h, off_ref[level, h], column)
    return column


def level_one_keys(off_ref, heads, rows, length):
    pair = offset_column(off_ref, 0, heads, rows)
    wide = offset_column(off_ref, 1, heads, rows)
    lane = iota((rows, length), 1)
    chosen = jnp.bitwise_and(wide, 1) == pair
    return jnp.logical_and(jnp.bitwise_and(lane, 1) == pair, chosen)


def row_weights(off_ref, heads, length):
    both = level_one_keys(off_ref, heads, 32, length).astype(F32)
    return jnp.where(iota((32, length), 0) < 16, 1.0 + both, both)


def pack_kernel(heads, off_ref, q_ref, g_ref, out_ref, buf, acc, sems):
    dh = out_ref.shape[1]
    copies = []
    for s, ref in enumerate((q_ref, g_ref)):
        for h in range(heads):
            base = pl.multiple_of(jnp.bitwise_and(off_ref[1, h], ~15), 16)
            slot = s * heads + h
            copy = pltpu.make_async_copy(
                ref.at[pl.ds(base, 16), pl.ds(h * dh, dh)], buf.at[slot], sems.at[slot]
            )
            copy.start()
            copies.append(copy)
    acc[...] = jnp.zeros_like(acc)
    row = iota((16, dh), 0)
    for s in range(2):
        for h in range(heads):
            slot = s * heads + h
            copies[slot].wait()
            own = row == jnp.bitwise_and(off_ref[1, h], 15)
            block = jnp.where(own, buf[slot].astype(F32), 0.0)
            acc[16 * s + h : 16 * s + h + 1, :] = jnp.sum(block, axis=0, keepdims=True)
    out_ref[...] = acc[...].astype(BF16)


def stats_kernel(
    heads, span, off_hbm, own_ref, far_ref, k_ref, v_ref, load_ref, s_ref, dp_ref,
    off_ref, acc, load, off_sem, sems,
):
    offsets = pltpu.make_async_copy(off_hbm, off_ref, off_sem)
    offsets.start()
    dh = own_ref.shape[1]
    length = k_ref.shape[0]
    own, far = own_ref[...].astype(F32), far_ref[...].astype(F32)

    def both_rows(first):
        return jnp.concatenate(
            [block_rows(rows[first : first + 16, :], heads) for rows in (own, far)], axis=0
        )

    s = dot_nt(both_rows(0), k_ref[...]) * (dh**-0.5 * LOG2E)
    dp = dot_nt(both_rows(16), v_ref[...])
    s_ref[...] = s
    dp_ref[...] = dp
    offsets.wait()
    part, slots = heads // 2, load_ref.shape[1]

    def slot(array, h):
        return (h // part) * slots + array * part + h % part

    place = iota((16, dh), 0)
    for i, ref in enumerate((k_ref, v_ref)):
        for h in range(heads):
            base = pl.multiple_of(jnp.bitwise_and(off_ref[1, h], ~15), 16)
            block = ref[pl.ds(base, 16), h * dh : (h + 1) * dh].astype(F32)
            block = jnp.where(place == jnp.bitwise_and(off_ref[1, h], 15), block, 0.0)
            acc[slot(i, h) : slot(i, h) + 1, :] = jnp.sum(block, axis=0, keepdims=True)
    for i, first in ((2, 0), (3, 16)):
        for c in range(2):
            row = slot(i, c * part)
            acc[row : row + part, :] = own[first + c * part : first + (c + 1) * part, :]
    weight = row_weights(off_ref, heads, length)
    masked = jnp.where(weight > 0.0, s, NEG)
    m = jnp.max(masked, axis=1, keepdims=True)
    e = jnp.exp2(masked - m) * weight
    t = jnp.sum(e, axis=1, keepdims=True)
    d = jnp.sum(e * dp, axis=1, keepdims=True)
    lane = iota((32, 128), 1)
    table = jnp.where(lane == 0, m, jnp.where(lane == 1, t, jnp.where(lane == 2, d, 0.0)))
    table = jnp.concatenate([table, jnp.zeros((96, 128), F32)], axis=0).T[0:STAT_ROWS, :]
    high = table.astype(BF16).astype(F32)
    rest = table - high
    middle = rest.astype(BF16).astype(F32)
    low = (rest - middle).astype(BF16).astype(F32)
    table = high + pltpu.roll(middle, 32, 1) + pltpu.roll(low, 64, 1)
    for c in range(2):
        acc[c * slots + 4 * part : (c + 1) * slots, :] = table
    halves = acc[...].astype(BF16).reshape(2, slots, dh)
    repeat = load.shape[0]
    for i in range(repeat // 2):
        load[2 * i : 2 * i + 2] = halves
    copies = [
        pltpu.make_async_copy(load, load_ref.at[pl.ds(i * repeat, repeat)], sems.at[i])
        for i in range(span // repeat)
    ]
    for copy in copies:
        copy.start()
    for copy in copies:
        copy.wait()


def near_head(off_ref, h, inputs, outputs, wait, send):
    q_ref, k_ref, v_ref, g_ref, kf_ref, vf_ref = inputs
    dq_ref, dk_ref, dv_ref, ret_ref = outputs
    length, dh = q_ref.shape[0], q_ref.shape[1] // off_ref.shape[1]
    half = length // 2
    scale = dh**-0.5
    cols = slice(h * dh, (h + 1) * dh)
    wait(h)
    pair, wide = off_ref[0, h], off_ref[1, h]
    q, k, v, g = q_ref[:, cols], k_ref[:, cols], v_ref[:, cols], g_ref[:, cols]
    pick = (iota((half, length), 1) == 2 * iota((half, length), 0) + pair).astype(BF16)
    kc = dot_nn(pick, kf_ref[:, cols]).astype(BF16)
    yield
    lanes = iota((1, length), 1)
    chosen = jnp.bitwise_and(lanes, 1) == pair
    a_t = chosen.astype(F32)
    a_u = (jnp.bitwise_and(iota((length, 1), 0), 1) == pair).astype(F32)
    s1 = dot_nt(k, q)
    s2 = dot_nt(kc, q) + jnp.where(chosen, 0.0, NEG)
    vc = dot_nn(pick, vf_ref[:, cols]).astype(BF16)
    yield
    m = jnp.maximum(jnp.max(s1, axis=0, keepdims=True), jnp.max(s2, axis=0, keepdims=True))
    m = m * (scale * LOG2E)
    dp1 = dot_nt(v, g)
    dp2 = dot_nt(vc, g)
    yield
    e1 = jnp.exp2(s1 * (scale * LOG2E) - m) * (1.0 + a_t * a_u)
    e2 = jnp.exp2(s2 * (scale * LOG2E) - m)
    total = jnp.sum(e1, axis=0, keepdims=True) + jnp.sum(e2, axis=0, keepdims=True)
    part = jnp.sum(e1 * dp1, axis=0, keepdims=True) + jnp.sum(e2 * dp2, axis=0, keepdims=True)
    yield
    inverse = jnp.where(lanes == wide, 0.0, 1.0 / total)
    delta = part * inverse
    p1 = e1 * inverse
    p2 = e2 * inverse
    ds1 = (scale * p1 * (dp1 - delta)).astype(BF16)
    ds2 = (scale * p2 * (dp2 - delta)).astype(BF16)
    p1 = p1.astype(BF16)
    p2 = p2.astype(BF16)
    yield
    dk_ref[:, cols] = dot_nn(ds1, q)
    dv_ref[:, cols] = dot_nn(p1, g)
    ret_ref[:half, cols] = dot_nn(ds2, q).astype(BF16)
    ret_ref[half:, cols] = dot_nn(p2, g).astype(BF16)
    dq_ref[:, cols] = (dot_tn(k, ds1) + dot_tn(kc, ds2)).T.astype(BF16)
    send(h)
    yield


def main_kernel(
    heads, off_hbm, after_ref, own_ref, q_ref, k_ref, v_ref, g_ref, kf_ref, vf_ref,
    dq_hbm, dk_hbm, dv_hbm, ret_hbm, far_hbm,
    off_ref, dq_ref, dk_ref, dv_ref, ret_ref, far_scores, off_sem, far_sem, out_sems,
):
    offsets = pltpu.make_async_copy(off_hbm, off_ref, off_sem)
    offsets.start()
    dh = q_ref.shape[1] // heads
    near = (dq_ref, dk_ref, dv_ref, ret_ref)
    writes = []

    def wait(h):
        if h == 0:
            offsets.wait()

    def send(h):
        if h % 2 == 1:
            cols = slice((h - 1) * dh, (h + 1) * dh)
            for i, (a, b) in enumerate(zip(near, (dq_hbm, dk_hbm, dv_hbm, ret_hbm))):
                sem = out_sems.at[h // 2, i]
                copy = pltpu.make_async_copy(a.at[:, cols], b.at[:, cols], sem)
                copy.start()
                writes.append(copy)

    inputs = (q_ref, k_ref, v_ref, g_ref, kf_ref, vf_ref)
    work = [near_head(off_ref, h, inputs, near, wait, send) for h in range(heads)]
    steps, lag = 6, 2
    for turn in range(steps + lag * (heads - 1)):
        for h in reversed(range(heads)):
            if 0 <= turn - lag * h < steps:
                next(work[h])
        if turn == steps:
            own = own_ref[...].astype(F32)
            queries, grads = block_rows(own[:16, :], heads), block_rows(own[16:, :], heads)
            far_scores[:16, :] = dot_nt(queries, kf_ref[...]) * (dh**-0.5 * LOG2E)
            far_scores[16:, :] = dot_nt(grads, vf_ref[...])
            copy = pltpu.make_async_copy(far_scores, far_hbm, far_sem)
            copy.start()
            writes.append(copy)
    for copy in writes:
        copy.wait()


def wide_kernel(
    heads, span, recv_ref, mine_ref, theirs_ref, flat
):
    part, slots, dh = heads // 2, recv_ref.shape[1], recv_ref.shape[2]
    scale = dh**-0.5
    me = lax.rem(lax.axis_index("ctx"), span)
    mate = jnp.bitwise_xor(me, 1)
    first = jnp.bitwise_and(me, 1) == 0
    flat[...] = recv_ref[...].astype(F32).reshape(span * slots, dh)

    def gathered(slot):
        return flat[pl.ds(slot, span, stride=slots), :]

    even = jnp.bitwise_and(iota((8, 128), 1), 1) == 0

    def stat(index):
        x = gathered(4 * part + index)
        x = x + pltpu.roll(x, 96, 1) + pltpu.roll(x, 64, 1)
        if span < 128:
            x = jnp.concatenate([x, jnp.zeros((128 - span, 128), F32)], axis=0)
        x = x.T
        near = jnp.where(first, x[0:8, :], x[part : part + 8, :])
        other = jnp.where(first, x[16:24, :], x[16 + part : 24 + part, :])
        other = jnp.where(even, pltpu.roll(other, 127, 1), pltpu.roll(other, 1, 1))
        return near[:, :span], other[:, :span]

    (m_a, m_b), (t_a, t_b), (d_a, d_b) = stat(0), stat(1), stat(2)
    row = iota((16, span), 0)
    device = iota((span, 1), 0)
    k_w, v_w, q_w, g_w = [
        [gathered(i * part + j).astype(BF16) for j in range(part)] for i in range(4)
    ]
    m_c, t_c, d_c = [jnp.zeros((8, span), F32) for _ in range(3)]
    s_key, dp_key, s_row, dp_row = [jnp.zeros((16, span), F32) for _ in range(4)]

    def two_rows(x, j, table):
        for index, device_of in enumerate((me, mate)):
            one = jnp.sum(jnp.where(device == device_of, x, 0.0), axis=0, keepdims=True)
            table = jnp.where(row == 8 * index + j, one, table)
        return table

    for j in range(part):
        s = dot_nt(k_w[j], q_w[j]) * (scale * LOG2E)
        dp = dot_nt(v_w[j], g_w[j])
        m = jnp.max(s, axis=0, keepdims=True)
        e = jnp.exp2(s - m)
        here = row[:8] == j
        m_c = jnp.where(here, m, m_c)
        t_c = jnp.where(here, jnp.sum(e, axis=0, keepdims=True), t_c)
        d_c = jnp.where(here, jnp.sum(e * dp, axis=0, keepdims=True), d_c)
        s_key = two_rows(s, j, s_key)
        dp_key = two_rows(dp, j, dp_key)
        s_row = two_rows(dot_nt(q_w[j], k_w[j]) * (scale * LOG2E), j, s_row)
        dp_row = two_rows(dot_nt(g_w[j], v_w[j]), j, dp_row)
    m_all = jnp.maximum(jnp.maximum(m_a, m_b), m_c)
    w_a, w_b, w_c = jnp.exp2(m_a - m_all), jnp.exp2(m_b - m_all), jnp.exp2(m_c - m_all)
    inverse = 1.0 / (t_a * w_a + t_b * w_b + t_c * w_c)
    delta = (d_a * w_a + d_b * w_b + d_c * w_c) * inverse

    def twice(x):
        return jnp.concatenate([x, x], axis=0)

    def column(x, index):
        return jnp.sum(jnp.where(iota((8, span), 1) == index, x, 0.0), axis=1, keepdims=True)

    p_key = jnp.exp2(s_key - twice(m_all)) * twice(inverse)
    ds_key = scale * p_key * (dp_key - twice(delta))
    of_me = [column(x, me) for x in (m_all, inverse, delta)]
    of_mate = [column(x, mate) for x in (m_all, inverse, delta)]
    m_r, i_r, d_r = [jnp.concatenate(pair, axis=0) for pair in zip(of_me, of_mate)]
    ds_row = scale * (jnp.exp2(s_row - m_r) * i_r) * (dp_row - d_r)

    def times(left, right):
        index = jnp.bitwise_and(row, 7)
        return sum(
            dot_nn(jnp.where(index == j, left, 0.0).astype(BF16), right[j]) for j in range(part)
        )

    terms = (times(ds_row, k_w), times(ds_key, q_w), times(p_key, g_w))
    lane = iota((8, dh), 1)
    for ref, base, columns in ((mine_ref, 0, of_me + of_mate), (theirs_ref, 8, of_mate + of_me)):
        for i, term in enumerate(terms):
            ref[8 * i : 8 * i + 8, :] = term[base : base + 8, :]
        table = jnp.zeros((8, dh), F32)
        for i, value in enumerate(columns):
            table = jnp.where(lane == i, value, table)
        ref[24:32, :] = table


def final_kernel(
    heads, off_hbm, mine_ref, got_ref, own_ref, far_ref, s_ref, dp_ref,
    k_ref, kf_ref, ret, dki, dvi, far_hbm, dq_in, dq_ref, dk_ref, dv_ref,
    off_ref, far_scores, full, blocks, dko, dvo, off_sem, far_sem, block_sems, write_sems,
):
    offsets = pltpu.make_async_copy(off_hbm, off_ref, off_sem)
    offsets.start()
    scores = pltpu.make_async_copy(far_hbm, far_scores, far_sem)
    scores.start()
    length, dh = k_ref.shape[0], own_ref.shape[1]
    half, part = length // 2, heads // 2
    scale = dh**-0.5

    def place(ref, h):
        base = pl.multiple_of(jnp.bitwise_and(off_ref[1, h], ~15), 16)
        return ref.at[pl.ds(base, 16), pl.ds(h * dh, dh)]

    chunks = [slice(2 * j * dh, 2 * (j + 1) * dh) for j in range(part)]
    own, far = own_ref[...].astype(F32), far_ref[...].astype(F32)
    first = jnp.bitwise_and(lax.axis_index("ctx"), 1) == 0
    mine, got = mine_ref[...], got_ref[...]
    low, high = jnp.where(first, mine, got), jnp.where(first, got, mine)
    full[...] = jnp.zeros_like(full)
    for i in range(4):
        full[16 * i : 16 * i + part, :] = low[8 * i : 8 * i + part, :]
        full[16 * i + part : 16 * i + heads, :] = high[8 * i : 8 * i + part, :]
    dq_wide, dk_rows, dv_rows, table = [full[16 * i : 16 * i + 16, :] for i in range(4)]
    m_me, i_me, d_me = [table[:, i : i + 1] for i in range(3)]
    m_two, i_two, d_two = [
        jnp.concatenate([table[:, i : i + 1], table[:, i + 3 : i + 4]], axis=0) for i in range(3)
    ]
    offsets.wait()
    reads = [
        pltpu.make_async_copy(place(dq_in, h), blocks.at[h], block_sems.at[h]) for h in range(heads)
    ]
    for copy in reads:
        copy.start()
    weight = row_weights(off_ref, heads, length)
    p_two = jnp.exp2(jnp.where(weight > 0.0, s_ref[...] - m_two, NEG)) * weight * i_two
    ds_two = scale * p_two * (dp_ref[...] - d_two)
    met = level_one_keys(off_ref, heads, 16, length)
    scores.wait()
    p_far = jnp.exp2(jnp.where(met, far_scores[:16, :] - m_me, NEG)) * i_me
    ds_far = scale * p_far * (far_scores[16:, :] - d_me)
    dq_rows = dq_wide + own_columns(
        dot_nn(ds_two[0:16, :].astype(BF16), k_ref[...]) + dot_nn(ds_far.astype(BF16), kf_ref[...]),
        heads,
    )
    wide = offset_column(off_ref, 1, heads, 32)
    spot = (iota((32, length), 1) == wide).astype(F32)

    def spread(left, first, rows):
        high = rows.astype(BF16).astype(F32)
        left = jnp.concatenate([left, spot], axis=0).T.astype(BF16)
        parts = (own[first : first + 16, :], far[first : first + 16, :], high, rows - high)
        return left, jnp.concatenate([block_rows(part, heads) for part in parts], axis=0)

    writes = []
    for index, (base, out, out_ref, left, right) in enumerate(
        (
            (dki, dko, dk_ref) + spread(ds_two, 0, dk_rows),
            (dvi, dvo, dv_ref) + spread(p_two, 16, dv_rows),
        )
    ):
        back = slice(index * half, (index + 1) * half)
        for j, chunk in enumerate(chunks):
            for h in (2 * j, 2 * j + 1):
                cols = slice(h * dh, (h + 1) * dh)
                pick = iota((length, half), 0) == 2 * iota((length, half), 1) + off_ref[0, h]
                added = dot_nn(left, right[:, cols]) + dot_nn(pick.astype(BF16), ret[back, cols])
                out[:, cols] = (base[:, cols] + added).astype(BF16)
            sem = write_sems.at[index, j]
            copy = pltpu.make_async_copy(out.at[:, chunk], out_ref.at[:, chunk], sem)
            copy.start()
            writes.append(copy)
    for h in range(heads):
        reads[h].wait()
        here = iota((16, dh), 0) == jnp.bitwise_and(off_ref[1, h], 15)
        blocks[h] = jnp.where(here, dq_rows[h : h + 1, :], blocks[h].astype(F32)).astype(BF16)
        copy = pltpu.make_async_copy(blocks.at[h], place(dq_ref, h), block_sems.at[h])
        copy.start()
        writes.append(copy)
    for copy in writes:
        copy.wait()


def on_device(query, key, value, grad_out, offsets):
    length, width = query.shape
    heads = offsets.shape[1]
    dh = width // heads
    size = lax.axis_size("ctx")
    span = min(size, 128)
    slots = 2 * heads + STAT_ROWS
    mates = [(i, i ^ 1) for i in range(size)]
    vmem = pl.BlockSpec(memory_space=pltpu.VMEM)
    smem = pl.BlockSpec(memory_space=pltpu.SMEM)
    hbm = pl.BlockSpec(memory_space=pltpu.HBM)
    params = pltpu.CompilerParams(vmem_limit_bytes=VMEM_LIMIT)
    small = pl.CostEstimate(flops=1000, bytes_accessed=1000, transcendentals=0)
    large = pl.CostEstimate(flops=7 * 10**9, bytes_accessed=1000, transcendentals=0)

    def call(kernel, name, out_shape, in_specs, out_specs, scratch, cost=small, **kwargs):
        return pl.pallas_call(
            kernel,
            out_shape=out_shape,
            in_specs=in_specs,
            out_specs=out_specs,
            scratch_shapes=scratch,
            compiler_params=params,
            cost_estimate=cost,
            name=name,
            **kwargs,
        )

    def far_memory(*arrays):
        return [pltpu.with_memory_space_constraint(array, pltpu.HBM) for array in arrays]

    def near_memory(*arrays):
        return [pltpu.with_memory_space_constraint(array, pltpu.VMEM) for array in arrays]

    own = call(
        functools.partial(pack_kernel, heads),
        "pack_rows",
        pltpu.VMEM((32, dh), BF16),
        [smem] + [hbm] * 2,
        vmem,
        [
            pltpu.VMEM((2 * heads, 16, dh), BF16),
            pltpu.VMEM((32, dh), F32),
            pltpu.SemaphoreType.DMA((2 * heads,)),
        ],
    )(*far_memory(offsets, query, grad_out))
    far = lax.ppermute(own, "ctx", mates)
    key_far = lax.ppermute(key, "ctx", mates)
    value_far = lax.ppermute(value, "ctx", mates)
    repeat = min(span, 8)
    load, s_rows, dp_rows = call(
        functools.partial(stats_kernel, heads, span),
        "row_stats",
        (
            pltpu.HBM((span, slots, dh), BF16),
            pltpu.VMEM((32, length), F32),
            pltpu.VMEM((32, length), F32),
        ),
        [hbm] + [vmem] * 4,
        (hbm, vmem, vmem),
        [
            pltpu.SMEM(offsets.shape, jnp.int32),
            pltpu.VMEM((2 * slots, dh), F32),
            pltpu.VMEM((repeat, slots, dh), BF16),
            pltpu.SemaphoreType.DMA,
            pltpu.SemaphoreType.DMA((span // repeat,)),
        ],
    )(*far_memory(offsets), *near_memory(own, far, key, value))
    groups = None
    if size > span:
        groups = [list(range(base, base + span)) for base in range(0, size, span)]
    received = lax.all_to_all(load, "ctx", 0, 0, axis_index_groups=groups, tiled=True)
    whole = pltpu.VMEM((length, width), BF16)
    wide = pltpu.VMEM((length, width), F32)
    rows = pltpu.VMEM((32, dh), F32)
    dq, dk, dv, partial, far_scores = call(
        functools.partial(main_kernel, heads),
        "near_levels",
        (
            pltpu.HBM((length, width), BF16),
            pltpu.HBM((length, width), F32),
            pltpu.HBM((length, width), F32),
            pltpu.HBM((length, width), BF16),
            pltpu.HBM((32, length), F32),
        ),
        [hbm] + [vmem] * 8,
        (hbm,) * 5,
        [
            pltpu.SMEM(offsets.shape, jnp.int32),
            whole,
            wide,
            wide,
            whole,
            pltpu.VMEM((32, length), F32),
            pltpu.SemaphoreType.DMA,
            pltpu.SemaphoreType.DMA,
            pltpu.SemaphoreType.DMA((heads // 2, 4)),
        ],
        cost=large,
    )(
        *far_memory(offsets),
        *near_memory(s_rows, own, query, key, value, grad_out, key_far, value_far),
    )
    returned = lax.ppermute(partial, "ctx", mates)
    mine, theirs = call(
        functools.partial(wide_kernel, heads, span),
        "third_level",
        (rows, rows),
        [vmem],
        (vmem,) * 2,
        [pltpu.VMEM((span * slots, dh), F32)],
        cost=large,
    )(*near_memory(received))
    got = lax.ppermute(theirs, "ctx", mates)
    return call(
        functools.partial(final_kernel, heads),
        "join",
        (pltpu.HBM((length, width), BF16),) * 3,
        [hbm] + [vmem] * 11 + [hbm] * 2,
        (hbm,) * 3,
        [
            pltpu.SMEM(offsets.shape, jnp.int32),
            pltpu.VMEM((32, length), F32),
            pltpu.VMEM((64, dh), F32),
            pltpu.VMEM((heads, 16, dh), BF16),
            whole,
            whole,
            pltpu.SemaphoreType.DMA,
            pltpu.SemaphoreType.DMA,
            pltpu.SemaphoreType.DMA((heads,)),
            pltpu.SemaphoreType.DMA((2, heads // 2)),
        ],
        input_output_aliases={13: 0},
    )(
        *far_memory(offsets),
        *near_memory(mine, got, own, far, s_rows, dp_rows),
        *near_memory(key, key_far, returned, dk, dv),
        *far_memory(far_scores, dq),
    )


def solution(mesh):
    placed = (P("ctx", None), P("ctx", None), P("ctx", None), P("ctx", None), P())
    return jax.shard_map(
        on_device,
        mesh=mesh,
        in_specs=placed,
        out_specs=(P("ctx", None), P("ctx", None), P("ctx", None)),
        check_vma=False,
    )
```

```python
import functools

import jax
import jax.numpy as jnp
from jax import lax
from jax.experimental import pallas as pl
from jax.experimental.pallas import tpu as pltpu
from jax.sharding import PartitionSpec as P

NEG = -1e30
F32 = jnp.float32
BF16 = jnp.bfloat16
STAT_ROWS = 4
VMEM_LIMIT = 16 * 1024 * 1024
LOG2E = 1.4426950408889634


def iota(shape, dim):
    return lax.broadcasted_iota(jnp.int32, shape, dim)


def dot_nt(a, b):
    return lax.dot_general(a, b, (((1,), (1,)), ((), ())), preferred_element_type=F32)


def dot_tn(a, b):
    return lax.dot_general(a, b, (((0,), (0,)), ((), ())), preferred_element_type=F32)


def dot_nn(a, b):
    return lax.dot_general(a, b, (((1,), (0,)), ((), ())), preferred_element_type=F32)


def block_rows(rows, heads):
    row = iota(rows.shape, 0)
    return jnp.concatenate(
        [jnp.where(row == h, rows, 0.0).astype(BF16) for h in range(heads)], axis=1
    )


def own_columns(wide_rows, heads):
    dh = wide_rows.shape[1] // heads
    row = iota((16, dh), 0)
    return sum(
        jnp.where(row == h, wide_rows[:, h * dh : (h + 1) * dh], 0.0) for h in range(heads)
    )


def offset_column(off_ref, level, heads, rows):
    row = jnp.bitwise_and(iota((rows, 1), 0), 15)
    column = jnp.zeros((rows, 1), jnp.int32)
    for h in range(heads):
        column = jnp.where(row == h, off_ref[level, h], column)
    return column


def level_one_keys(off_ref, heads, rows, length):
    pair = offset_column(off_ref, 0, heads, rows)
    wide = offset_column(off_ref, 1, heads, rows)
    lane = iota((rows, length), 1)
    chosen = jnp.bitwise_and(wide, 1) == pair
    return jnp.logical_and(jnp.bitwise_and(lane, 1) == pair, chosen)


def row_weights(off_ref, heads, length):
    both = level_one_keys(off_ref, heads, 32, length).astype(F32)
    return jnp.where(iota((32, length), 0) < 16, 1.0 + both, both)


def pack_kernel(
    heads, off_ref, k_ref, v_ref, q_ref, g_ref, out_ref, spot_ref, weight_ref, buf, acc, sems
):
    length, dh = k_ref.shape[0], out_ref.shape[1]
    copies = []
    for s, ref in enumerate((k_ref, v_ref, q_ref, g_ref)):
        for h in range(heads):
            base = pl.multiple_of(jnp.bitwise_and(off_ref[1, h], ~15), 16)
            slot = s * heads + h
            copy = pltpu.make_async_copy(
                ref.at[pl.ds(base, 16), pl.ds(h * dh, dh)], buf.at[slot], sems.at[slot]
            )
            copy.start()
            copies.append(copy)
    wide = offset_column(off_ref, 1, heads, 32)
    spot_ref[...] = (iota((32, length), 1) == wide).astype(F32)
    weight_ref[...] = row_weights(off_ref, heads, length)
    acc[...] = jnp.zeros_like(acc)
    row = iota((16, dh), 0)
    for s in range(4):
        for h in range(heads):
            slot = s * heads + h
            copies[slot].wait()
            own = row == jnp.bitwise_and(off_ref[1, h], 15)
            block = jnp.where(own, buf[slot].astype(F32), 0.0)
            acc[slot : slot + 1, :] = jnp.sum(block, axis=0, keepdims=True)
    out_ref[...] = acc[...].astype(BF16)


def stats_kernel(
    heads, span, own_ref, spot_ref, weight_ref, qf_ref, gf_ref, k_ref, v_ref,
    load_ref, s_hbm, dp_hbm, far_hbm, s_ref, dp_ref, far_ref, acc, load, sems, row_sems,
):
    dh = own_ref.shape[1]
    part, slots = heads // 2, load_ref.shape[1]
    own = own_ref[...].astype(F32)
    spot = spot_ref[0:16, :].astype(BF16)

    def both_rows(array, whole, first):
        far = own_columns(dot_nn(spot, whole), heads)
        far_ref[first : first + 16, :] = far.astype(BF16)
        near = own[array * heads : array * heads + 16, :]
        return jnp.concatenate([block_rows(near, heads), block_rows(far, heads)], axis=0)

    queries, grads = both_rows(2, qf_ref[...], 0), both_rows(3, gf_ref[...], 16)
    s = dot_nt(queries, k_ref[...]) * (dh**-0.5 * LOG2E)
    dp = dot_nt(grads, v_ref[...])
    s_ref[...] = s
    dp_ref[...] = dp
    for i in range(4):
        for c in range(2):
            slot, row = c * slots + i * part, i * heads + c * part
            acc[slot : slot + part, :] = own[row : row + part, :]
    weight = weight_ref[...]
    masked = jnp.where(weight > 0.0, s, NEG)
    m = jnp.max(masked, axis=1, keepdims=True)
    e = jnp.exp2(masked - m) * weight
    t = jnp.sum(e, axis=1, keepdims=True)
    d = jnp.sum(e * dp, axis=1, keepdims=True)
    lane = iota((32, 128), 1)
    table = jnp.where(lane == 0, m, jnp.where(lane == 1, t, jnp.where(lane == 2, d, 0.0)))
    table = jnp.concatenate([table, jnp.zeros((96, 128), F32)], axis=0).T[0:STAT_ROWS, :]
    high = table.astype(BF16).astype(F32)
    rest = table - high
    middle = rest.astype(BF16).astype(F32)
    low = (rest - middle).astype(BF16).astype(F32)
    table = high + pltpu.roll(middle, 32, 1) + pltpu.roll(low, 64, 1)
    for c in range(2):
        acc[c * slots + 4 * part : (c + 1) * slots, :] = table
    halves = acc[...].astype(BF16).reshape(2, slots, dh)
    repeat = load.shape[0]
    for i in range(repeat // 2):
        load[2 * i : 2 * i + 2] = halves
    copies = [
        pltpu.make_async_copy(load, load_ref.at[pl.ds(i * repeat, repeat)], sems.at[i])
        for i in range(span // repeat)
    ]
    for i, (near, away) in enumerate(((s_ref, s_hbm), (dp_ref, dp_hbm), (far_ref, far_hbm))):
        copies.append(pltpu.make_async_copy(near, away, row_sems.at[i]))
    for copy in copies:
        copy.start()
    for copy in copies:
        copy.wait()


def near_head(off_ref, h, inputs, outputs, wait, send):
    q_ref, k_ref, v_ref, g_ref, kf_ref, vf_ref = inputs
    dq_ref, dk_ref, dv_ref, ret_ref = outputs
    length, dh = q_ref.shape[0], q_ref.shape[1] // off_ref.shape[1]
    half = length // 2
    scale = dh**-0.5
    cols = slice(h * dh, (h + 1) * dh)
    wait(h)
    pair, wide = off_ref[0, h], off_ref[1, h]
    q, k, v, g = q_ref[:, cols], k_ref[:, cols], v_ref[:, cols], g_ref[:, cols]
    pick = (iota((half, length), 1) == 2 * iota((half, length), 0) + pair).astype(BF16)
    kc = dot_nn(pick, kf_ref[:, cols]).astype(BF16)
    yield
    lanes = iota((1, length), 1)
    chosen = jnp.bitwise_and(lanes, 1) == pair
    a_t = chosen.astype(F32)
    a_u = (jnp.bitwise_and(iota((length, 1), 0), 1) == pair).astype(F32)
    s1 = dot_nt(k, q)
    s2 = dot_nt(kc, q) + jnp.where(chosen, 0.0, NEG)
    vc = dot_nn(pick, vf_ref[:, cols]).astype(BF16)
    yield
    m = jnp.maximum(jnp.max(s1, axis=0, keepdims=True), jnp.max(s2, axis=0, keepdims=True))
    m = m * (scale * LOG2E)
    dp1 = dot_nt(v, g)
    dp2 = dot_nt(vc, g)
    yield
    e1 = jnp.exp2(s1 * (scale * LOG2E) - m) * (1.0 + a_t * a_u)
    e2 = jnp.exp2(s2 * (scale * LOG2E) - m)
    total = jnp.sum(e1, axis=0, keepdims=True) + jnp.sum(e2, axis=0, keepdims=True)
    part = jnp.sum(e1 * dp1, axis=0, keepdims=True) + jnp.sum(e2 * dp2, axis=0, keepdims=True)
    yield
    inverse = jnp.where(lanes == wide, 0.0, 1.0 / total)
    delta = part * inverse
    p1 = e1 * inverse
    p2 = e2 * inverse
    ds1 = (scale * p1 * (dp1 - delta)).astype(BF16)
    ds2 = (scale * p2 * (dp2 - delta)).astype(BF16)
    p1 = p1.astype(BF16)
    p2 = p2.astype(BF16)
    yield
    dk_ref[:, cols] = dot_nn(ds1, q)
    dv_ref[:, cols] = dot_nn(p1, g)
    ret_ref[:half, cols] = dot_nn(ds2, q).astype(BF16)
    ret_ref[half:, cols] = dot_nn(p2, g).astype(BF16)
    dq_ref[:, cols] = (dot_tn(k, ds1) + dot_tn(kc, ds2)).T.astype(BF16)
    send(h)
    yield


def main_kernel(
    heads, off_hbm, after_ref, own_ref, q_ref, k_ref, v_ref, g_ref, kf_ref, vf_ref,
    dq_hbm, dk_hbm, dv_hbm, ret_hbm, far_hbm,
    off_ref, dq_ref, dk_ref, dv_ref, ret_ref, far_scores, off_sem, far_sem, out_sems,
):
    offsets = pltpu.make_async_copy(off_hbm, off_ref, off_sem)
    offsets.start()
    dh = q_ref.shape[1] // heads
    near = (dq_ref, dk_ref, dv_ref, ret_ref)
    writes = []

    def wait(h):
        if h == 0:
            offsets.wait()

    def send(h):
        if h % 2 == 1:
            cols = slice((h - 1) * dh, (h + 1) * dh)
            for i, (a, b) in enumerate(zip(near, (dq_hbm, dk_hbm, dv_hbm, ret_hbm))):
                sem = out_sems.at[h // 2, i]
                copy = pltpu.make_async_copy(a.at[:, cols], b.at[:, cols], sem)
                copy.start()
                writes.append(copy)

    inputs = (q_ref, k_ref, v_ref, g_ref, kf_ref, vf_ref)
    work = [near_head(off_ref, h, inputs, near, wait, send) for h in range(heads)]
    steps, lag = 6, 2
    for turn in range(steps + lag * (heads - 1)):
        for h in reversed(range(heads)):
            if 0 <= turn - lag * h < steps:
                next(work[h])
        if turn == steps:
            own = own_ref[...].astype(F32)
            queries = block_rows(own[2 * heads : 2 * heads + 16, :], heads)
            grads = block_rows(own[3 * heads : 3 * heads + 16, :], heads)
            far_scores[:16, :] = dot_nt(queries, kf_ref[...]) * (dh**-0.5 * LOG2E)
            far_scores[16:, :] = dot_nt(grads, vf_ref[...])
            copy = pltpu.make_async_copy(far_scores, far_hbm, far_sem)
            copy.start()
            writes.append(copy)
    for copy in writes:
        copy.wait()


def wide_kernel(
    heads, span, recv_ref, mine_ref, theirs_ref, flat
):
    part, slots, dh = heads // 2, recv_ref.shape[1], recv_ref.shape[2]
    scale = dh**-0.5
    me = lax.rem(lax.axis_index("ctx"), span)
    mate = jnp.bitwise_xor(me, 1)
    first = jnp.bitwise_and(me, 1) == 0
    flat[...] = recv_ref[...].astype(F32).reshape(span * slots, dh)

    def gathered(slot):
        return flat[pl.ds(slot, span, stride=slots), :]

    even = jnp.bitwise_and(iota((8, 128), 1), 1) == 0

    def stat(index):
        x = gathered(4 * part + index)
        x = x + pltpu.roll(x, 96, 1) + pltpu.roll(x, 64, 1)
        if span < 128:
            x = jnp.concatenate([x, jnp.zeros((128 - span, 128), F32)], axis=0)
        x = x.T
        near = jnp.where(first, x[0:8, :], x[part : part + 8, :])
        other = jnp.where(first, x[16:24, :], x[16 + part : 24 + part, :])
        other = jnp.where(even, pltpu.roll(other, 127, 1), pltpu.roll(other, 1, 1))
        return near[:, :span], other[:, :span]

    (m_a, m_b), (t_a, t_b), (d_a, d_b) = stat(0), stat(1), stat(2)
    row = iota((16, span), 0)
    device = iota((span, 1), 0)
    k_w, v_w, q_w, g_w = [
        [gathered(i * part + j).astype(BF16) for j in range(part)] for i in range(4)
    ]
    m_c, t_c, d_c = [jnp.zeros((8, span), F32) for _ in range(3)]
    s_key, dp_key, s_row, dp_row = [jnp.zeros((16, span), F32) for _ in range(4)]

    def two_rows(x, j, table):
        for index, device_of in enumerate((me, mate)):
            one = jnp.sum(jnp.where(device == device_of, x, 0.0), axis=0, keepdims=True)
            table = jnp.where(row == 8 * index + j, one, table)
        return table

    for j in range(part):
        s = dot_nt(k_w[j], q_w[j]) * (scale * LOG2E)
        dp = dot_nt(v_w[j], g_w[j])
        m = jnp.max(s, axis=0, keepdims=True)
        e = jnp.exp2(s - m)
        here = row[:8] == j
        m_c = jnp.where(here, m, m_c)
        t_c = jnp.where(here, jnp.sum(e, axis=0, keepdims=True), t_c)
        d_c = jnp.where(here, jnp.sum(e * dp, axis=0, keepdims=True), d_c)
        s_key = two_rows(s, j, s_key)
        dp_key = two_rows(dp, j, dp_key)
        s_row = two_rows(dot_nt(q_w[j], k_w[j]) * (scale * LOG2E), j, s_row)
        dp_row = two_rows(dot_nt(g_w[j], v_w[j]), j, dp_row)
    m_all = jnp.maximum(jnp.maximum(m_a, m_b), m_c)
    w_a, w_b, w_c = jnp.exp2(m_a - m_all), jnp.exp2(m_b - m_all), jnp.exp2(m_c - m_all)
    inverse = 1.0 / (t_a * w_a + t_b * w_b + t_c * w_c)
    delta = (d_a * w_a + d_b * w_b + d_c * w_c) * inverse

    def twice(x):
        return jnp.concatenate([x, x], axis=0)

    def column(x, index):
        return jnp.sum(jnp.where(iota((8, span), 1) == index, x, 0.0), axis=1, keepdims=True)

    p_key = jnp.exp2(s_key - twice(m_all)) * twice(inverse)
    ds_key = scale * p_key * (dp_key - twice(delta))
    of_me = [column(x, me) for x in (m_all, inverse, delta)]
    of_mate = [column(x, mate) for x in (m_all, inverse, delta)]
    m_r, i_r, d_r = [jnp.concatenate(pair, axis=0) for pair in zip(of_me, of_mate)]
    ds_row = scale * (jnp.exp2(s_row - m_r) * i_r) * (dp_row - d_r)

    def times(left, right):
        index = jnp.bitwise_and(row, 7)
        return sum(
            dot_nn(jnp.where(index == j, left, 0.0).astype(BF16), right[j]) for j in range(part)
        )

    terms = (times(ds_row, k_w), times(ds_key, q_w), times(p_key, g_w))
    lane = iota((8, dh), 1)
    for ref, base, columns in ((mine_ref, 0, of_me + of_mate), (theirs_ref, 8, of_mate + of_me)):
        for i, term in enumerate(terms):
            ref[8 * i : 8 * i + 8, :] = term[base : base + 8, :]
        table = jnp.zeros((8, dh), F32)
        for i, value in enumerate(columns):
            table = jnp.where(lane == i, value, table)
        ref[24:32, :] = table


def final_kernel(
    heads, off_hbm, mine_ref, got_ref, own_ref, far_ref, spot_ref, weight_ref, s_ref, dp_ref,
    k_ref, kf_ref, dki, dvi, ret_hbm, far_hbm, dq_in, dq_ref, dk_ref, dv_ref,
    off_ref, ret, far_scores, full, blocks, dko, dvo, off_sem, far_sem, ret_sems, block_sems, write_sems,
):
    offsets = pltpu.make_async_copy(off_hbm, off_ref, off_sem)
    offsets.start()
    scores = pltpu.make_async_copy(far_hbm, far_scores, far_sem)
    scores.start()
    length, dh = k_ref.shape[0], own_ref.shape[1]
    half, part = length // 2, heads // 2
    scale = dh**-0.5

    def place(ref, h):
        base = pl.multiple_of(jnp.bitwise_and(off_ref[1, h], ~15), 16)
        return ref.at[pl.ds(base, 16), pl.ds(h * dh, dh)]

    chunks = [slice(2 * j * dh, 2 * (j + 1) * dh) for j in range(part)]
    fetches = [
        pltpu.make_async_copy(ret_hbm.at[:, cols], ret.at[:, cols], ret_sems.at[j])
        for j, cols in enumerate(chunks)
    ]
    for copy in fetches:
        copy.start()
    own, far = own_ref[...].astype(F32), far_ref[...].astype(F32)
    first = jnp.bitwise_and(lax.axis_index("ctx"), 1) == 0
    mine, got = mine_ref[...], got_ref[...]
    low, high = jnp.where(first, mine, got), jnp.where(first, got, mine)
    full[...] = jnp.zeros_like(full)
    for i in range(4):
        full[16 * i : 16 * i + part, :] = low[8 * i : 8 * i + part, :]
        full[16 * i + part : 16 * i + heads, :] = high[8 * i : 8 * i + part, :]
    dq_wide, dk_rows, dv_rows, table = [full[16 * i : 16 * i + 16, :] for i in range(4)]
    m_me, i_me, d_me = [table[:, i : i + 1] for i in range(3)]
    m_two, i_two, d_two = [
        jnp.concatenate([table[:, i : i + 1], table[:, i + 3 : i + 4]], axis=0) for i in range(3)
    ]
    weight = weight_ref[...]
    p_two = jnp.exp2(jnp.where(weight > 0.0, s_ref[...] - m_two, NEG)) * weight * i_two
    ds_two = scale * p_two * (dp_ref[...] - d_two)
    met = weight[0:16, :] > 1.0
    scores.wait()
    p_far = jnp.exp2(jnp.where(met, far_scores[:16, :] - m_me, NEG)) * i_me
    ds_far = scale * p_far * (far_scores[16:, :] - d_me)
    dq_rows = dq_wide + own_columns(
        dot_nn(ds_two[0:16, :].astype(BF16), k_ref[...]) + dot_nn(ds_far.astype(BF16), kf_ref[...]),
        heads,
    )
    spot = spot_ref[...]
    offsets.wait()
    reads = [
        pltpu.make_async_copy(place(dq_in, h), blocks.at[h], block_sems.at[h]) for h in range(heads)
    ]
    for copy in reads:
        copy.start()

    def spread(left, array, rows):
        near = own[(array + 2) * heads : (array + 2) * heads + 16, :]
        high = rows.astype(BF16).astype(F32)
        left = jnp.concatenate([left, spot], axis=0).T.astype(BF16)
        parts = (near, far[16 * array : 16 * array + 16, :], high, rows - high)
        return left, jnp.concatenate([block_rows(part, heads) for part in parts], axis=0)

    writes = []
    for index, (base, out, out_ref, left, right) in enumerate(
        (
            (dki, dko, dk_ref) + spread(ds_two, 0, dk_rows),
            (dvi, dvo, dv_ref) + spread(p_two, 1, dv_rows),
        )
    ):
        back = slice(index * half, (index + 1) * half)
        for j, chunk in enumerate(chunks):
            if index == 0:
                fetches[j].wait()
            for h in (2 * j, 2 * j + 1):
                cols = slice(h * dh, (h + 1) * dh)
                pick = iota((length, half), 0) == 2 * iota((length, half), 1) + off_ref[0, h]
                added = dot_nn(left, right[:, cols]) + dot_nn(pick.astype(BF16), ret[back, cols])
                out[:, cols] = (base[:, cols] + added).astype(BF16)
            sem = write_sems.at[index, j]
            copy = pltpu.make_async_copy(out.at[:, chunk], out_ref.at[:, chunk], sem)
            copy.start()
            writes.append(copy)
    for h in range(heads):
        reads[h].wait()
        here = iota((16, dh), 0) == jnp.bitwise_and(off_ref[1, h], 15)
        blocks[h] = jnp.where(here, dq_rows[h : h + 1, :], blocks[h].astype(F32)).astype(BF16)
        copy = pltpu.make_async_copy(blocks.at[h], place(dq_ref, h), block_sems.at[h])
        copy.start()
        writes.append(copy)
    for copy in writes:
        copy.wait()


def on_device(query, key, value, grad_out, offsets):
    length, width = query.shape
    heads = offsets.shape[1]
    dh = width // heads
    size = lax.axis_size("ctx")
    span = min(size, 128)
    slots = 2 * heads + STAT_ROWS
    mates = [(i, i ^ 1) for i in range(size)]
    vmem = pl.BlockSpec(memory_space=pltpu.VMEM)
    smem = pl.BlockSpec(memory_space=pltpu.SMEM)
    hbm = pl.BlockSpec(memory_space=pltpu.HBM)
    params = pltpu.CompilerParams(vmem_limit_bytes=VMEM_LIMIT)
    small = pl.CostEstimate(flops=1000, bytes_accessed=1000, transcendentals=0)
    large = pl.CostEstimate(flops=7 * 10**9, bytes_accessed=1000, transcendentals=0)

    def call(kernel, name, out_shape, in_specs, out_specs, scratch, cost=small, **kwargs):
        return pl.pallas_call(
            kernel,
            out_shape=out_shape,
            in_specs=in_specs,
            out_specs=out_specs,
            scratch_shapes=scratch,
            compiler_params=params,
            cost_estimate=cost,
            name=name,
            **kwargs,
        )

    def far_memory(*arrays):
        return [pltpu.with_memory_space_constraint(array, pltpu.HBM) for array in arrays]

    def near_memory(*arrays):
        return [pltpu.with_memory_space_constraint(array, pltpu.VMEM) for array in arrays]

    query_far = lax.ppermute(query, "ctx", mates)
    grad_far = lax.ppermute(grad_out, "ctx", mates)
    table = pltpu.VMEM((32, length), F32)
    own, spot, weight = call(
        functools.partial(pack_kernel, heads),
        "pack_rows",
        (pltpu.VMEM((48, dh), BF16), table, table),
        [smem] + [hbm] * 4,
        (vmem,) * 3,
        [
            pltpu.VMEM((4 * heads, 16, dh), BF16),
            pltpu.VMEM((48, dh), F32),
            pltpu.SemaphoreType.DMA((4 * heads,)),
        ],
        cost=large,
    )(*far_memory(offsets, key, value, query, grad_out))
    key_later, value_later, own = lax.optimization_barrier((key, value, own))
    key_far = lax.ppermute(key_later, "ctx", mates)
    value_far = lax.ppermute(value_later, "ctx", mates)
    repeat = min(span, 8)
    load, s_rows, dp_rows, far = call(
        functools.partial(stats_kernel, heads, span),
        "row_stats",
        (
            pltpu.HBM((span, slots, dh), BF16),
            pltpu.HBM((32, length), F32),
            pltpu.HBM((32, length), F32),
            pltpu.HBM((32, dh), BF16),
        ),
        [vmem] * 7,
        (hbm,) * 4,
        [
            table,
            table,
            pltpu.VMEM((32, dh), BF16),
            pltpu.VMEM((2 * slots, dh), F32),
            pltpu.VMEM((repeat, slots, dh), BF16),
            pltpu.SemaphoreType.DMA((span // repeat,)),
            pltpu.SemaphoreType.DMA((3,)),
        ],
    )(*near_memory(own, spot, weight, query_far, grad_far, key, value))
    groups = None
    if size > span:
        groups = [list(range(base, base + span)) for base in range(0, size, span)]
    received = lax.all_to_all(load, "ctx", 0, 0, axis_index_groups=groups, tiled=True)
    whole = pltpu.VMEM((length, width), BF16)
    wide = pltpu.VMEM((length, width), F32)
    rows = pltpu.VMEM((32, dh), F32)
    dq, dk, dv, partial, far_scores = call(
        functools.partial(main_kernel, heads),
        "near_levels",
        (
            pltpu.HBM((length, width), BF16),
            pltpu.HBM((length, width), F32),
            pltpu.HBM((length, width), F32),
            pltpu.HBM((length, width), BF16),
            pltpu.HBM((32, length), F32),
        ),
        [hbm] * 2 + [vmem] * 7,
        (hbm,) * 5,
        [
            pltpu.SMEM(offsets.shape, jnp.int32),
            whole,
            wide,
            wide,
            whole,
            pltpu.VMEM((32, length), F32),
            pltpu.SemaphoreType.DMA,
            pltpu.SemaphoreType.DMA,
            pltpu.SemaphoreType.DMA((heads // 2, 4)),
        ],
        cost=large,
    )(
        *far_memory(offsets, s_rows),
        *near_memory(own, query, key, value, grad_out, key_far, value_far),
    )
    returned = lax.ppermute(partial, "ctx", mates)
    mine, theirs = call(
        functools.partial(wide_kernel, heads, span),
        "third_level",
        (rows, rows),
        [vmem],
        (vmem,) * 2,
        [pltpu.VMEM((span * slots, dh), F32)],
        cost=large,
    )(*near_memory(received))
    got = lax.ppermute(theirs, "ctx", mates)
    return call(
        functools.partial(final_kernel, heads),
        "join",
        (pltpu.HBM((length, width), BF16),) * 3,
        [hbm] + [vmem] * 12 + [hbm] * 3,
        (hbm,) * 3,
        [
            pltpu.SMEM(offsets.shape, jnp.int32),
            whole,
            pltpu.VMEM((32, length), F32),
            pltpu.VMEM((64, dh), F32),
            pltpu.VMEM((heads, 16, dh), BF16),
            whole,
            whole,
            pltpu.SemaphoreType.DMA,
            pltpu.SemaphoreType.DMA,
            pltpu.SemaphoreType.DMA((heads // 2,)),
            pltpu.SemaphoreType.DMA((heads,)),
            pltpu.SemaphoreType.DMA((2, heads // 2)),
        ],
        input_output_aliases={15: 0},
    )(
        *far_memory(offsets),
        *near_memory(mine, got, own, far, spot, weight, s_rows, dp_rows),
        *near_memory(key, key_far, dk, dv),
        *far_memory(returned, far_scores, dq),
    )


def solution(mesh):
    placed = (P("ctx", None), P("ctx", None), P("ctx", None), P("ctx", None), P())
    return jax.shard_map(
        on_device,
        mesh=mesh,
        in_specs=placed,
        out_specs=(P("ctx", None), P("ctx", None), P("ctx", None)),
        check_vma=False,
    )
```

```python
import functools

import jax
import jax.numpy as jnp
from jax import lax
from jax.experimental import pallas as pl
from jax.experimental.pallas import tpu as pltpu
from jax.sharding import PartitionSpec as P

NEG = -1e30
F32 = jnp.float32
BF16 = jnp.bfloat16
STAT_ROWS = 4
VMEM_LIMIT = 16 * 1024 * 1024
LOG2E = 1.4426950408889634


def iota(shape, dim):
    return lax.broadcasted_iota(jnp.int32, shape, dim)


def dot_nt(a, b):
    return lax.dot_general(a, b, (((1,), (1,)), ((), ())), preferred_element_type=F32)


def dot_tn(a, b):
    return lax.dot_general(a, b, (((0,), (0,)), ((), ())), preferred_element_type=F32)


def dot_nn(a, b):
    return lax.dot_general(a, b, (((1,), (0,)), ((), ())), preferred_element_type=F32)


def block_rows(rows, heads):
    row = iota(rows.shape, 0)
    return jnp.concatenate(
        [jnp.where(row == h, rows, 0.0).astype(BF16) for h in range(heads)], axis=1
    )


def own_columns(wide_rows, heads):
    dh = wide_rows.shape[1] // heads
    row = iota((16, dh), 0)
    return sum(
        jnp.where(row == h, wide_rows[:, h * dh : (h + 1) * dh], 0.0) for h in range(heads)
    )


def offset_column(off_ref, level, heads, rows):
    row = jnp.bitwise_and(iota((rows, 1), 0), 15)
    column = jnp.zeros((rows, 1), jnp.int32)
    for h in range(heads):
        column = jnp.where(row == h, off_ref[level, h], column)
    return column


def level_one_keys(off_ref, heads, rows, length):
    pair = offset_column(off_ref, 0, heads, rows)
    wide = offset_column(off_ref, 1, heads, rows)
    lane = iota((rows, length), 1)
    chosen = jnp.bitwise_and(wide, 1) == pair
    return jnp.logical_and(jnp.bitwise_and(lane, 1) == pair, chosen)


def row_weights(off_ref, heads, length):
    both = level_one_keys(off_ref, heads, 32, length).astype(F32)
    return jnp.where(iota((32, length), 0) < 16, 1.0 + both, both)


def pack_kernel(
    heads, off_ref, k_ref, v_ref, q_ref, g_ref, out_ref, spot_ref, weight_ref, buf, acc, sems
):
    length, dh = k_ref.shape[0], out_ref.shape[1]
    copies = []
    for s, ref in enumerate((k_ref, v_ref, q_ref, g_ref)):
        for h in range(heads):
            base = pl.multiple_of(jnp.bitwise_and(off_ref[1, h], ~15), 16)
            slot = s * heads + h
            copy = pltpu.make_async_copy(
                ref.at[pl.ds(base, 16), pl.ds(h * dh, dh)], buf.at[slot], sems.at[slot]
            )
            copy.start()
            copies.append(copy)
    wide = offset_column(off_ref, 1, heads, 32)
    spot_ref[...] = (iota((32, length), 1) == wide).astype(F32)
    weight_ref[...] = row_weights(off_ref, heads, length)
    acc[...] = jnp.zeros_like(acc)
    row = iota((16, dh), 0)
    for s in range(4):
        for h in range(heads):
            slot = s * heads + h
            copies[slot].wait()
            own = row == jnp.bitwise_and(off_ref[1, h], 15)
            block = jnp.where(own, buf[slot].astype(F32), 0.0)
            acc[slot : slot + 1, :] = jnp.sum(block, axis=0, keepdims=True)
    out_ref[...] = acc[...].astype(BF16)


def stats_kernel(
    heads, span, own_ref, spot_ref, weight_ref, qf_ref, gf_ref, k_ref, v_ref,
    load_ref, s_hbm, dp_hbm, far_hbm, s_ref, dp_ref, far_ref, acc, load, sems, row_sems,
):
    dh = own_ref.shape[1]
    part, slots = heads // 2, load_ref.shape[1]
    own = own_ref[...].astype(F32)
    spot = spot_ref[0:16, :].astype(BF16)

    def both_rows(array, whole, first):
        far = own_columns(dot_nn(spot, whole), heads)
        far_ref[first : first + 16, :] = far.astype(BF16)
        near = own[array * heads : array * heads + 16, :]
        return jnp.concatenate([block_rows(near, heads), block_rows(far, heads)], axis=0)

    queries, grads = both_rows(2, qf_ref[...], 0), both_rows(3, gf_ref[...], 16)
    s = dot_nt(queries, k_ref[...]) * (dh**-0.5 * LOG2E)
    dp = dot_nt(grads, v_ref[...])
    s_ref[...] = s
    dp_ref[...] = dp
    for i in range(4):
        for c in range(2):
            slot, row = c * slots + i * part, i * heads + c * part
            acc[slot : slot + part, :] = own[row : row + part, :]
    weight = weight_ref[...]
    masked = jnp.where(weight > 0.0, s, NEG)
    m = jnp.max(masked, axis=1, keepdims=True)
    e = jnp.exp2(masked - m) * weight
    t = jnp.sum(e, axis=1, keepdims=True)
    d = jnp.sum(e * dp, axis=1, keepdims=True)
    lane = iota((32, 128), 1)
    table = jnp.where(lane == 0, m, jnp.where(lane == 1, t, jnp.where(lane == 2, d, 0.0)))
    table = jnp.concatenate([table, jnp.zeros((96, 128), F32)], axis=0).T[0:STAT_ROWS, :]
    high = table.astype(BF16).astype(F32)
    rest = table - high
    middle = rest.astype(BF16).astype(F32)
    low = (rest - middle).astype(BF16).astype(F32)
    table = high + pltpu.roll(middle, 32, 1) + pltpu.roll(low, 64, 1)
    for c in range(2):
        acc[c * slots + 4 * part : (c + 1) * slots, :] = table
    halves = acc[...].astype(BF16).reshape(2, slots, dh)
    repeat = load.shape[0]
    for i in range(repeat // 2):
        load[2 * i : 2 * i + 2] = halves
    copies = [
        pltpu.make_async_copy(load, load_ref.at[pl.ds(i * repeat, repeat)], sems.at[i])
        for i in range(span // repeat)
    ]
    for i, (near, away) in enumerate(((s_ref, s_hbm), (dp_ref, dp_hbm), (far_ref, far_hbm))):
        copies.append(pltpu.make_async_copy(near, away, row_sems.at[i]))
    for copy in copies:
        copy.start()
    for copy in copies:
        copy.wait()


def near_head(off_ref, h, inputs, outputs, waits, send):
    q_ref, k_ref, v_ref, g_ref, kf_ref, vf_ref = inputs
    dq_ref, dk_ref, dv_ref, ret_ref = outputs
    length, dh = q_ref.shape[0], q_ref.shape[1] // off_ref.shape[1]
    half = length // 2
    scale = dh**-0.5
    cols = slice(h * dh, (h + 1) * dh)
    q, k, v, g = q_ref[:, cols], k_ref[:, cols], v_ref[:, cols], g_ref[:, cols]
    if h == 0:
        s1, dp1 = dot_nt(k, q), dot_nt(v, g)
        waits[0].wait()
    pair, wide = off_ref[0, h], off_ref[1, h]
    pick = (iota((half, length), 1) == 2 * iota((half, length), 0) + pair).astype(BF16)
    kc = dot_nn(pick, kf_ref[:, cols]).astype(BF16)
    yield
    lanes = iota((1, length), 1)
    chosen = jnp.bitwise_and(lanes, 1) == pair
    a_t = chosen.astype(F32)
    a_u = (jnp.bitwise_and(iota((length, 1), 0), 1) == pair).astype(F32)
    if h > 0:
        s1 = dot_nt(k, q)
    s2 = dot_nt(kc, q) + jnp.where(chosen, 0.0, NEG)
    if h == 0:
        waits[1].wait()
    vc = dot_nn(pick, vf_ref[:, cols]).astype(BF16)
    yield
    m = jnp.maximum(jnp.max(s1, axis=0, keepdims=True), jnp.max(s2, axis=0, keepdims=True))
    m = m * (scale * LOG2E)
    if h > 0:
        dp1 = dot_nt(v, g)
    dp2 = dot_nt(vc, g)
    yield
    e1 = jnp.exp2(s1 * (scale * LOG2E) - m) * (1.0 + a_t * a_u)
    e2 = jnp.exp2(s2 * (scale * LOG2E) - m)
    total = jnp.sum(e1, axis=0, keepdims=True) + jnp.sum(e2, axis=0, keepdims=True)
    part = jnp.sum(e1 * dp1, axis=0, keepdims=True) + jnp.sum(e2 * dp2, axis=0, keepdims=True)
    yield
    inverse = jnp.where(lanes == wide, 0.0, 1.0 / total)
    delta = part * inverse
    p1 = e1 * inverse
    p2 = e2 * inverse
    ds1 = (scale * p1 * (dp1 - delta)).astype(BF16)
    ds2 = (scale * p2 * (dp2 - delta)).astype(BF16)
    p1 = p1.astype(BF16)
    p2 = p2.astype(BF16)
    yield
    dk_ref[:, cols] = dot_nn(ds1, q)
    dv_ref[:, cols] = dot_nn(p1, g)
    ret_ref[:half, cols] = dot_nn(ds2, q).astype(BF16)
    ret_ref[half:, cols] = dot_nn(p2, g).astype(BF16)
    dq_ref[:, cols] = (dot_tn(k, ds1) + dot_tn(kc, ds2)).T.astype(BF16)
    send(h)
    yield


def main_kernel(
    heads, off_hbm, after_ref, vf_hbm, own_ref, q_ref, k_ref, v_ref, g_ref, kf_ref,
    dq_hbm, dk_hbm, dv_hbm, ret_hbm, far_hbm, blocks_hbm,
    off_ref, vf_ref, dq_ref, dk_ref, dv_ref, ret_ref, far_scores, blocks,
    off_sem, in_sem, far_sem, block_sem, out_sems,
):
    offsets = pltpu.make_async_copy(off_hbm, off_ref, off_sem)
    offsets.start()
    values = pltpu.make_async_copy(vf_hbm, vf_ref, in_sem)
    values.start()
    dh = q_ref.shape[1] // heads
    near = (dq_ref, dk_ref, dv_ref, ret_ref)
    writes = []

    def send(h):
        base = pl.multiple_of(jnp.bitwise_and(off_ref[1, h], ~15), 16)
        blocks[h] = dq_ref[pl.ds(base, 16), h * dh : (h + 1) * dh]
        if h == heads - 1:
            copy = pltpu.make_async_copy(blocks, blocks_hbm, block_sem)
            copy.start()
            writes.append(copy)
        if h % 2 == 1:
            cols = slice((h - 1) * dh, (h + 1) * dh)
            for i, (a, b) in enumerate(zip(near, (dq_hbm, dk_hbm, dv_hbm, ret_hbm))):
                sem = out_sems.at[h // 2, i]
                copy = pltpu.make_async_copy(a.at[:, cols], b.at[:, cols], sem)
                copy.start()
                writes.append(copy)

    inputs = (q_ref, k_ref, v_ref, g_ref, kf_ref, vf_ref)
    work = [near_head(off_ref, h, inputs, near, (offsets, values), send) for h in range(heads)]
    steps, lag = 6, 2
    for turn in range(steps + lag * (heads - 1)):
        for h in reversed(range(heads)):
            if 0 <= turn - lag * h < steps:
                next(work[h])
        if turn == steps:
            own = own_ref[...].astype(F32)
            queries = block_rows(own[2 * heads : 2 * heads + 16, :], heads)
            grads = block_rows(own[3 * heads : 3 * heads + 16, :], heads)
            far_scores[:16, :] = dot_nt(queries, kf_ref[...]) * (dh**-0.5 * LOG2E)
            far_scores[16:, :] = dot_nt(grads, vf_ref[...])
            copy = pltpu.make_async_copy(far_scores, far_hbm, far_sem)
            copy.start()
            writes.append(copy)
    for copy in writes:
        copy.wait()


def wide_kernel(
    heads, span, recv_ref, mine_ref, theirs_ref, flat
):
    part, slots, dh = heads // 2, recv_ref.shape[1], recv_ref.shape[2]
    scale = dh**-0.5
    me = lax.rem(lax.axis_index("ctx"), span)
    mate = jnp.bitwise_xor(me, 1)
    first = jnp.bitwise_and(me, 1) == 0
    flat[...] = recv_ref[...].astype(F32).reshape(span * slots, dh)

    def gathered(slot):
        return flat[pl.ds(slot, span, stride=slots), :]

    even = jnp.bitwise_and(iota((8, 128), 1), 1) == 0

    def stat(index):
        x = gathered(4 * part + index)
        x = x + pltpu.roll(x, 96, 1) + pltpu.roll(x, 64, 1)
        if span < 128:
            x = jnp.concatenate([x, jnp.zeros((128 - span, 128), F32)], axis=0)
        x = x.T
        near = jnp.where(first, x[0:8, :], x[part : part + 8, :])
        other = jnp.where(first, x[16:24, :], x[16 + part : 24 + part, :])
        other = jnp.where(even, pltpu.roll(other, 127, 1), pltpu.roll(other, 1, 1))
        return near[:, :span], other[:, :span]

    (m_a, m_b), (t_a, t_b), (d_a, d_b) = stat(0), stat(1), stat(2)
    row = iota((16, span), 0)
    device = iota((span, 1), 0)
    k_w, v_w, q_w, g_w = [
        [gathered(i * part + j).astype(BF16) for j in range(part)] for i in range(4)
    ]
    m_c, t_c, d_c = [jnp.zeros((8, span), F32) for _ in range(3)]
    s_key, dp_key, s_row, dp_row = [jnp.zeros((16, span), F32) for _ in range(4)]

    def two_rows(x, j, table):
        for index, device_of in enumerate((me, mate)):
            one = jnp.sum(jnp.where(device == device_of, x, 0.0), axis=0, keepdims=True)
            table = jnp.where(row == 8 * index + j, one, table)
        return table

    for j in range(part):
        s = dot_nt(k_w[j], q_w[j]) * (scale * LOG2E)
        dp = dot_nt(v_w[j], g_w[j])
        m = jnp.max(s, axis=0, keepdims=True)
        e = jnp.exp2(s - m)
        here = row[:8] == j
        m_c = jnp.where(here, m, m_c)
        t_c = jnp.where(here, jnp.sum(e, axis=0, keepdims=True), t_c)
        d_c = jnp.where(here, jnp.sum(e * dp, axis=0, keepdims=True), d_c)
        s_key = two_rows(s, j, s_key)
        dp_key = two_rows(dp, j, dp_key)
        s_row = two_rows(dot_nt(q_w[j], k_w[j]) * (scale * LOG2E), j, s_row)
        dp_row = two_rows(dot_nt(g_w[j], v_w[j]), j, dp_row)
    m_all = jnp.maximum(jnp.maximum(m_a, m_b), m_c)
    w_a, w_b, w_c = jnp.exp2(m_a - m_all), jnp.exp2(m_b - m_all), jnp.exp2(m_c - m_all)
    inverse = 1.0 / (t_a * w_a + t_b * w_b + t_c * w_c)
    delta = (d_a * w_a + d_b * w_b + d_c * w_c) * inverse

    def twice(x):
        return jnp.concatenate([x, x], axis=0)

    def column(x, index):
        return jnp.sum(jnp.where(iota((8, span), 1) == index, x, 0.0), axis=1, keepdims=True)

    p_key = jnp.exp2(s_key - twice(m_all)) * twice(inverse)
    ds_key = scale * p_key * (dp_key - twice(delta))
    of_me = [column(x, me) for x in (m_all, inverse, delta)]
    of_mate = [column(x, mate) for x in (m_all, inverse, delta)]
    m_r, i_r, d_r = [jnp.concatenate(pair, axis=0) for pair in zip(of_me, of_mate)]
    ds_row = scale * (jnp.exp2(s_row - m_r) * i_r) * (dp_row - d_r)

    def times(left, right):
        index = jnp.bitwise_and(row, 7)
        return sum(
            dot_nn(jnp.where(index == j, left, 0.0).astype(BF16), right[j]) for j in range(part)
        )

    terms = (times(ds_row, k_w), times(ds_key, q_w), times(p_key, g_w))
    lane = iota((8, dh), 1)
    for ref, base, columns in ((mine_ref, 0, of_me + of_mate), (theirs_ref, 8, of_mate + of_me)):
        for i, term in enumerate(terms):
            ref[8 * i : 8 * i + 8, :] = term[base : base + 8, :]
        table = jnp.zeros((8, dh), F32)
        for i, value in enumerate(columns):
            table = jnp.where(lane == i, value, table)
        ref[24:32, :] = table


def final_kernel(
    heads, off_hbm, mine_ref, got_ref, own_ref, far_ref, spot_ref, weight_ref, s_ref, dp_ref,
    dki, dvi, blocks_in, ret, k_hbm, kf_hbm, far_hbm, dq_in, dq_ref, dk_ref, dv_ref,
    off_ref, k_ref, kf_ref, far_scores, full, blocks, dko, dvo, off_sem, key_sems, far_sem, block_sems, write_sems,
):
    offsets = pltpu.make_async_copy(off_hbm, off_ref, off_sem)
    offsets.start()
    scores = pltpu.make_async_copy(far_hbm, far_scores, far_sem)
    scores.start()
    keys = [
        pltpu.make_async_copy(k_hbm, k_ref, key_sems.at[0]),
        pltpu.make_async_copy(kf_hbm, kf_ref, key_sems.at[1]),
    ]
    for copy in keys:
        copy.start()
    length, dh = k_hbm.shape[0], own_ref.shape[1]
    half, part = length // 2, heads // 2
    scale = dh**-0.5

    def place(ref, h):
        base = pl.multiple_of(jnp.bitwise_and(off_ref[1, h], ~15), 16)
        return ref.at[pl.ds(base, 16), pl.ds(h * dh, dh)]

    chunks = [slice(2 * j * dh, 2 * (j + 1) * dh) for j in range(part)]
    own, far = own_ref[...].astype(F32), far_ref[...].astype(F32)
    first = jnp.bitwise_and(lax.axis_index("ctx"), 1) == 0
    mine, got = mine_ref[...], got_ref[...]
    low, high = jnp.where(first, mine, got), jnp.where(first, got, mine)
    full[...] = jnp.zeros_like(full)
    for i in range(4):
        full[16 * i : 16 * i + part, :] = low[8 * i : 8 * i + part, :]
        full[16 * i + part : 16 * i + heads, :] = high[8 * i : 8 * i + part, :]
    dq_wide, dk_rows, dv_rows, table = [full[16 * i : 16 * i + 16, :] for i in range(4)]
    m_me, i_me, d_me = [table[:, i : i + 1] for i in range(3)]
    m_two, i_two, d_two = [
        jnp.concatenate([table[:, i : i + 1], table[:, i + 3 : i + 4]], axis=0) for i in range(3)
    ]
    weight = weight_ref[...]
    p_two = jnp.exp2(jnp.where(weight > 0.0, s_ref[...] - m_two, NEG)) * weight * i_two
    ds_two = scale * p_two * (dp_ref[...] - d_two)
    met = weight[0:16, :] > 1.0
    scores.wait()
    p_far = jnp.exp2(jnp.where(met, far_scores[:16, :] - m_me, NEG)) * i_me
    ds_far = scale * p_far * (far_scores[16:, :] - d_me)
    spot = spot_ref[...]
    offsets.wait()
    writes = []

    def spread(left, array, rows):
        near = own[(array + 2) * heads : (array + 2) * heads + 16, :]
        high = rows.astype(BF16).astype(F32)
        left = jnp.concatenate([left, spot], axis=0).T.astype(BF16)
        parts = (near, far[16 * array : 16 * array + 16, :], high, rows - high)
        return left, jnp.concatenate([block_rows(part, heads) for part in parts], axis=0)

    for index, (base, out, out_ref, left, right) in enumerate(
        (
            (dki, dko, dk_ref) + spread(ds_two, 0, dk_rows),
            (dvi, dvo, dv_ref) + spread(p_two, 1, dv_rows),
        )
    ):
        back = slice(index * half, (index + 1) * half)
        for j, chunk in enumerate(chunks):
            for h in (2 * j, 2 * j + 1):
                cols = slice(h * dh, (h + 1) * dh)
                pick = iota((length, half), 0) == 2 * iota((length, half), 1) + off_ref[0, h]
                added = dot_nn(left, right[:, cols]) + dot_nn(pick.astype(BF16), ret[back, cols])
                out[:, cols] = (base[:, cols] + added).astype(BF16)
            sem = write_sems.at[index, j]
            copy = pltpu.make_async_copy(out.at[:, chunk], out_ref.at[:, chunk], sem)
            copy.start()
            writes.append(copy)
    for copy in keys:
        copy.wait()
    dq_rows = dq_wide + own_columns(
        dot_nn(ds_two[0:16, :].astype(BF16), k_ref[...]) + dot_nn(ds_far.astype(BF16), kf_ref[...]),
        heads,
    )
    for h in range(heads):
        here = iota((16, dh), 0) == jnp.bitwise_and(off_ref[1, h], 15)
        block = jnp.where(here, dq_rows[h : h + 1, :], blocks_in[h].astype(F32))
        blocks[h] = block.astype(BF16)
        copy = pltpu.make_async_copy(blocks.at[h], place(dq_ref, h), block_sems.at[h])
        copy.start()
        writes.append(copy)
    for copy in writes:
        copy.wait()


def on_device(query, key, value, grad_out, offsets):
    length, width = query.shape
    heads = offsets.shape[1]
    dh = width // heads
    size = lax.axis_size("ctx")
    span = min(size, 128)
    slots = 2 * heads + STAT_ROWS
    mates = [(i, i ^ 1) for i in range(size)]
    vmem = pl.BlockSpec(memory_space=pltpu.VMEM)
    smem = pl.BlockSpec(memory_space=pltpu.SMEM)
    hbm = pl.BlockSpec(memory_space=pltpu.HBM)
    params = pltpu.CompilerParams(vmem_limit_bytes=VMEM_LIMIT)
    small = pl.CostEstimate(flops=1000, bytes_accessed=1000, transcendentals=0)
    large = pl.CostEstimate(flops=7 * 10**9, bytes_accessed=1000, transcendentals=0)

    def call(kernel, name, out_shape, in_specs, out_specs, scratch, cost=small, **kwargs):
        return pl.pallas_call(
            kernel,
            out_shape=out_shape,
            in_specs=in_specs,
            out_specs=out_specs,
            scratch_shapes=scratch,
            compiler_params=params,
            cost_estimate=cost,
            name=name,
            **kwargs,
        )

    def far_memory(*arrays):
        return [pltpu.with_memory_space_constraint(array, pltpu.HBM) for array in arrays]

    def near_memory(*arrays):
        return [pltpu.with_memory_space_constraint(array, pltpu.VMEM) for array in arrays]

    query_far = lax.ppermute(query, "ctx", mates)
    grad_far = lax.ppermute(grad_out, "ctx", mates)
    table = pltpu.VMEM((32, length), F32)
    own, spot, weight = call(
        functools.partial(pack_kernel, heads),
        "pack_rows",
        (pltpu.VMEM((48, dh), BF16), table, table),
        [smem] + [hbm] * 4,
        (vmem,) * 3,
        [
            pltpu.VMEM((4 * heads, 16, dh), BF16),
            pltpu.VMEM((48, dh), F32),
            pltpu.SemaphoreType.DMA((4 * heads,)),
        ],
        cost=large,
    )(*far_memory(offsets, key, value, query, grad_out))
    key_later, value_later, own = lax.optimization_barrier((key, value, own))
    key_far = lax.ppermute(key_later, "ctx", mates)
    value_far = lax.ppermute(value_later, "ctx", mates)
    repeat = min(span, 8)
    load, s_rows, dp_rows, far = call(
        functools.partial(stats_kernel, heads, span),
        "row_stats",
        (
            pltpu.HBM((span, slots, dh), BF16),
            pltpu.HBM((32, length), F32),
            pltpu.HBM((32, length), F32),
            pltpu.HBM((32, dh), BF16),
        ),
        [vmem] * 7,
        (hbm,) * 4,
        [
            table,
            table,
            pltpu.VMEM((32, dh), BF16),
            pltpu.VMEM((2 * slots, dh), F32),
            pltpu.VMEM((repeat, slots, dh), BF16),
            pltpu.SemaphoreType.DMA((span // repeat,)),
            pltpu.SemaphoreType.DMA((3,)),
        ],
    )(*near_memory(own, spot, weight, query_far, grad_far, key, value))
    groups = None
    if size > span:
        groups = [list(range(base, base + span)) for base in range(0, size, span)]
    received = lax.all_to_all(load, "ctx", 0, 0, axis_index_groups=groups, tiled=True)
    whole = pltpu.VMEM((length, width), BF16)
    wide = pltpu.VMEM((length, width), F32)
    rows = pltpu.VMEM((32, dh), F32)
    dq, dk, dv, partial, far_scores, blocks = call(
        functools.partial(main_kernel, heads),
        "near_levels",
        (
            pltpu.HBM((length, width), BF16),
            pltpu.HBM((length, width), F32),
            pltpu.HBM((length, width), F32),
            pltpu.HBM((length, width), BF16),
            pltpu.HBM((32, length), F32),
            pltpu.HBM((heads, 16, dh), BF16),
        ),
        [hbm] * 3 + [vmem] * 6,
        (hbm,) * 6,
        [
            pltpu.SMEM(offsets.shape, jnp.int32),
            whole,
            whole,
            wide,
            wide,
            whole,
            pltpu.VMEM((32, length), F32),
            pltpu.VMEM((heads, 16, dh), BF16),
            pltpu.SemaphoreType.DMA,
            pltpu.SemaphoreType.DMA,
            pltpu.SemaphoreType.DMA,
            pltpu.SemaphoreType.DMA,
            pltpu.SemaphoreType.DMA((heads // 2, 4)),
        ],
        cost=large,
    )(
        *far_memory(offsets, s_rows, value_far),
        *near_memory(own, query, key, value, grad_out, key_far),
    )
    returned = lax.ppermute(partial, "ctx", mates)
    mine, theirs = call(
        functools.partial(wide_kernel, heads, span),
        "third_level",
        (rows, rows),
        [vmem],
        (vmem,) * 2,
        [pltpu.VMEM((span * slots, dh), F32)],
        cost=large,
    )(*near_memory(received))
    got = lax.ppermute(theirs, "ctx", mates)
    return call(
        functools.partial(final_kernel, heads),
        "join",
        (pltpu.HBM((length, width), BF16),) * 3,
        [hbm] + [vmem] * 12 + [hbm] * 4,
        (hbm,) * 3,
        [
            pltpu.SMEM(offsets.shape, jnp.int32),
            whole,
            whole,
            pltpu.VMEM((32, length), F32),
            pltpu.VMEM((64, dh), F32),
            pltpu.VMEM((heads, 16, dh), BF16),
            whole,
            whole,
            pltpu.SemaphoreType.DMA,
            pltpu.SemaphoreType.DMA((2,)),
            pltpu.SemaphoreType.DMA,
            pltpu.SemaphoreType.DMA((heads,)),
            pltpu.SemaphoreType.DMA((2, heads // 2)),
        ],
        input_output_aliases={16: 0},
    )(
        *far_memory(offsets),
        *near_memory(mine, got, own, far, spot, weight, s_rows, dp_rows),
        *near_memory(dk, dv, blocks, returned),
        *far_memory(key, key_far, far_scores, dq),
    )


def solution(mesh):
    placed = (P("ctx", None), P("ctx", None), P("ctx", None), P("ctx", None), P())
    return jax.shard_map(
        on_device,
        mesh=mesh,
        in_specs=placed,
        out_specs=(P("ctx", None), P("ctx", None), P("ctx", None)),
        check_vma=False,
    )
```

```python
import functools

import jax
import jax.numpy as jnp
from jax import lax
from jax.experimental import pallas as pl
from jax.experimental.pallas import tpu as pltpu
from jax.sharding import PartitionSpec as P

NEG = -1e30
F32 = jnp.float32
BF16 = jnp.bfloat16
STAT_ROWS = 4
VMEM_LIMIT = 16 * 1024 * 1024
LOG2E = 1.4426950408889634


def iota(shape, dim):
    return lax.broadcasted_iota(jnp.int32, shape, dim)


def dot_nt(a, b):
    return lax.dot_general(a, b, (((1,), (1,)), ((), ())), preferred_element_type=F32)


def dot_tn(a, b):
    return lax.dot_general(a, b, (((0,), (0,)), ((), ())), preferred_element_type=F32)


def dot_nn(a, b):
    return lax.dot_general(a, b, (((1,), (0,)), ((), ())), preferred_element_type=F32)


def block_rows(rows, heads):
    row = iota(rows.shape, 0)
    return jnp.concatenate(
        [jnp.where(row == h, rows, 0.0).astype(BF16) for h in range(heads)], axis=1
    )


def own_columns(wide_rows, heads):
    dh = wide_rows.shape[1] // heads
    row = iota((16, dh), 0)
    return sum(
        jnp.where(row == h, wide_rows[:, h * dh : (h + 1) * dh], 0.0) for h in range(heads)
    )


def offset_column(off_ref, level, heads, rows):
    row = jnp.bitwise_and(iota((rows, 1), 0), 15)
    column = jnp.zeros((rows, 1), jnp.int32)
    for h in range(heads):
        column = jnp.where(row == h, off_ref[level, h], column)
    return column


def level_one_keys(off_ref, heads, rows, length):
    pair = offset_column(off_ref, 0, heads, rows)
    wide = offset_column(off_ref, 1, heads, rows)
    lane = iota((rows, length), 1)
    chosen = jnp.bitwise_and(wide, 1) == pair
    return jnp.logical_and(jnp.bitwise_and(lane, 1) == pair, chosen)


def row_weights(off_ref, heads, length):
    both = level_one_keys(off_ref, heads, 32, length).astype(F32)
    return jnp.where(iota((32, length), 0) < 16, 1.0 + both, both)


def pack_kernel(
    heads, off_ref, k_ref, v_ref, q_ref, g_ref, out_ref, spot_ref, weight_ref, buf, acc, sems
):
    length, dh = k_ref.shape[0], out_ref.shape[1]
    copies = []
    for s, ref in enumerate((k_ref, v_ref, q_ref, g_ref)):
        for h in range(heads):
            base = pl.multiple_of(jnp.bitwise_and(off_ref[1, h], ~15), 16)
            slot = s * heads + h
            copy = pltpu.make_async_copy(
                ref.at[pl.ds(base, 16), pl.ds(h * dh, dh)], buf.at[slot], sems.at[slot]
            )
            copy.start()
            copies.append(copy)
    wide = offset_column(off_ref, 1, heads, 32)
    spot_ref[...] = (iota((32, length), 1) == wide).astype(F32)
    weight_ref[...] = row_weights(off_ref, heads, length)
    acc[...] = jnp.zeros_like(acc)
    row = iota((16, dh), 0)
    for s in range(4):
        for h in range(heads):
            slot = s * heads + h
            copies[slot].wait()
            own = row == jnp.bitwise_and(off_ref[1, h], 15)
            block = jnp.where(own, buf[slot].astype(F32), 0.0)
            acc[slot : slot + 1, :] = jnp.sum(block, axis=0, keepdims=True)
    out_ref[...] = acc[...].astype(BF16)


def stats_kernel(
    heads, span, own_ref, spot_ref, weight_ref, qf_ref, gf_ref, k_ref, v_ref,
    load_ref, s_hbm, dp_hbm, far_hbm, s_ref, dp_ref, far_ref, acc, load, sems, row_sems,
):
    dh = own_ref.shape[1]
    part, slots = heads // 2, load_ref.shape[0] // span
    own = own_ref[...].astype(F32)
    spot = spot_ref[0:16, :].astype(BF16)

    def both_rows(array, whole, first):
        far = own_columns(dot_nn(spot, whole), heads)
        far_ref[first : first + 16, :] = far.astype(BF16)
        near = own[array * heads : array * heads + 16, :]
        return jnp.concatenate([block_rows(near, heads), block_rows(far, heads)], axis=0)

    queries, grads = both_rows(2, qf_ref[...], 0), both_rows(3, gf_ref[...], 16)
    s = dot_nt(queries, k_ref[...]) * (dh**-0.5 * LOG2E)
    dp = dot_nt(grads, v_ref[...])
    s_ref[...] = s
    dp_ref[...] = dp
    for i in range(4):
        for c in range(2):
            slot, row = c * slots + i * part, i * heads + c * part
            acc[slot : slot + part, :] = own[row : row + part, :]
    weight = weight_ref[...]
    masked = jnp.where(weight > 0.0, s, NEG)
    m = jnp.max(masked, axis=1, keepdims=True)
    e = jnp.exp2(masked - m) * weight
    t = jnp.sum(e, axis=1, keepdims=True)
    d = jnp.sum(e * dp, axis=1, keepdims=True)
    lane = iota((32, 128), 1)
    table = jnp.where(lane == 0, m, jnp.where(lane == 1, t, jnp.where(lane == 2, d, 0.0)))
    table = jnp.concatenate([table, jnp.zeros((96, 128), F32)], axis=0).T[0:STAT_ROWS, :]
    high = table.astype(BF16).astype(F32)
    rest = table - high
    middle = rest.astype(BF16).astype(F32)
    low = (rest - middle).astype(BF16).astype(F32)
    table = high + pltpu.roll(middle, 32, 1) + pltpu.roll(low, 64, 1)
    for c in range(2):
        acc[c * slots + 4 * part : (c + 1) * slots, :] = table
    halves = acc[...].astype(BF16)
    stride = load.shape[0]
    for i in range(stride // (2 * slots)):
        load[2 * i * slots : 2 * (i + 1) * slots, :] = halves
    copies = [
        pltpu.make_async_copy(load, load_ref.at[pl.ds(i * stride, stride), :], sems.at[i])
        for i in range(span * slots // stride)
    ]
    for i, (near, away) in enumerate(((s_ref, s_hbm), (dp_ref, dp_hbm), (far_ref, far_hbm))):
        copies.append(pltpu.make_async_copy(near, away, row_sems.at[i]))
    for copy in copies:
        copy.start()
    for copy in copies:
        copy.wait()


def near_head(off_ref, h, inputs, outputs, waits, send):
    q_ref, k_ref, v_ref, g_ref, kf_ref, vf_ref = inputs
    dq_ref, dk_ref, dv_ref, ret_ref = outputs
    length, dh = q_ref.shape[0], q_ref.shape[1] // off_ref.shape[1]
    half = length // 2
    scale = dh**-0.5
    cols = slice(h * dh, (h + 1) * dh)
    q, k, v, g = q_ref[:, cols], k_ref[:, cols], v_ref[:, cols], g_ref[:, cols]
    if h == 0:
        s1, dp1 = dot_nt(k, q), dot_nt(v, g)
        waits[0].wait()
    pair, wide = off_ref[0, h], off_ref[1, h]
    pick = (iota((half, length), 1) == 2 * iota((half, length), 0) + pair).astype(BF16)
    kc = dot_nn(pick, kf_ref[:, cols]).astype(BF16)
    yield
    lanes = iota((1, length), 1)
    chosen = jnp.bitwise_and(lanes, 1) == pair
    a_t = chosen.astype(F32)
    a_u = (jnp.bitwise_and(iota((length, 1), 0), 1) == pair).astype(F32)
    if h > 0:
        s1 = dot_nt(k, q)
    s2 = dot_nt(kc, q) + jnp.where(chosen, 0.0, NEG)
    if h == 0:
        waits[1].wait()
    vc = dot_nn(pick, vf_ref[:, cols]).astype(BF16)
    yield
    m = jnp.maximum(jnp.max(s1, axis=0, keepdims=True), jnp.max(s2, axis=0, keepdims=True))
    m = m * (scale * LOG2E)
    if h > 0:
        dp1 = dot_nt(v, g)
    dp2 = dot_nt(vc, g)
    yield
    e1 = jnp.exp2(s1 * (scale * LOG2E) - m) * (1.0 + a_t * a_u)
    e2 = jnp.exp2(s2 * (scale * LOG2E) - m)
    total = jnp.sum(e1, axis=0, keepdims=True) + jnp.sum(e2, axis=0, keepdims=True)
    part = jnp.sum(e1 * dp1, axis=0, keepdims=True) + jnp.sum(e2 * dp2, axis=0, keepdims=True)
    yield
    inverse = jnp.where(lanes == wide, 0.0, 1.0 / total)
    delta = part * inverse
    p1 = e1 * inverse
    p2 = e2 * inverse
    ds1 = (scale * p1 * (dp1 - delta)).astype(BF16)
    ds2 = (scale * p2 * (dp2 - delta)).astype(BF16)
    p1 = p1.astype(BF16)
    p2 = p2.astype(BF16)
    yield
    dk_ref[:, cols] = dot_nn(ds1, q)
    dv_ref[:, cols] = dot_nn(p1, g)
    ret_ref[:half, cols] = dot_nn(ds2, q).astype(BF16)
    ret_ref[half:, cols] = dot_nn(p2, g).astype(BF16)
    dq_ref[:, cols] = (dot_tn(k, ds1) + dot_tn(kc, ds2)).T.astype(BF16)
    send(h)
    yield


def main_kernel(
    heads, off_hbm, after_ref, vf_hbm, own_ref, q_ref, k_ref, v_ref, g_ref, kf_ref,
    dq_hbm, dk_hbm, dv_hbm, ret_hbm, far_hbm, blocks_hbm,
    off_ref, vf_ref, dq_ref, dk_ref, dv_ref, ret_ref, far_scores, blocks,
    off_sem, in_sem, far_sem, block_sem, out_sems,
):
    offsets = pltpu.make_async_copy(off_hbm, off_ref, off_sem)
    offsets.start()
    values = pltpu.make_async_copy(vf_hbm, vf_ref, in_sem)
    values.start()
    dh = q_ref.shape[1] // heads
    near = (dq_ref, dk_ref, dv_ref, ret_ref)
    writes = []

    def send(h):
        base = pl.multiple_of(jnp.bitwise_and(off_ref[1, h], ~15), 16)
        blocks[h] = dq_ref[pl.ds(base, 16), h * dh : (h + 1) * dh]
        if h == heads - 1:
            copy = pltpu.make_async_copy(blocks, blocks_hbm, block_sem)
            copy.start()
            writes.append(copy)
        if h % 2 == 1:
            cols = slice((h - 1) * dh, (h + 1) * dh)
            for i, (a, b) in enumerate(zip(near, (dq_hbm, dk_hbm, dv_hbm, ret_hbm))):
                sem = out_sems.at[h // 2, i]
                copy = pltpu.make_async_copy(a.at[:, cols], b.at[:, cols], sem)
                copy.start()
                writes.append(copy)

    inputs = (q_ref, k_ref, v_ref, g_ref, kf_ref, vf_ref)
    work = [near_head(off_ref, h, inputs, near, (offsets, values), send) for h in range(heads)]
    steps, lag = 6, 2
    for turn in range(steps + lag * (heads - 1)):
        for h in reversed(range(heads)):
            if 0 <= turn - lag * h < steps:
                next(work[h])
        if turn == steps:
            own = own_ref[...].astype(F32)
            queries = block_rows(own[2 * heads : 2 * heads + 16, :], heads)
            grads = block_rows(own[3 * heads : 3 * heads + 16, :], heads)
            far_scores[:16, :] = dot_nt(queries, kf_ref[...]) * (dh**-0.5 * LOG2E)
            far_scores[16:, :] = dot_nt(grads, vf_ref[...])
            copy = pltpu.make_async_copy(far_scores, far_hbm, far_sem)
            copy.start()
            writes.append(copy)
    for copy in writes:
        copy.wait()


def wide_kernel(
    heads, span, recv_ref, mine_ref, theirs_ref, flat
):
    part, slots, dh = heads // 2, recv_ref.shape[0] // span, recv_ref.shape[1]
    scale = dh**-0.5
    me = lax.rem(lax.axis_index("ctx"), span)
    mate = jnp.bitwise_xor(me, 1)
    first = jnp.bitwise_and(me, 1) == 0
    flat[...] = recv_ref[...].astype(F32)

    def gathered(slot):
        return flat[pl.ds(slot, span, stride=slots), :]

    even = jnp.bitwise_and(iota((8, 128), 1), 1) == 0

    def stat(index):
        x = gathered(4 * part + index)
        x = x + pltpu.roll(x, 96, 1) + pltpu.roll(x, 64, 1)
        if span < 128:
            x = jnp.concatenate([x, jnp.zeros((128 - span, 128), F32)], axis=0)
        x = x.T
        near = jnp.where(first, x[0:8, :], x[part : part + 8, :])
        other = jnp.where(first, x[16:24, :], x[16 + part : 24 + part, :])
        other = jnp.where(even, pltpu.roll(other, 127, 1), pltpu.roll(other, 1, 1))
        return near[:, :span], other[:, :span]

    (m_a, m_b), (t_a, t_b), (d_a, d_b) = stat(0), stat(1), stat(2)
    row = iota((16, span), 0)
    device = iota((span, 1), 0)
    k_w, v_w, q_w, g_w = [
        [gathered(i * part + j).astype(BF16) for j in range(part)] for i in range(4)
    ]
    m_c, t_c, d_c = [jnp.zeros((8, span), F32) for _ in range(3)]
    s_key, dp_key, s_row, dp_row = [jnp.zeros((16, span), F32) for _ in range(4)]

    def two_rows(x, j, table):
        for index, device_of in enumerate((me, mate)):
            one = jnp.sum(jnp.where(device == device_of, x, 0.0), axis=0, keepdims=True)
            table = jnp.where(row == 8 * index + j, one, table)
        return table

    for j in range(part):
        s = dot_nt(k_w[j], q_w[j]) * (scale * LOG2E)
        dp = dot_nt(v_w[j], g_w[j])
        m = jnp.max(s, axis=0, keepdims=True)
        e = jnp.exp2(s - m)
        here = row[:8] == j
        m_c = jnp.where(here, m, m_c)
        t_c = jnp.where(here, jnp.sum(e, axis=0, keepdims=True), t_c)
        d_c = jnp.where(here, jnp.sum(e * dp, axis=0, keepdims=True), d_c)
        s_key = two_rows(s, j, s_key)
        dp_key = two_rows(dp, j, dp_key)
        s_row = two_rows(dot_nt(q_w[j], k_w[j]) * (scale * LOG2E), j, s_row)
        dp_row = two_rows(dot_nt(g_w[j], v_w[j]), j, dp_row)
    m_all = jnp.maximum(jnp.maximum(m_a, m_b), m_c)
    w_a, w_b, w_c = jnp.exp2(m_a - m_all), jnp.exp2(m_b - m_all), jnp.exp2(m_c - m_all)
    inverse = 1.0 / (t_a * w_a + t_b * w_b + t_c * w_c)
    delta = (d_a * w_a + d_b * w_b + d_c * w_c) * inverse

    def twice(x):
        return jnp.concatenate([x, x], axis=0)

    def column(x, index):
        return jnp.sum(jnp.where(iota((8, span), 1) == index, x, 0.0), axis=1, keepdims=True)

    p_key = jnp.exp2(s_key - twice(m_all)) * twice(inverse)
    ds_key = scale * p_key * (dp_key - twice(delta))
    of_me = [column(x, me) for x in (m_all, inverse, delta)]
    of_mate = [column(x, mate) for x in (m_all, inverse, delta)]
    m_r, i_r, d_r = [jnp.concatenate(pair, axis=0) for pair in zip(of_me, of_mate)]
    ds_row = scale * (jnp.exp2(s_row - m_r) * i_r) * (dp_row - d_r)

    def times(left, right):
        index = jnp.bitwise_and(row, 7)
        return sum(
            dot_nn(jnp.where(index == j, left, 0.0).astype(BF16), right[j]) for j in range(part)
        )

    terms = (times(ds_row, k_w), times(ds_key, q_w), times(p_key, g_w))
    lane = iota((8, dh), 1)
    for ref, base, columns in ((mine_ref, 0, of_me + of_mate), (theirs_ref, 8, of_mate + of_me)):
        for i, term in enumerate(terms):
            ref[8 * i : 8 * i + 8, :] = term[base : base + 8, :]
        table = jnp.zeros((8, dh), F32)
        for i, value in enumerate(columns):
            table = jnp.where(lane == i, value, table)
        ref[24:32, :] = table


def final_kernel(
    heads, off_hbm, mine_ref, got_ref, own_ref, far_ref, spot_ref, weight_ref, s_ref, dp_ref,
    dki, dvi, blocks_in, ret, k_hbm, kf_hbm, far_hbm, dq_in, dq_ref, dk_ref, dv_ref,
    off_ref, k_ref, kf_ref, far_scores, full, blocks, dko, dvo, off_sem, key_sems, far_sem, block_sems, write_sems,
):
    offsets = pltpu.make_async_copy(off_hbm, off_ref, off_sem)
    offsets.start()
    scores = pltpu.make_async_copy(far_hbm, far_scores, far_sem)
    scores.start()
    keys = [
        pltpu.make_async_copy(k_hbm, k_ref, key_sems.at[0]),
        pltpu.make_async_copy(kf_hbm, kf_ref, key_sems.at[1]),
    ]
    for copy in keys:
        copy.start()
    length, dh = k_hbm.shape[0], own_ref.shape[1]
    half, part = length // 2, heads // 2
    scale = dh**-0.5

    def place(ref, h):
        base = pl.multiple_of(jnp.bitwise_and(off_ref[1, h], ~15), 16)
        return ref.at[pl.ds(base, 16), pl.ds(h * dh, dh)]

    chunks = [slice(2 * j * dh, 2 * (j + 1) * dh) for j in range(part)]
    own, far = own_ref[...].astype(F32), far_ref[...].astype(F32)
    first = jnp.bitwise_and(lax.axis_index("ctx"), 1) == 0
    mine, got = mine_ref[...], got_ref[...]
    low, high = jnp.where(first, mine, got), jnp.where(first, got, mine)
    full[...] = jnp.zeros_like(full)
    for i in range(4):
        full[16 * i : 16 * i + part, :] = low[8 * i : 8 * i + part, :]
        full[16 * i + part : 16 * i + heads, :] = high[8 * i : 8 * i + part, :]
    dq_wide, dk_rows, dv_rows, table = [full[16 * i : 16 * i + 16, :] for i in range(4)]
    m_me, i_me, d_me = [table[:, i : i + 1] for i in range(3)]
    m_two, i_two, d_two = [
        jnp.concatenate([table[:, i : i + 1], table[:, i + 3 : i + 4]], axis=0) for i in range(3)
    ]
    weight = weight_ref[...]
    p_two = jnp.exp2(jnp.where(weight > 0.0, s_ref[...] - m_two, NEG)) * weight * i_two
    ds_two = scale * p_two * (dp_ref[...] - d_two)
    met = weight[0:16, :] > 1.0
    scores.wait()
    p_far = jnp.exp2(jnp.where(met, far_scores[:16, :] - m_me, NEG)) * i_me
    ds_far = scale * p_far * (far_scores[16:, :] - d_me)
    spot = spot_ref[...]
    offsets.wait()
    writes = []

    def spread(left, array, rows):
        near = own[(array + 2) * heads : (array + 2) * heads + 16, :]
        high = rows.astype(BF16).astype(F32)
        left = jnp.concatenate([left, spot], axis=0).T.astype(BF16)
        parts = (near, far[16 * array : 16 * array + 16, :], high, rows - high)
        return left, jnp.concatenate([block_rows(part, heads) for part in parts], axis=0)

    for index, (base, out, out_ref, left, right) in enumerate(
        (
            (dki, dko, dk_ref) + spread(ds_two, 0, dk_rows),
            (dvi, dvo, dv_ref) + spread(p_two, 1, dv_rows),
        )
    ):
        back = slice(index * half, (index + 1) * half)
        for j, chunk in enumerate(chunks):
            for h in (2 * j, 2 * j + 1):
                cols = slice(h * dh, (h + 1) * dh)
                pick = iota((length, half), 0) == 2 * iota((length, half), 1) + off_ref[0, h]
                added = dot_nn(left, right[:, cols]) + dot_nn(pick.astype(BF16), ret[back, cols])
                out[:, cols] = (base[:, cols] + added).astype(BF16)
            sem = write_sems.at[index, j]
            copy = pltpu.make_async_copy(out.at[:, chunk], out_ref.at[:, chunk], sem)
            copy.start()
            writes.append(copy)
    for copy in keys:
        copy.wait()
    dq_rows = dq_wide + own_columns(
        dot_nn(ds_two[0:16, :].astype(BF16), k_ref[...]) + dot_nn(ds_far.astype(BF16), kf_ref[...]),
        heads,
    )
    for h in range(heads):
        here = iota((16, dh), 0) == jnp.bitwise_and(off_ref[1, h], 15)
        block = jnp.where(here, dq_rows[h : h + 1, :], blocks_in[h].astype(F32))
        blocks[h] = block.astype(BF16)
        copy = pltpu.make_async_copy(blocks.at[h], place(dq_ref, h), block_sems.at[h])
        copy.start()
        writes.append(copy)
    for copy in writes:
        copy.wait()


def on_device(query, key, value, grad_out, offsets):
    length, width = query.shape
    heads = offsets.shape[1]
    dh = width // heads
    size = lax.axis_size("ctx")
    span = min(size, 128)
    slots = 2 * heads + STAT_ROWS
    mates = [(i, i ^ 1) for i in range(size)]
    vmem = pl.BlockSpec(memory_space=pltpu.VMEM)
    smem = pl.BlockSpec(memory_space=pltpu.SMEM)
    hbm = pl.BlockSpec(memory_space=pltpu.HBM)
    params = pltpu.CompilerParams(vmem_limit_bytes=VMEM_LIMIT)
    small = pl.CostEstimate(flops=1000, bytes_accessed=1000, transcendentals=0)
    large = pl.CostEstimate(flops=7 * 10**9, bytes_accessed=1000, transcendentals=0)

    def call(kernel, name, out_shape, in_specs, out_specs, scratch, cost=small, **kwargs):
        return pl.pallas_call(
            kernel,
            out_shape=out_shape,
            in_specs=in_specs,
            out_specs=out_specs,
            scratch_shapes=scratch,
            compiler_params=params,
            cost_estimate=cost,
            name=name,
            **kwargs,
        )

    def far_memory(*arrays):
        return [pltpu.with_memory_space_constraint(array, pltpu.HBM) for array in arrays]

    def near_memory(*arrays):
        return [pltpu.with_memory_space_constraint(array, pltpu.VMEM) for array in arrays]

    query_far = lax.ppermute(query, "ctx", mates)
    grad_far = lax.ppermute(grad_out, "ctx", mates)
    table = pltpu.VMEM((32, length), F32)
    own, spot, weight = call(
        functools.partial(pack_kernel, heads),
        "pack_rows",
        (pltpu.VMEM((48, dh), BF16), table, table),
        [smem] + [hbm] * 4,
        (vmem,) * 3,
        [
            pltpu.VMEM((4 * heads, 16, dh), BF16),
            pltpu.VMEM((48, dh), F32),
            pltpu.SemaphoreType.DMA((4 * heads,)),
        ],
        cost=large,
    )(*far_memory(offsets, key, value, query, grad_out))
    key_later, value_later, own = lax.optimization_barrier((key, value, own))
    key_far = lax.ppermute(key_later, "ctx", mates)
    value_far = lax.ppermute(value_later, "ctx", mates)
    repeat = min(span, 8)
    load, s_rows, dp_rows, far = call(
        functools.partial(stats_kernel, heads, span),
        "row_stats",
        (
            pltpu.HBM((span * slots, dh), BF16),
            pltpu.HBM((32, length), F32),
            pltpu.HBM((32, length), F32),
            pltpu.HBM((32, dh), BF16),
        ),
        [vmem] * 7,
        (hbm,) * 4,
        [
            table,
            table,
            pltpu.VMEM((32, dh), BF16),
            pltpu.VMEM((2 * slots, dh), F32),
            pltpu.VMEM((repeat * slots, dh), BF16),
            pltpu.SemaphoreType.DMA((span // repeat,)),
            pltpu.SemaphoreType.DMA((3,)),
        ],
    )(*near_memory(own, spot, weight, query_far, grad_far, key, value))
    groups = None
    if size > span:
        groups = [list(range(base, base + span)) for base in range(0, size, span)]
    received = lax.all_to_all(load, "ctx", 0, 0, axis_index_groups=groups, tiled=True)
    whole = pltpu.VMEM((length, width), BF16)
    wide = pltpu.VMEM((length, width), F32)
    rows = pltpu.VMEM((32, dh), F32)
    dq, dk, dv, partial, far_scores, blocks = call(
        functools.partial(main_kernel, heads),
        "near_levels",
        (
            pltpu.HBM((length, width), BF16),
            pltpu.HBM((length, width), F32),
            pltpu.HBM((length, width), F32),
            pltpu.HBM((length, width), BF16),
            pltpu.HBM((32, length), F32),
            pltpu.HBM((heads, 16, dh), BF16),
        ),
        [hbm] * 3 + [vmem] * 6,
        (hbm,) * 6,
        [
            pltpu.SMEM(offsets.shape, jnp.int32),
            whole,
            whole,
            wide,
            wide,
            whole,
            pltpu.VMEM((32, length), F32),
            pltpu.VMEM((heads, 16, dh), BF16),
            pltpu.SemaphoreType.DMA,
            pltpu.SemaphoreType.DMA,
            pltpu.SemaphoreType.DMA,
            pltpu.SemaphoreType.DMA,
            pltpu.SemaphoreType.DMA((heads // 2, 4)),
        ],
        cost=large,
    )(
        *far_memory(offsets, s_rows, value_far),
        *near_memory(own, query, key, value, grad_out, key_far),
    )
    returned = lax.ppermute(partial, "ctx", mates)
    mine, theirs = call(
        functools.partial(wide_kernel, heads, span),
        "third_level",
        (rows, rows),
        [vmem],
        (vmem,) * 2,
        [pltpu.VMEM((span * slots, dh), F32)],
        cost=large,
    )(*near_memory(received))
    got = lax.ppermute(theirs, "ctx", mates)
    return call(
        functools.partial(final_kernel, heads),
        "join",
        (pltpu.HBM((length, width), BF16),) * 3,
        [hbm] + [vmem] * 12 + [hbm] * 4,
        (hbm,) * 3,
        [
            pltpu.SMEM(offsets.shape, jnp.int32),
            whole,
            whole,
            pltpu.VMEM((32, length), F32),
            pltpu.VMEM((64, dh), F32),
            pltpu.VMEM((heads, 16, dh), BF16),
            whole,
            whole,
            pltpu.SemaphoreType.DMA,
            pltpu.SemaphoreType.DMA((2,)),
            pltpu.SemaphoreType.DMA,
            pltpu.SemaphoreType.DMA((heads,)),
            pltpu.SemaphoreType.DMA((2, heads // 2)),
        ],
        input_output_aliases={16: 0},
    )(
        *far_memory(offsets),
        *near_memory(mine, got, own, far, spot, weight, s_rows, dp_rows),
        *near_memory(dk, dv, blocks, returned),
        *far_memory(key, key_far, far_scores, dq),
    )


def solution(mesh):
    placed = (P("ctx", None), P("ctx", None), P("ctx", None), P("ctx", None), P())
    return jax.shard_map(
        on_device,
        mesh=mesh,
        in_specs=placed,
        out_specs=(P("ctx", None), P("ctx", None), P("ctx", None)),
        check_vma=False,
    )
```

```python
import functools

import jax
import jax.numpy as jnp
from jax import lax
from jax.experimental import pallas as pl
from jax.experimental.pallas import tpu as pltpu
from jax.sharding import PartitionSpec as P

NEG = -1e30
F32 = jnp.float32
BF16 = jnp.bfloat16
STAT_ROWS = 4
VMEM_LIMIT = 16 * 1024 * 1024
LOG2E = 1.4426950408889634


def iota(shape, dim):
    return lax.broadcasted_iota(jnp.int32, shape, dim)


def dot_nt(a, b):
    return lax.dot_general(a, b, (((1,), (1,)), ((), ())), preferred_element_type=F32)


def dot_tn(a, b):
    return lax.dot_general(a, b, (((0,), (0,)), ((), ())), preferred_element_type=F32)


def dot_nn(a, b):
    return lax.dot_general(a, b, (((1,), (0,)), ((), ())), preferred_element_type=F32)


def block_rows(rows, heads):
    row = iota(rows.shape, 0)
    return jnp.concatenate(
        [jnp.where(row == h, rows, 0.0).astype(BF16) for h in range(heads)], axis=1
    )


def own_columns(wide_rows, heads):
    dh = wide_rows.shape[1] // heads
    row = iota((16, dh), 0)
    return sum(
        jnp.where(row == h, wide_rows[:, h * dh : (h + 1) * dh], 0.0) for h in range(heads)
    )


def offset_column(off_ref, level, heads, rows):
    row = jnp.bitwise_and(iota((rows, 1), 0), 15)
    column = jnp.zeros((rows, 1), jnp.int32)
    for h in range(heads):
        column = jnp.where(row == h, off_ref[level, h], column)
    return column


def level_one_keys(off_ref, heads, rows, length):
    pair = offset_column(off_ref, 0, heads, rows)
    wide = offset_column(off_ref, 1, heads, rows)
    lane = iota((rows, length), 1)
    chosen = jnp.bitwise_and(wide, 1) == pair
    return jnp.logical_and(jnp.bitwise_and(lane, 1) == pair, chosen)


def row_weights(off_ref, heads, length):
    both = level_one_keys(off_ref, heads, 32, length).astype(F32)
    return jnp.where(iota((32, length), 0) < 16, 1.0 + both, both)


def pack_kernel(
    heads, off_ref, k_ref, v_ref, q_ref, g_ref, out_ref, spot_ref, weight_ref, buf, acc, sems
):
    length, dh = k_ref.shape[0], out_ref.shape[1]
    copies = []
    for s, ref in enumerate((k_ref, v_ref, q_ref, g_ref)):
        for h in range(heads):
            base = pl.multiple_of(jnp.bitwise_and(off_ref[1, h], ~15), 16)
            slot = s * heads + h
            copy = pltpu.make_async_copy(
                ref.at[pl.ds(base, 16), pl.ds(h * dh, dh)], buf.at[slot], sems.at[slot]
            )
            copy.start()
            copies.append(copy)
    wide = offset_column(off_ref, 1, heads, 32)
    spot_ref[...] = (iota((32, length), 1) == wide).astype(F32)
    weight_ref[...] = row_weights(off_ref, heads, length)
    acc[...] = jnp.zeros_like(acc)
    row = iota((16, dh), 0)
    for s in range(4):
        for h in range(heads):
            slot = s * heads + h
            copies[slot].wait()
            own = row == jnp.bitwise_and(off_ref[1, h], 15)
            block = jnp.where(own, buf[slot].astype(F32), 0.0)
            acc[slot : slot + 1, :] = jnp.sum(block, axis=0, keepdims=True)
    out_ref[...] = acc[...].astype(BF16)


def stats_kernel(
    heads, span, own_ref, spot_ref, weight_ref, qf_ref, gf_ref, k_ref, v_ref,
    load_ref, s_hbm, dp_hbm, far_hbm, s_ref, dp_ref, far_ref, acc, load, sems, row_sems,
):
    dh = own_ref.shape[1]
    part, slots = heads // 2, load_ref.shape[0] // span
    own = own_ref[...].astype(F32)
    spot = spot_ref[0:16, :].astype(BF16)

    def both_rows(array, whole, first):
        far = own_columns(dot_nn(spot, whole), heads)
        far_ref[first : first + 16, :] = far.astype(BF16)
        near = own[array * heads : array * heads + 16, :]
        return jnp.concatenate([block_rows(near, heads), block_rows(far, heads)], axis=0)

    queries, grads = both_rows(2, qf_ref[...], 0), both_rows(3, gf_ref[...], 16)
    s = dot_nt(queries, k_ref[...]) * (dh**-0.5 * LOG2E)
    dp = dot_nt(grads, v_ref[...])
    s_ref[...] = s
    dp_ref[...] = dp
    for i in range(4):
        for c in range(2):
            slot, row = c * slots + i * part, i * heads + c * part
            acc[slot : slot + part, :] = own[row : row + part, :]
    weight = weight_ref[...]
    masked = jnp.where(weight > 0.0, s, NEG)
    m = jnp.max(masked, axis=1, keepdims=True)
    e = jnp.exp2(masked - m) * weight
    t = jnp.sum(e, axis=1, keepdims=True)
    d = jnp.sum(e * dp, axis=1, keepdims=True)
    lane = iota((32, 128), 1)
    table = jnp.where(lane == 0, m, jnp.where(lane == 1, t, jnp.where(lane == 2, d, 0.0)))
    table = jnp.concatenate([table, jnp.zeros((96, 128), F32)], axis=0).T[0:STAT_ROWS, :]
    high = table.astype(BF16).astype(F32)
    rest = table - high
    middle = rest.astype(BF16).astype(F32)
    low = (rest - middle).astype(BF16).astype(F32)
    table = high + pltpu.roll(middle, 32, 1) + pltpu.roll(low, 64, 1)
    for c in range(2):
        acc[c * slots + 4 * part : (c + 1) * slots, :] = table
    halves = acc[...].astype(BF16)
    stride = load.shape[0]
    for i in range(stride // (2 * slots)):
        load[2 * i * slots : 2 * (i + 1) * slots, :] = halves
    copies = [
        pltpu.make_async_copy(load, load_ref.at[pl.ds(i * stride, stride), :], sems.at[i])
        for i in range(span * slots // stride)
    ]
    for i, (near, away) in enumerate(((s_ref, s_hbm), (dp_ref, dp_hbm), (far_ref, far_hbm))):
        copies.append(pltpu.make_async_copy(near, away, row_sems.at[i]))
    for copy in copies:
        copy.start()
    for copy in copies:
        copy.wait()


def near_head(off_ref, h, inputs, outputs, waits, send):
    q_ref, k_ref, v_ref, g_ref, kf_ref, vf_ref = inputs
    dq_ref, dk_ref, dv_ref, ret_ref = outputs
    length, dh = q_ref.shape[0], q_ref.shape[1] // off_ref.shape[1]
    half = length // 2
    scale = dh**-0.5
    cols = slice(h * dh, (h + 1) * dh)
    q, k, v, g = q_ref[:, cols], k_ref[:, cols], v_ref[:, cols], g_ref[:, cols]
    if h == 0:
        s1, dp1 = dot_nt(k, q), dot_nt(v, g)
        waits[0].wait()
    pair, wide = off_ref[0, h], off_ref[1, h]
    pick = (iota((half, length), 1) == 2 * iota((half, length), 0) + pair).astype(BF16)
    kc = dot_nn(pick, kf_ref[:, cols]).astype(BF16)
    yield
    lanes = iota((1, length), 1)
    chosen = jnp.bitwise_and(lanes, 1) == pair
    a_t = chosen.astype(F32)
    a_u = (jnp.bitwise_and(iota((length, 1), 0), 1) == pair).astype(F32)
    if h > 0:
        s1 = dot_nt(k, q)
    s2 = dot_nt(kc, q) + jnp.where(chosen, 0.0, NEG)
    if h == 0:
        waits[1].wait()
    vc = dot_nn(pick, vf_ref[:, cols]).astype(BF16)
    yield
    m = jnp.maximum(jnp.max(s1, axis=0, keepdims=True), jnp.max(s2, axis=0, keepdims=True))
    m = m * (scale * LOG2E)
    if h > 0:
        dp1 = dot_nt(v, g)
    dp2 = dot_nt(vc, g)
    yield
    e1 = jnp.exp2(s1 * (scale * LOG2E) - m) * (1.0 + a_t * a_u)
    e2 = jnp.exp2(s2 * (scale * LOG2E) - m)
    total = jnp.sum(e1, axis=0, keepdims=True) + jnp.sum(e2, axis=0, keepdims=True)
    part = jnp.sum(e1 * dp1, axis=0, keepdims=True) + jnp.sum(e2 * dp2, axis=0, keepdims=True)
    yield
    inverse = jnp.where(lanes == wide, 0.0, 1.0 / total)
    delta = part * inverse
    p1 = e1 * inverse
    p2 = e2 * inverse
    ds1 = (scale * p1 * (dp1 - delta)).astype(BF16)
    ds2 = (scale * p2 * (dp2 - delta)).astype(BF16)
    p1 = p1.astype(BF16)
    p2 = p2.astype(BF16)
    yield
    dk_ref[:, cols] = dot_nn(ds1, q)
    dv_ref[:, cols] = dot_nn(p1, g)
    ret_ref[:half, cols] = dot_nn(ds2, q).astype(BF16)
    ret_ref[half:, cols] = dot_nn(p2, g).astype(BF16)
    dq_ref[:, cols] = (dot_tn(k, ds1) + dot_tn(kc, ds2)).T.astype(BF16)
    send(h)
    yield


def row_terms(heads, scores, products, weight, keys):
    masked = jnp.where(weight > 0.0, scores, NEG)
    peak = jnp.max(masked, axis=1, keepdims=True)
    e = jnp.exp2(masked - peak) * weight
    parts = []
    for x in (e * products, e):
        high = x.astype(BF16)
        parts += [high, (x - high.astype(F32)).astype(BF16)]
    sums = dot_nn(jnp.concatenate(parts, axis=0), keys)
    first = own_columns(sums[0:16, :] + sums[16:32, :], heads)
    second = own_columns(sums[32:48, :] + sums[48:64, :], heads)
    return first, second, peak


def main_kernel(
    heads, off_hbm, s_hbm, dp_hbm, vf_hbm, own_ref, weight_ref, q_ref, k_ref, v_ref, g_ref, kf_ref,
    dq_hbm, dk_hbm, dv_hbm, ret_hbm, terms_hbm, blocks_hbm,
    off_ref, s_ref, dp_ref, vf_ref, dq_ref, dk_ref, dv_ref, ret_ref, terms, blocks,
    off_sem, in_sem, row_sems, terms_sem, block_sem, out_sems,
):
    offsets = pltpu.make_async_copy(off_hbm, off_ref, off_sem)
    offsets.start()
    values = pltpu.make_async_copy(vf_hbm, vf_ref, in_sem)
    values.start()
    stats = [
        pltpu.make_async_copy(s_hbm, s_ref, row_sems.at[0]),
        pltpu.make_async_copy(dp_hbm, dp_ref, row_sems.at[1]),
    ]
    for copy in stats:
        copy.start()
    dh = q_ref.shape[1] // heads
    near = (dq_ref, dk_ref, dv_ref, ret_ref)
    writes = []

    def send(h):
        base = pl.multiple_of(jnp.bitwise_and(off_ref[1, h], ~15), 16)
        blocks[h] = dq_ref[pl.ds(base, 16), h * dh : (h + 1) * dh]
        if h == heads - 1:
            copy = pltpu.make_async_copy(blocks, blocks_hbm, block_sem)
            copy.start()
            writes.append(copy)
        if h % 2 == 1:
            cols = slice((h - 1) * dh, (h + 1) * dh)
            for i, (a, b) in enumerate(zip(near, (dq_hbm, dk_hbm, dv_hbm, ret_hbm))):
                sem = out_sems.at[h // 2, i]
                copy = pltpu.make_async_copy(a.at[:, cols], b.at[:, cols], sem)
                copy.start()
                writes.append(copy)

    inputs = (q_ref, k_ref, v_ref, g_ref, kf_ref, vf_ref)
    work = [near_head(off_ref, h, inputs, near, (offsets, values), send) for h in range(heads)]
    steps, lag = 6, 2
    for turn in range(steps + lag * (heads - 1)):
        for h in reversed(range(heads)):
            if 0 <= turn - lag * h < steps:
                next(work[h])
        if turn == steps:
            own = own_ref[...].astype(F32)
            queries = block_rows(own[2 * heads : 2 * heads + 16, :], heads)
            grads = block_rows(own[3 * heads : 3 * heads + 16, :], heads)
            far_s = dot_nt(queries, kf_ref[...]) * (dh**-0.5 * LOG2E)
            far_dp = dot_nt(grads, vf_ref[...])
            for copy in stats:
                copy.wait()
            weight = weight_ref[0:16, :]
            met = (weight > 1.0).astype(F32)
            near_row = row_terms(heads, s_ref[0:16, :], dp_ref[0:16, :], weight, k_ref[...])
            far_row = row_terms(heads, far_s, far_dp, met, kf_ref[...])
            lane = iota((16, dh), 1)
            peaks = jnp.where(lane == 0, near_row[2], jnp.where(lane == 1, far_row[2], 0.0))
            for i, term in enumerate(near_row[:2] + far_row[:2] + (peaks,)):
                terms[16 * i : 16 * i + 16, :] = term
            copy = pltpu.make_async_copy(terms, terms_hbm, terms_sem)
            copy.start()
            writes.append(copy)
    for copy in writes:
        copy.wait()


def wide_kernel(
    heads, span, recv_ref, mine_ref, theirs_ref, flat
):
    part, slots, dh = heads // 2, recv_ref.shape[0] // span, recv_ref.shape[1]
    scale = dh**-0.5
    me = lax.rem(lax.axis_index("ctx"), span)
    mate = jnp.bitwise_xor(me, 1)
    first = jnp.bitwise_and(me, 1) == 0
    flat[...] = recv_ref[...].astype(F32)

    def gathered(slot):
        return flat[pl.ds(slot, span, stride=slots), :]

    even = jnp.bitwise_and(iota((8, 128), 1), 1) == 0

    def stat(index):
        x = gathered(4 * part + index)
        x = x + pltpu.roll(x, 96, 1) + pltpu.roll(x, 64, 1)
        if span < 128:
            x = jnp.concatenate([x, jnp.zeros((128 - span, 128), F32)], axis=0)
        x = x.T
        near = jnp.where(first, x[0:8, :], x[part : part + 8, :])
        other = jnp.where(first, x[16:24, :], x[16 + part : 24 + part, :])
        other = jnp.where(even, pltpu.roll(other, 127, 1), pltpu.roll(other, 1, 1))
        return near[:, :span], other[:, :span]

    (m_a, m_b), (t_a, t_b), (d_a, d_b) = stat(0), stat(1), stat(2)
    row = iota((16, span), 0)
    device = iota((span, 1), 0)
    k_w, v_w, q_w, g_w = [
        [gathered(i * part + j).astype(BF16) for j in range(part)] for i in range(4)
    ]
    m_c, t_c, d_c = [jnp.zeros((8, span), F32) for _ in range(3)]
    s_key, dp_key, s_row, dp_row = [jnp.zeros((16, span), F32) for _ in range(4)]

    def two_rows(x, j, table):
        for index, device_of in enumerate((me, mate)):
            one = jnp.sum(jnp.where(device == device_of, x, 0.0), axis=0, keepdims=True)
            table = jnp.where(row == 8 * index + j, one, table)
        return table

    for j in range(part):
        s = dot_nt(k_w[j], q_w[j]) * (scale * LOG2E)
        dp = dot_nt(v_w[j], g_w[j])
        m = jnp.max(s, axis=0, keepdims=True)
        e = jnp.exp2(s - m)
        here = row[:8] == j
        m_c = jnp.where(here, m, m_c)
        t_c = jnp.where(here, jnp.sum(e, axis=0, keepdims=True), t_c)
        d_c = jnp.where(here, jnp.sum(e * dp, axis=0, keepdims=True), d_c)
        s_key = two_rows(s, j, s_key)
        dp_key = two_rows(dp, j, dp_key)
        s_row = two_rows(dot_nt(q_w[j], k_w[j]) * (scale * LOG2E), j, s_row)
        dp_row = two_rows(dot_nt(g_w[j], v_w[j]), j, dp_row)
    m_all = jnp.maximum(jnp.maximum(m_a, m_b), m_c)
    w_a, w_b, w_c = jnp.exp2(m_a - m_all), jnp.exp2(m_b - m_all), jnp.exp2(m_c - m_all)
    inverse = 1.0 / (t_a * w_a + t_b * w_b + t_c * w_c)
    delta = (d_a * w_a + d_b * w_b + d_c * w_c) * inverse

    def twice(x):
        return jnp.concatenate([x, x], axis=0)

    def column(x, index):
        return jnp.sum(jnp.where(iota((8, span), 1) == index, x, 0.0), axis=1, keepdims=True)

    p_key = jnp.exp2(s_key - twice(m_all)) * twice(inverse)
    ds_key = scale * p_key * (dp_key - twice(delta))
    of_me = [column(x, me) for x in (m_all, inverse, delta)]
    of_mate = [column(x, mate) for x in (m_all, inverse, delta)]
    m_r, i_r, d_r = [jnp.concatenate(pair, axis=0) for pair in zip(of_me, of_mate)]
    ds_row = scale * (jnp.exp2(s_row - m_r) * i_r) * (dp_row - d_r)

    def times(left, right):
        index = jnp.bitwise_and(row, 7)
        return sum(
            dot_nn(jnp.where(index == j, left, 0.0).astype(BF16), right[j]) for j in range(part)
        )

    terms = (times(ds_row, k_w), times(ds_key, q_w), times(p_key, g_w))
    lane = iota((8, dh), 1)
    for ref, base, columns in ((mine_ref, 0, of_me + of_mate), (theirs_ref, 8, of_mate + of_me)):
        for i, term in enumerate(terms):
            ref[8 * i : 8 * i + 8, :] = term[base : base + 8, :]
        table = jnp.zeros((8, dh), F32)
        for i, value in enumerate(columns):
            table = jnp.where(lane == i, value, table)
        ref[24:32, :] = table


def final_kernel(
    heads, off_hbm, mine_ref, got_ref, own_ref, far_ref, spot_ref, weight_ref, s_ref, dp_ref,
    terms_ref, dki, dvi, blocks_in, ret, dq_in, dq_ref, dk_ref, dv_ref,
    off_ref, full, blocks, dko, dvo, off_sem, block_sems, write_sems,
):
    offsets = pltpu.make_async_copy(off_hbm, off_ref, off_sem)
    offsets.start()
    length, dh = dki.shape[0], own_ref.shape[1]
    half, part = length // 2, heads // 2
    scale = dh**-0.5

    def place(ref, h):
        base = pl.multiple_of(jnp.bitwise_and(off_ref[1, h], ~15), 16)
        return ref.at[pl.ds(base, 16), pl.ds(h * dh, dh)]

    chunks = [slice(2 * j * dh, 2 * (j + 1) * dh) for j in range(part)]
    own, far = own_ref[...].astype(F32), far_ref[...].astype(F32)
    first = jnp.bitwise_and(lax.axis_index("ctx"), 1) == 0
    mine, got = mine_ref[...], got_ref[...]
    low, high = jnp.where(first, mine, got), jnp.where(first, got, mine)
    full[...] = jnp.zeros_like(full)
    for i in range(4):
        full[16 * i : 16 * i + part, :] = low[8 * i : 8 * i + part, :]
        full[16 * i + part : 16 * i + heads, :] = high[8 * i : 8 * i + part, :]
    dq_wide, dk_rows, dv_rows, table = [full[16 * i : 16 * i + 16, :] for i in range(4)]
    m_me, i_me, d_me = [table[:, i : i + 1] for i in range(3)]
    m_two, i_two, d_two = [
        jnp.concatenate([table[:, i : i + 1], table[:, i + 3 : i + 4]], axis=0) for i in range(3)
    ]
    weight = weight_ref[...]
    p_two = jnp.exp2(jnp.where(weight > 0.0, s_ref[...] - m_two, NEG)) * weight * i_two
    ds_two = scale * p_two * (dp_ref[...] - d_two)
    terms = [terms_ref[16 * i : 16 * i + 16, :] for i in range(5)]
    dq_rows = dq_wide
    for i in range(2):
        share = scale * jnp.exp2(terms[4][:, i : i + 1] - m_me) * i_me
        dq_rows += share * (terms[2 * i] - d_me * terms[2 * i + 1])
    spot = spot_ref[...]
    offsets.wait()
    writes = []

    def spread(left, array, rows):
        near = own[(array + 2) * heads : (array + 2) * heads + 16, :]
        high = rows.astype(BF16).astype(F32)
        left = jnp.concatenate([left, spot], axis=0).T.astype(BF16)
        parts = (near, far[16 * array : 16 * array + 16, :], high, rows - high)
        return left, jnp.concatenate([block_rows(part, heads) for part in parts], axis=0)

    for index, (base, out, out_ref, left, right) in enumerate(
        (
            (dki, dko, dk_ref) + spread(ds_two, 0, dk_rows),
            (dvi, dvo, dv_ref) + spread(p_two, 1, dv_rows),
        )
    ):
        back = slice(index * half, (index + 1) * half)
        for j, chunk in enumerate(chunks):
            for h in (2 * j, 2 * j + 1):
                cols = slice(h * dh, (h + 1) * dh)
                pick = iota((length, half), 0) == 2 * iota((length, half), 1) + off_ref[0, h]
                added = dot_nn(left, right[:, cols]) + dot_nn(pick.astype(BF16), ret[back, cols])
                out[:, cols] = (base[:, cols] + added).astype(BF16)
            sem = write_sems.at[index, j]
            copy = pltpu.make_async_copy(out.at[:, chunk], out_ref.at[:, chunk], sem)
            copy.start()
            writes.append(copy)
    for h in range(heads):
        here = iota((16, dh), 0) == jnp.bitwise_and(off_ref[1, h], 15)
        block = jnp.where(here, dq_rows[h : h + 1, :], blocks_in[h].astype(F32))
        blocks[h] = block.astype(BF16)
        copy = pltpu.make_async_copy(blocks.at[h], place(dq_ref, h), block_sems.at[h])
        copy.start()
        writes.append(copy)
    for copy in writes:
        copy.wait()


def on_device(query, key, value, grad_out, offsets):
    length, width = query.shape
    heads = offsets.shape[1]
    dh = width // heads
    size = lax.axis_size("ctx")
    span = min(size, 128)
    slots = 2 * heads + STAT_ROWS
    mates = [(i, i ^ 1) for i in range(size)]
    vmem = pl.BlockSpec(memory_space=pltpu.VMEM)
    smem = pl.BlockSpec(memory_space=pltpu.SMEM)
    hbm = pl.BlockSpec(memory_space=pltpu.HBM)
    params = pltpu.CompilerParams(vmem_limit_bytes=VMEM_LIMIT)
    small = pl.CostEstimate(flops=1000, bytes_accessed=1000, transcendentals=0)
    large = pl.CostEstimate(flops=7 * 10**9, bytes_accessed=1000, transcendentals=0)

    def call(kernel, name, out_shape, in_specs, out_specs, scratch, cost=small, **kwargs):
        return pl.pallas_call(
            kernel,
            out_shape=out_shape,
            in_specs=in_specs,
            out_specs=out_specs,
            scratch_shapes=scratch,
            compiler_params=params,
            cost_estimate=cost,
            name=name,
            **kwargs,
        )

    def far_memory(*arrays):
        return [pltpu.with_memory_space_constraint(array, pltpu.HBM) for array in arrays]

    def near_memory(*arrays):
        return [pltpu.with_memory_space_constraint(array, pltpu.VMEM) for array in arrays]

    query_far = lax.ppermute(query, "ctx", mates)
    grad_far = lax.ppermute(grad_out, "ctx", mates)
    table = pltpu.VMEM((32, length), F32)
    own, spot, weight = call(
        functools.partial(pack_kernel, heads),
        "pack_rows",
        (pltpu.VMEM((48, dh), BF16), table, table),
        [smem] + [hbm] * 4,
        (vmem,) * 3,
        [
            pltpu.VMEM((4 * heads, 16, dh), BF16),
            pltpu.VMEM((48, dh), F32),
            pltpu.SemaphoreType.DMA((4 * heads,)),
        ],
        cost=large,
    )(*far_memory(offsets, key, value, query, grad_out))
    key_later, value_later, own = lax.optimization_barrier((key, value, own))
    key_far = lax.ppermute(key_later, "ctx", mates)
    value_far = lax.ppermute(value_later, "ctx", mates)
    repeat = min(span, 8)
    load, s_rows, dp_rows, far = call(
        functools.partial(stats_kernel, heads, span),
        "row_stats",
        (
            pltpu.HBM((span * slots, dh), BF16),
            pltpu.HBM((32, length), F32),
            pltpu.HBM((32, length), F32),
            pltpu.HBM((32, dh), BF16),
        ),
        [vmem] * 7,
        (hbm,) * 4,
        [
            table,
            table,
            pltpu.VMEM((32, dh), BF16),
            pltpu.VMEM((2 * slots, dh), F32),
            pltpu.VMEM((repeat * slots, dh), BF16),
            pltpu.SemaphoreType.DMA((span // repeat,)),
            pltpu.SemaphoreType.DMA((3,)),
        ],
    )(*near_memory(own, spot, weight, query_far, grad_far, key, value))
    groups = None
    if size > span:
        groups = [list(range(base, base + span)) for base in range(0, size, span)]
    received = lax.all_to_all(load, "ctx", 0, 0, axis_index_groups=groups, tiled=True)
    whole = pltpu.VMEM((length, width), BF16)
    wide = pltpu.VMEM((length, width), F32)
    rows = pltpu.VMEM((32, dh), F32)
    dq, dk, dv, partial, terms, blocks = call(
        functools.partial(main_kernel, heads),
        "near_levels",
        (
            pltpu.HBM((length, width), BF16),
            pltpu.HBM((length, width), F32),
            pltpu.HBM((length, width), F32),
            pltpu.HBM((length, width), BF16),
            pltpu.HBM((80, dh), F32),
            pltpu.HBM((heads, 16, dh), BF16),
        ),
        [hbm] * 4 + [vmem] * 7,
        (hbm,) * 6,
        [
            pltpu.SMEM(offsets.shape, jnp.int32),
            table,
            table,
            whole,
            whole,
            wide,
            wide,
            whole,
            pltpu.VMEM((80, dh), F32),
            pltpu.VMEM((heads, 16, dh), BF16),
            pltpu.SemaphoreType.DMA,
            pltpu.SemaphoreType.DMA,
            pltpu.SemaphoreType.DMA((2,)),
            pltpu.SemaphoreType.DMA,
            pltpu.SemaphoreType.DMA,
            pltpu.SemaphoreType.DMA((heads // 2, 4)),
        ],
        cost=large,
    )(
        *far_memory(offsets, s_rows, dp_rows, value_far),
        *near_memory(own, weight, query, key, value, grad_out, key_far),
    )
    returned = lax.ppermute(partial, "ctx", mates)
    mine, theirs = call(
        functools.partial(wide_kernel, heads, span),
        "third_level",
        (rows, rows),
        [vmem],
        (vmem,) * 2,
        [pltpu.VMEM((span * slots, dh), F32)],
        cost=large,
    )(*near_memory(received))
    got = lax.ppermute(theirs, "ctx", mates)
    return call(
        functools.partial(final_kernel, heads),
        "join",
        (pltpu.HBM((length, width), BF16),) * 3,
        [hbm] + [vmem] * 13 + [hbm],
        (hbm,) * 3,
        [
            pltpu.SMEM(offsets.shape, jnp.int32),
            pltpu.VMEM((64, dh), F32),
            pltpu.VMEM((heads, 16, dh), BF16),
            whole,
            whole,
            pltpu.SemaphoreType.DMA,
            pltpu.SemaphoreType.DMA((heads,)),
            pltpu.SemaphoreType.DMA((2, heads // 2)),
        ],
        input_output_aliases={14: 0},
    )(
        *far_memory(offsets),
        *near_memory(mine, got, own, far, spot, weight, s_rows, dp_rows, terms),
        *near_memory(dk, dv, blocks, returned),
        *far_memory(dq),
    )


def solution(mesh):
    placed = (P("ctx", None), P("ctx", None), P("ctx", None), P("ctx", None), P())
    return jax.shard_map(
        on_device,
        mesh=mesh,
        in_specs=placed,
        out_specs=(P("ctx", None), P("ctx", None), P("ctx", None)),
        check_vma=False,
    )
```

```python
import functools

import jax
import jax.numpy as jnp
from jax import lax
from jax.experimental import pallas as pl
from jax.experimental.pallas import tpu as pltpu
from jax.sharding import PartitionSpec as P

NEG = -1e30
F32 = jnp.float32
BF16 = jnp.bfloat16
STAT_ROWS = 4
VMEM_LIMIT = 16 * 1024 * 1024
LOG2E = 1.4426950408889634


def iota(shape, dim):
    return lax.broadcasted_iota(jnp.int32, shape, dim)


def dot_nt(a, b):
    return lax.dot_general(a, b, (((1,), (1,)), ((), ())), preferred_element_type=F32)


def dot_tn(a, b):
    return lax.dot_general(a, b, (((0,), (0,)), ((), ())), preferred_element_type=F32)


def dot_nn(a, b):
    return lax.dot_general(a, b, (((1,), (0,)), ((), ())), preferred_element_type=F32)


def block_rows(rows, heads):
    row = iota(rows.shape, 0)
    return jnp.concatenate(
        [jnp.where(row == h, rows, 0.0).astype(BF16) for h in range(heads)], axis=1
    )


def own_columns(wide_rows, heads):
    dh = wide_rows.shape[1] // heads
    row = iota((16, dh), 0)
    return sum(
        jnp.where(row == h, wide_rows[:, h * dh : (h + 1) * dh], 0.0) for h in range(heads)
    )


def offset_column(off_ref, level, heads, rows):
    row = jnp.bitwise_and(iota((rows, 1), 0), 15)
    column = jnp.zeros((rows, 1), jnp.int32)
    for h in range(heads):
        column = jnp.where(row == h, off_ref[level, h], column)
    return column


def level_one_keys(off_ref, heads, rows, length):
    pair = offset_column(off_ref, 0, heads, rows)
    wide = offset_column(off_ref, 1, heads, rows)
    lane = iota((rows, length), 1)
    chosen = jnp.bitwise_and(wide, 1) == pair
    return jnp.logical_and(jnp.bitwise_and(lane, 1) == pair, chosen)


def row_weights(off_ref, heads, length):
    both = level_one_keys(off_ref, heads, 32, length).astype(F32)
    return jnp.where(iota((32, length), 0) < 16, 1.0 + both, both)


def pack_kernel(
    heads, off_ref, q_ref, g_ref, out_ref, spot_ref, weight_ref, buf, acc, sems
):
    length, dh = q_ref.shape[0], out_ref.shape[1]
    copies = []
    for s, ref in enumerate((q_ref, g_ref)):
        for h in range(heads):
            base = pl.multiple_of(jnp.bitwise_and(off_ref[1, h], ~15), 16)
            slot = s * heads + h
            copy = pltpu.make_async_copy(
                ref.at[pl.ds(base, 16), pl.ds(h * dh, dh)], buf.at[slot], sems.at[slot]
            )
            copy.start()
            copies.append(copy)
    wide = offset_column(off_ref, 1, heads, 32)
    spot_ref[...] = (iota((32, length), 1) == wide).astype(F32)
    weight_ref[...] = row_weights(off_ref, heads, length)
    acc[...] = jnp.zeros_like(acc)
    row = iota((16, dh), 0)
    for s in range(2):
        for h in range(heads):
            slot = s * heads + h
            copies[slot].wait()
            own = row == jnp.bitwise_and(off_ref[1, h], 15)
            block = jnp.where(own, buf[slot].astype(F32), 0.0)
            acc[16 * s + h : 16 * s + h + 1, :] = jnp.sum(block, axis=0, keepdims=True)
    out_ref[...] = acc[...].astype(BF16)


def stats_kernel(
    heads, span, own_ref, spot_ref, weight_ref, qf_ref, gf_ref, k_ref, v_ref,
    load_ref, s_hbm, dp_hbm, far_hbm, s_ref, dp_ref, far_ref, acc, load, sems, row_sems,
):
    dh = own_ref.shape[1]
    part, slots = heads // 2, load_ref.shape[0] // span
    own = own_ref[...].astype(F32)
    spot = spot_ref[0:16, :].astype(BF16)

    def both_rows(whole, first):
        far = own_columns(dot_nn(spot, whole), heads)
        far_ref[first : first + 16, :] = far.astype(BF16)
        near = own[first : first + 16, :]
        return jnp.concatenate([block_rows(near, heads), block_rows(far, heads)], axis=0)

    queries, grads = both_rows(qf_ref[...], 0), both_rows(gf_ref[...], 16)
    s = dot_nt(queries, k_ref[...]) * (dh**-0.5 * LOG2E)
    dp = dot_nt(grads, v_ref[...])
    s_ref[...] = s
    dp_ref[...] = dp
    rows = [own_columns(dot_nn(spot, ref[...]), heads) for ref in (k_ref, v_ref)]
    rows += [own[0:16, :], own[16:32, :]]
    for i in range(4):
        for c in range(2):
            slot = c * slots + i * part
            acc[slot : slot + part, :] = rows[i][c * part : (c + 1) * part, :]
    weight = weight_ref[...]
    masked = jnp.where(weight > 0.0, s, NEG)
    m = jnp.max(masked, axis=1, keepdims=True)
    e = jnp.exp2(masked - m) * weight
    t = jnp.sum(e, axis=1, keepdims=True)
    d = jnp.sum(e * dp, axis=1, keepdims=True)
    lane = iota((32, 128), 1)
    table = jnp.where(lane == 0, m, jnp.where(lane == 1, t, jnp.where(lane == 2, d, 0.0)))
    table = jnp.concatenate([table, jnp.zeros((96, 128), F32)], axis=0).T[0:STAT_ROWS, :]
    high = table.astype(BF16).astype(F32)
    rest = table - high
    middle = rest.astype(BF16).astype(F32)
    low = (rest - middle).astype(BF16).astype(F32)
    table = high + pltpu.roll(middle, 32, 1) + pltpu.roll(low, 64, 1)
    for c in range(2):
        acc[c * slots + 4 * part : (c + 1) * slots, :] = table
    halves = acc[...].astype(BF16)
    stride = load.shape[0]
    for i in range(stride // (2 * slots)):
        load[2 * i * slots : 2 * (i + 1) * slots, :] = halves
    copies = [
        pltpu.make_async_copy(load, load_ref.at[pl.ds(i * stride, stride), :], sems.at[i])
        for i in range(span * slots // stride)
    ]
    for i, (near, away) in enumerate(((s_ref, s_hbm), (dp_ref, dp_hbm), (far_ref, far_hbm))):
        copies.append(pltpu.make_async_copy(near, away, row_sems.at[i]))
    for copy in copies:
        copy.start()
    for copy in copies:
        copy.wait()


def near_head(off_ref, h, inputs, outputs, waits, send):
    q_ref, k_ref, v_ref, g_ref, kf_ref, vf_ref = inputs
    dq_ref, dk_ref, dv_ref, ret_ref = outputs
    length, dh = q_ref.shape[0], q_ref.shape[1] // off_ref.shape[1]
    half = length // 2
    scale = dh**-0.5
    cols = slice(h * dh, (h + 1) * dh)
    q, k, v, g = q_ref[:, cols], k_ref[:, cols], v_ref[:, cols], g_ref[:, cols]
    if h == 0:
        s1, dp1 = dot_nt(k, q), dot_nt(v, g)
        waits[0].wait()
    pair, wide = off_ref[0, h], off_ref[1, h]
    pick = (iota((half, length), 1) == 2 * iota((half, length), 0) + pair).astype(BF16)
    kc = dot_nn(pick, kf_ref[:, cols]).astype(BF16)
    yield
    lanes = iota((1, length), 1)
    chosen = jnp.bitwise_and(lanes, 1) == pair
    a_t = chosen.astype(F32)
    a_u = (jnp.bitwise_and(iota((length, 1), 0), 1) == pair).astype(F32)
    if h > 0:
        s1 = dot_nt(k, q)
    s2 = dot_nt(kc, q) + jnp.where(chosen, 0.0, NEG)
    if h == 0:
        waits[1].wait()
    vc = dot_nn(pick, vf_ref[:, cols]).astype(BF16)
    yield
    m = jnp.maximum(jnp.max(s1, axis=0, keepdims=True), jnp.max(s2, axis=0, keepdims=True))
    m = m * (scale * LOG2E)
    if h > 0:
        dp1 = dot_nt(v, g)
    dp2 = dot_nt(vc, g)
    yield
    e1 = jnp.exp2(s1 * (scale * LOG2E) - m) * (1.0 + a_t * a_u)
    e2 = jnp.exp2(s2 * (scale * LOG2E) - m)
    total = jnp.sum(e1, axis=0, keepdims=True) + jnp.sum(e2, axis=0, keepdims=True)
    part = jnp.sum(e1 * dp1, axis=0, keepdims=True) + jnp.sum(e2 * dp2, axis=0, keepdims=True)
    yield
    inverse = jnp.where(lanes == wide, 0.0, 1.0 / total)
    delta = part * inverse
    p1 = e1 * inverse
    p2 = e2 * inverse
    ds1 = (scale * p1 * (dp1 - delta)).astype(BF16)
    ds2 = (scale * p2 * (dp2 - delta)).astype(BF16)
    p1 = p1.astype(BF16)
    p2 = p2.astype(BF16)
    yield
    dk_ref[:, cols] = dot_nn(ds1, q)
    dv_ref[:, cols] = dot_nn(p1, g)
    ret_ref[:half, cols] = dot_nn(ds2, q).astype(BF16)
    ret_ref[half:, cols] = dot_nn(p2, g).astype(BF16)
    dq_ref[:, cols] = (dot_tn(k, ds1) + dot_tn(kc, ds2)).T.astype(BF16)
    send(h)
    yield


def row_terms(heads, scores, products, weight, keys):
    masked = jnp.where(weight > 0.0, scores, NEG)
    peak = jnp.max(masked, axis=1, keepdims=True)
    e = jnp.exp2(masked - peak) * weight
    parts = []
    for x in (e * products, e):
        high = x.astype(BF16)
        parts += [high, (x - high.astype(F32)).astype(BF16)]
    sums = dot_nn(jnp.concatenate(parts, axis=0), keys)
    first = own_columns(sums[0:16, :] + sums[16:32, :], heads)
    second = own_columns(sums[32:48, :] + sums[48:64, :], heads)
    return first, second, peak


def main_kernel(
    heads, off_hbm, s_hbm, dp_hbm, vf_hbm, own_ref, weight_ref, q_ref, k_ref, v_ref, g_ref, kf_ref,
    dq_hbm, dk_hbm, dv_hbm, ret_hbm, terms_hbm, blocks_hbm,
    off_ref, s_ref, dp_ref, vf_ref, dq_ref, dk_ref, dv_ref, ret_ref, terms, blocks,
    off_sem, in_sem, row_sems, terms_sem, block_sem, out_sems,
):
    offsets = pltpu.make_async_copy(off_hbm, off_ref, off_sem)
    offsets.start()
    values = pltpu.make_async_copy(vf_hbm, vf_ref, in_sem)
    values.start()
    stats = [
        pltpu.make_async_copy(s_hbm, s_ref, row_sems.at[0]),
        pltpu.make_async_copy(dp_hbm, dp_ref, row_sems.at[1]),
    ]
    for copy in stats:
        copy.start()
    dh = q_ref.shape[1] // heads
    near = (dq_ref, dk_ref, dv_ref, ret_ref)
    writes = []

    def send(h):
        base = pl.multiple_of(jnp.bitwise_and(off_ref[1, h], ~15), 16)
        blocks[h] = dq_ref[pl.ds(base, 16), h * dh : (h + 1) * dh]
        if h == heads - 1:
            copy = pltpu.make_async_copy(blocks, blocks_hbm, block_sem)
            copy.start()
            writes.append(copy)
        if h % 2 == 1:
            cols = slice((h - 1) * dh, (h + 1) * dh)
            for i, (a, b) in enumerate(zip(near, (dq_hbm, dk_hbm, dv_hbm, ret_hbm))):
                sem = out_sems.at[h // 2, i]
                copy = pltpu.make_async_copy(a.at[:, cols], b.at[:, cols], sem)
                copy.start()
                writes.append(copy)

    inputs = (q_ref, k_ref, v_ref, g_ref, kf_ref, vf_ref)
    work = [near_head(off_ref, h, inputs, near, (offsets, values), send) for h in range(heads)]
    steps, lag = 6, 2
    for turn in range(steps + lag * (heads - 1)):
        for h in reversed(range(heads)):
            if 0 <= turn - lag * h < steps:
                next(work[h])
        if turn == steps:
            own = own_ref[...].astype(F32)
            queries, grads = block_rows(own[:16, :], heads), block_rows(own[16:, :], heads)
            far_s = dot_nt(queries, kf_ref[...]) * (dh**-0.5 * LOG2E)
            far_dp = dot_nt(grads, vf_ref[...])
            for copy in stats:
                copy.wait()
            weight = weight_ref[0:16, :]
            met = (weight > 1.0).astype(F32)
            near_row = row_terms(heads, s_ref[0:16, :], dp_ref[0:16, :], weight, k_ref[...])
            far_row = row_terms(heads, far_s, far_dp, met, kf_ref[...])
            lane = iota((16, dh), 1)
            peaks = jnp.where(lane == 0, near_row[2], jnp.where(lane == 1, far_row[2], 0.0))
            for i, term in enumerate(near_row[:2] + far_row[:2] + (peaks,)):
                terms[16 * i : 16 * i + 16, :] = term
            copy = pltpu.make_async_copy(terms, terms_hbm, terms_sem)
            copy.start()
            writes.append(copy)
    for copy in writes:
        copy.wait()


def wide_kernel(
    heads, span, recv_ref, mine_ref, theirs_ref, flat
):
    part, slots, dh = heads // 2, recv_ref.shape[0] // span, recv_ref.shape[1]
    scale = dh**-0.5
    me = lax.rem(lax.axis_index("ctx"), span)
    mate = jnp.bitwise_xor(me, 1)
    first = jnp.bitwise_and(me, 1) == 0
    flat[...] = recv_ref[...].astype(F32)

    def gathered(slot):
        return flat[pl.ds(slot, span, stride=slots), :]

    even = jnp.bitwise_and(iota((8, 128), 1), 1) == 0

    def stat(index):
        x = gathered(4 * part + index)
        x = x + pltpu.roll(x, 96, 1) + pltpu.roll(x, 64, 1)
        if span < 128:
            x = jnp.concatenate([x, jnp.zeros((128 - span, 128), F32)], axis=0)
        x = x.T
        near = jnp.where(first, x[0:8, :], x[part : part + 8, :])
        other = jnp.where(first, x[16:24, :], x[16 + part : 24 + part, :])
        other = jnp.where(even, pltpu.roll(other, 127, 1), pltpu.roll(other, 1, 1))
        return near[:, :span], other[:, :span]

    (m_a, m_b), (t_a, t_b), (d_a, d_b) = stat(0), stat(1), stat(2)
    row = iota((16, span), 0)
    device = iota((span, 1), 0)
    k_w, v_w, q_w, g_w = [
        [gathered(i * part + j).astype(BF16) for j in range(part)] for i in range(4)
    ]
    m_c, t_c, d_c = [jnp.zeros((8, span), F32) for _ in range(3)]
    s_key, dp_key, s_row, dp_row = [jnp.zeros((16, span), F32) for _ in range(4)]

    def two_rows(x, j, table):
        for index, device_of in enumerate((me, mate)):
            one = jnp.sum(jnp.where(device == device_of, x, 0.0), axis=0, keepdims=True)
            table = jnp.where(row == 8 * index + j, one, table)
        return table

    for j in range(part):
        s = dot_nt(k_w[j], q_w[j]) * (scale * LOG2E)
        dp = dot_nt(v_w[j], g_w[j])
        m = jnp.max(s, axis=0, keepdims=True)
        e = jnp.exp2(s - m)
        here = row[:8] == j
        m_c = jnp.where(here, m, m_c)
        t_c = jnp.where(here, jnp.sum(e, axis=0, keepdims=True), t_c)
        d_c = jnp.where(here, jnp.sum(e * dp, axis=0, keepdims=True), d_c)
        s_key = two_rows(s, j, s_key)
        dp_key = two_rows(dp, j, dp_key)
        s_row = two_rows(dot_nt(q_w[j], k_w[j]) * (scale * LOG2E), j, s_row)
        dp_row = two_rows(dot_nt(g_w[j], v_w[j]), j, dp_row)
    m_all = jnp.maximum(jnp.maximum(m_a, m_b), m_c)
    w_a, w_b, w_c = jnp.exp2(m_a - m_all), jnp.exp2(m_b - m_all), jnp.exp2(m_c - m_all)
    inverse = 1.0 / (t_a * w_a + t_b * w_b + t_c * w_c)
    delta = (d_a * w_a + d_b * w_b + d_c * w_c) * inverse

    def twice(x):
        return jnp.concatenate([x, x], axis=0)

    def column(x, index):
        return jnp.sum(jnp.where(iota((8, span), 1) == index, x, 0.0), axis=1, keepdims=True)

    p_key = jnp.exp2(s_key - twice(m_all)) * twice(inverse)
    ds_key = scale * p_key * (dp_key - twice(delta))
    of_me = [column(x, me) for x in (m_all, inverse, delta)]
    of_mate = [column(x, mate) for x in (m_all, inverse, delta)]
    m_r, i_r, d_r = [jnp.concatenate(pair, axis=0) for pair in zip(of_me, of_mate)]
    ds_row = scale * (jnp.exp2(s_row - m_r) * i_r) * (dp_row - d_r)

    def times(left, right):
        index = jnp.bitwise_and(row, 7)
        return sum(
            dot_nn(jnp.where(index == j, left, 0.0).astype(BF16), right[j]) for j in range(part)
        )

    terms = (times(ds_row, k_w), times(ds_key, q_w), times(p_key, g_w))
    lane = iota((8, dh), 1)
    for ref, base, columns in ((mine_ref, 0, of_me + of_mate), (theirs_ref, 8, of_mate + of_me)):
        for i, term in enumerate(terms):
            ref[8 * i : 8 * i + 8, :] = term[base : base + 8, :]
        table = jnp.zeros((8, dh), F32)
        for i, value in enumerate(columns):
            table = jnp.where(lane == i, value, table)
        ref[24:32, :] = table


def final_kernel(
    heads, off_hbm, mine_ref, got_ref, own_ref, far_ref, spot_ref, weight_ref, s_ref, dp_ref,
    terms_ref, dki, dvi, blocks_in, ret, dq_in, dq_ref, dk_ref, dv_ref,
    off_ref, full, blocks, dko, dvo, off_sem, block_sems, write_sems,
):
    offsets = pltpu.make_async_copy(off_hbm, off_ref, off_sem)
    offsets.start()
    length, dh = dki.shape[0], own_ref.shape[1]
    half, part = length // 2, heads // 2
    scale = dh**-0.5

    def place(ref, h):
        base = pl.multiple_of(jnp.bitwise_and(off_ref[1, h], ~15), 16)
        return ref.at[pl.ds(base, 16), pl.ds(h * dh, dh)]

    chunks = [slice(2 * j * dh, 2 * (j + 1) * dh) for j in range(part)]
    own, far = own_ref[...].astype(F32), far_ref[...].astype(F32)
    first = jnp.bitwise_and(lax.axis_index("ctx"), 1) == 0
    mine, got = mine_ref[...], got_ref[...]
    low, high = jnp.where(first, mine, got), jnp.where(first, got, mine)
    full[...] = jnp.zeros_like(full)
    for i in range(4):
        full[16 * i : 16 * i + part, :] = low[8 * i : 8 * i + part, :]
        full[16 * i + part : 16 * i + heads, :] = high[8 * i : 8 * i + part, :]
    dq_wide, dk_rows, dv_rows, table = [full[16 * i : 16 * i + 16, :] for i in range(4)]
    m_me, i_me, d_me = [table[:, i : i + 1] for i in range(3)]
    m_two, i_two, d_two = [
        jnp.concatenate([table[:, i : i + 1], table[:, i + 3 : i + 4]], axis=0) for i in range(3)
    ]
    weight = weight_ref[...]
    p_two = jnp.exp2(jnp.where(weight > 0.0, s_ref[...] - m_two, NEG)) * weight * i_two
    ds_two = scale * p_two * (dp_ref[...] - d_two)
    terms = [terms_ref[16 * i : 16 * i + 16, :] for i in range(5)]
    dq_rows = dq_wide
    for i in range(2):
        share = scale * jnp.exp2(terms[4][:, i : i + 1] - m_me) * i_me
        dq_rows += share * (terms[2 * i] - d_me * terms[2 * i + 1])
    spot = spot_ref[...]
    offsets.wait()
    writes = []

    def spread(left, array, rows):
        near = own[16 * array : 16 * array + 16, :]
        high = rows.astype(BF16).astype(F32)
        left = jnp.concatenate([left, spot], axis=0).T.astype(BF16)
        parts = (near, far[16 * array : 16 * array + 16, :], high, rows - high)
        return left, jnp.concatenate([block_rows(part, heads) for part in parts], axis=0)

    for index, (base, out, out_ref, left, right) in enumerate(
        (
            (dki, dko, dk_ref) + spread(ds_two, 0, dk_rows),
            (dvi, dvo, dv_ref) + spread(p_two, 1, dv_rows),
        )
    ):
        back = slice(index * half, (index + 1) * half)
        for j, chunk in enumerate(chunks):
            for h in (2 * j, 2 * j + 1):
                cols = slice(h * dh, (h + 1) * dh)
                pick = iota((length, half), 0) == 2 * iota((length, half), 1) + off_ref[0, h]
                added = dot_nn(left, right[:, cols]) + dot_nn(pick.astype(BF16), ret[back, cols])
                out[:, cols] = (base[:, cols] + added).astype(BF16)
            sem = write_sems.at[index, j]
            copy = pltpu.make_async_copy(out.at[:, chunk], out_ref.at[:, chunk], sem)
            copy.start()
            writes.append(copy)
    for h in range(heads):
        here = iota((16, dh), 0) == jnp.bitwise_and(off_ref[1, h], 15)
        block = jnp.where(here, dq_rows[h : h + 1, :], blocks_in[h].astype(F32))
        blocks[h] = block.astype(BF16)
        copy = pltpu.make_async_copy(blocks.at[h], place(dq_ref, h), block_sems.at[h])
        copy.start()
        writes.append(copy)
    for copy in writes:
        copy.wait()


def on_device(query, key, value, grad_out, offsets):
    length, width = query.shape
    heads = offsets.shape[1]
    dh = width // heads
    size = lax.axis_size("ctx")
    span = min(size, 128)
    slots = 2 * heads + STAT_ROWS
    mates = [(i, i ^ 1) for i in range(size)]
    vmem = pl.BlockSpec(memory_space=pltpu.VMEM)
    smem = pl.BlockSpec(memory_space=pltpu.SMEM)
    hbm = pl.BlockSpec(memory_space=pltpu.HBM)
    params = pltpu.CompilerParams(vmem_limit_bytes=VMEM_LIMIT)
    small = pl.CostEstimate(flops=1000, bytes_accessed=1000, transcendentals=0)
    large = pl.CostEstimate(flops=7 * 10**9, bytes_accessed=1000, transcendentals=0)

    def call(kernel, name, out_shape, in_specs, out_specs, scratch, cost=small, **kwargs):
        return pl.pallas_call(
            kernel,
            out_shape=out_shape,
            in_specs=in_specs,
            out_specs=out_specs,
            scratch_shapes=scratch,
            compiler_params=params,
            cost_estimate=cost,
            name=name,
            **kwargs,
        )

    def far_memory(*arrays):
        return [pltpu.with_memory_space_constraint(array, pltpu.HBM) for array in arrays]

    def near_memory(*arrays):
        return [pltpu.with_memory_space_constraint(array, pltpu.VMEM) for array in arrays]

    query_far = lax.ppermute(query, "ctx", mates)
    grad_far = lax.ppermute(grad_out, "ctx", mates)
    table = pltpu.VMEM((32, length), F32)
    own, spot, weight = call(
        functools.partial(pack_kernel, heads),
        "pack_rows",
        (pltpu.VMEM((32, dh), BF16), table, table),
        [smem] + [hbm] * 2,
        (vmem,) * 3,
        [
            pltpu.VMEM((2 * heads, 16, dh), BF16),
            pltpu.VMEM((32, dh), F32),
            pltpu.SemaphoreType.DMA((2 * heads,)),
        ],
        cost=large,
    )(*far_memory(offsets, query, grad_out))
    key_later, value_later, own = lax.optimization_barrier((key, value, own))
    key_far = lax.ppermute(key_later, "ctx", mates)
    value_far = lax.ppermute(value_later, "ctx", mates)
    repeat = min(span, 8)
    load, s_rows, dp_rows, far = call(
        functools.partial(stats_kernel, heads, span),
        "row_stats",
        (
            pltpu.HBM((span * slots, dh), BF16),
            pltpu.HBM((32, length), F32),
            pltpu.HBM((32, length), F32),
            pltpu.HBM((32, dh), BF16),
        ),
        [vmem] * 7,
        (hbm,) * 4,
        [
            table,
            table,
            pltpu.VMEM((32, dh), BF16),
            pltpu.VMEM((2 * slots, dh), F32),
            pltpu.VMEM((repeat * slots, dh), BF16),
            pltpu.SemaphoreType.DMA((span // repeat,)),
            pltpu.SemaphoreType.DMA((3,)),
        ],
    )(*near_memory(own, spot, weight, query_far, grad_far, key, value))
    groups = None
    if size > span:
        groups = [list(range(base, base + span)) for base in range(0, size, span)]
    received = lax.all_to_all(load, "ctx", 0, 0, axis_index_groups=groups, tiled=True)
    whole = pltpu.VMEM((length, width), BF16)
    wide = pltpu.VMEM((length, width), F32)
    rows = pltpu.VMEM((32, dh), F32)
    dq, dk, dv, partial, terms, blocks = call(
        functools.partial(main_kernel, heads),
        "near_levels",
        (
            pltpu.HBM((length, width), BF16),
            pltpu.HBM((length, width), F32),
            pltpu.HBM((length, width), F32),
            pltpu.HBM((length, width), BF16),
            pltpu.HBM((80, dh), F32),
            pltpu.HBM((heads, 16, dh), BF16),
        ),
        [hbm] * 4 + [vmem] * 7,
        (hbm,) * 6,
        [
            pltpu.SMEM(offsets.shape, jnp.int32),
            table,
            table,
            whole,
            whole,
            wide,
            wide,
            whole,
            pltpu.VMEM((80, dh), F32),
            pltpu.VMEM((heads, 16, dh), BF16),
            pltpu.SemaphoreType.DMA,
            pltpu.SemaphoreType.DMA,
            pltpu.SemaphoreType.DMA((2,)),
            pltpu.SemaphoreType.DMA,
            pltpu.SemaphoreType.DMA,
            pltpu.SemaphoreType.DMA((heads // 2, 4)),
        ],
        cost=large,
    )(
        *far_memory(offsets, s_rows, dp_rows, value_far),
        *near_memory(own, weight, query, key, value, grad_out, key_far),
    )
    returned = lax.ppermute(partial, "ctx", mates)
    mine, theirs = call(
        functools.partial(wide_kernel, heads, span),
        "third_level",
        (rows, rows),
        [vmem],
        (vmem,) * 2,
        [pltpu.VMEM((span * slots, dh), F32)],
        cost=large,
    )(*near_memory(received))
    got = lax.ppermute(theirs, "ctx", mates)
    return call(
        functools.partial(final_kernel, heads),
        "join",
        (pltpu.HBM((length, width), BF16),) * 3,
        [hbm] + [vmem] * 13 + [hbm],
        (hbm,) * 3,
        [
            pltpu.SMEM(offsets.shape, jnp.int32),
            pltpu.VMEM((64, dh), F32),
            pltpu.VMEM((heads, 16, dh), BF16),
            whole,
            whole,
            pltpu.SemaphoreType.DMA,
            pltpu.SemaphoreType.DMA((heads,)),
            pltpu.SemaphoreType.DMA((2, heads // 2)),
        ],
        input_output_aliases={14: 0},
    )(
        *far_memory(offsets),
        *near_memory(mine, got, own, far, spot, weight, s_rows, dp_rows, terms),
        *near_memory(dk, dv, blocks, returned),
        *far_memory(dq),
    )


def solution(mesh):
    placed = (P("ctx", None), P("ctx", None), P("ctx", None), P("ctx", None), P())
    return jax.shard_map(
        on_device,
        mesh=mesh,
        in_specs=placed,
        out_specs=(P("ctx", None), P("ctx", None), P("ctx", None)),
        check_vma=False,
    )
```

```python
import functools

import jax
import jax.numpy as jnp
from jax import lax
from jax.experimental import pallas as pl
from jax.experimental.pallas import tpu as pltpu
from jax.sharding import PartitionSpec as P

NEG = -1e30
F32 = jnp.float32
BF16 = jnp.bfloat16
STAT_ROWS = 4
VMEM_LIMIT = 16 * 1024 * 1024
LOG2E = 1.4426950408889634


def iota(shape, dim):
    return lax.broadcasted_iota(jnp.int32, shape, dim)


def dot_nt(a, b):
    return lax.dot_general(a, b, (((1,), (1,)), ((), ())), preferred_element_type=F32)


def dot_tn(a, b):
    return lax.dot_general(a, b, (((0,), (0,)), ((), ())), preferred_element_type=F32)


def dot_nn(a, b):
    return lax.dot_general(a, b, (((1,), (0,)), ((), ())), preferred_element_type=F32)


def block_rows(rows, heads):
    row = iota(rows.shape, 0)
    return jnp.concatenate(
        [jnp.where(row == h, rows, 0.0).astype(BF16) for h in range(heads)], axis=1
    )


def own_columns(wide_rows, heads):
    dh = wide_rows.shape[1] // heads
    row = iota((16, dh), 0)
    return sum(
        jnp.where(row == h, wide_rows[:, h * dh : (h + 1) * dh], 0.0) for h in range(heads)
    )


def offset_column(off_ref, level, heads, rows):
    row = jnp.bitwise_and(iota((rows, 1), 0), 15)
    column = jnp.zeros((rows, 1), jnp.int32)
    for h in range(heads):
        column = jnp.where(row == h, off_ref[level, h], column)
    return column


def level_one_keys(off_ref, heads, rows, length):
    pair = offset_column(off_ref, 0, heads, rows)
    wide = offset_column(off_ref, 1, heads, rows)
    lane = iota((rows, length), 1)
    chosen = jnp.bitwise_and(wide, 1) == pair
    return jnp.logical_and(jnp.bitwise_and(lane, 1) == pair, chosen)


def row_weights(off_ref, heads, length):
    both = level_one_keys(off_ref, heads, 32, length).astype(F32)
    return jnp.where(iota((32, length), 0) < 16, 1.0 + both, both)


def pack_kernel(
    heads, off_ref, q_ref, g_ref, out_ref, spot_ref, weight_ref, buf, acc, sems
):
    length, dh = q_ref.shape[0], out_ref.shape[1]
    copies = []
    for s, ref in enumerate((q_ref, g_ref)):
        for h in range(heads):
            base = pl.multiple_of(jnp.bitwise_and(off_ref[1, h], ~15), 16)
            slot = s * heads + h
            copy = pltpu.make_async_copy(
                ref.at[pl.ds(base, 16), pl.ds(h * dh, dh)], buf.at[slot], sems.at[slot]
            )
            copy.start()
            copies.append(copy)
    wide = offset_column(off_ref, 1, heads, 32)
    spot_ref[...] = (iota((32, length), 1) == wide).astype(F32)
    weight_ref[...] = row_weights(off_ref, heads, length)
    acc[...] = jnp.zeros_like(acc)
    row = iota((16, dh), 0)
    for s in range(2):
        for h in range(heads):
            slot = s * heads + h
            copies[slot].wait()
            own = row == jnp.bitwise_and(off_ref[1, h], 15)
            block = jnp.where(own, buf[slot].astype(F32), 0.0)
            acc[16 * s + h : 16 * s + h + 1, :] = jnp.sum(block, axis=0, keepdims=True)
    out_ref[...] = acc[...].astype(BF16)


def stats_kernel(
    heads, span, own_ref, spot_ref, weight_ref, qf_ref, gf_ref, k_ref, v_ref,
    load_ref, s_hbm, dp_hbm, far_hbm, s_ref, dp_ref, far_ref, acc, load, sems, row_sems,
):
    dh = own_ref.shape[1]
    part, slots = heads // 2, load_ref.shape[0] // span
    own = own_ref[...].astype(F32)
    spot = spot_ref[0:16, :].astype(BF16)

    def both_rows(whole, first):
        picked = dot_nn(spot, whole)
        far_ref[first : first + 16, :] = own_columns(picked, heads).astype(BF16)
        diagonal = iota(picked.shape, 1) // dh == iota(picked.shape, 0)
        far = jnp.where(diagonal, picked, 0.0).astype(BF16)
        return jnp.concatenate([block_rows(own[first : first + 16, :], heads), far], axis=0)

    queries, grads = both_rows(qf_ref[...], 0), both_rows(gf_ref[...], 16)
    s = dot_nt(queries, k_ref[...]) * (dh**-0.5 * LOG2E)
    dp = dot_nt(grads, v_ref[...])
    s_ref[...] = s
    dp_ref[...] = dp
    early = []
    for i, (near, away) in enumerate(((s_ref, s_hbm), (dp_ref, dp_hbm), (far_ref, far_hbm))):
        copy = pltpu.make_async_copy(near, away, row_sems.at[i])
        copy.start()
        early.append(copy)
    rows = [own_columns(dot_nn(spot, ref[...]), heads) for ref in (k_ref, v_ref)]
    rows += [own[0:16, :], own[16:32, :]]
    for i in range(4):
        for c in range(2):
            slot = c * slots + i * part
            acc[slot : slot + part, :] = rows[i][c * part : (c + 1) * part, :]
    weight = weight_ref[...]
    masked = jnp.where(weight > 0.0, s, NEG)
    m = jnp.max(masked, axis=1, keepdims=True)
    e = jnp.exp2(masked - m) * weight
    t = jnp.sum(e, axis=1, keepdims=True)
    d = jnp.sum(e * dp, axis=1, keepdims=True)
    lane = iota((32, 128), 1)
    table = jnp.where(lane == 0, m, jnp.where(lane == 1, t, jnp.where(lane == 2, d, 0.0)))
    table = jnp.concatenate([table, jnp.zeros((96, 128), F32)], axis=0).T[0:STAT_ROWS, :]
    high = table.astype(BF16).astype(F32)
    rest = table - high
    middle = rest.astype(BF16).astype(F32)
    low = (rest - middle).astype(BF16).astype(F32)
    table = high + pltpu.roll(middle, 32, 1) + pltpu.roll(low, 64, 1)
    for c in range(2):
        acc[c * slots + 4 * part : (c + 1) * slots, :] = table
    halves = acc[...].astype(BF16)
    stride = load.shape[0]
    for i in range(stride // (2 * slots)):
        load[2 * i * slots : 2 * (i + 1) * slots, :] = halves
    copies = [
        pltpu.make_async_copy(load, load_ref.at[pl.ds(i * stride, stride), :], sems.at[i])
        for i in range(span * slots // stride)
    ]
    for copy in copies:
        copy.start()
    for copy in copies + early:
        copy.wait()


def near_head(off_ref, h, inputs, outputs, waits, send):
    q_ref, k_ref, v_ref, g_ref, kf_ref, vf_ref = inputs
    dq_ref, dk_ref, dv_ref, ret_ref = outputs
    length, dh = q_ref.shape[0], q_ref.shape[1] // off_ref.shape[1]
    half = length // 2
    scale = dh**-0.5
    cols = slice(h * dh, (h + 1) * dh)
    q, k, v, g = q_ref[:, cols], k_ref[:, cols], v_ref[:, cols], g_ref[:, cols]
    if h == 0:
        s1, dp1 = dot_nt(k, q), dot_nt(v, g)
        waits[0].wait()
    pair, wide = off_ref[0, h], off_ref[1, h]
    pick = (iota((half, length), 1) == 2 * iota((half, length), 0) + pair).astype(BF16)
    kc = dot_nn(pick, kf_ref[:, cols]).astype(BF16)
    yield
    lanes = iota((1, length), 1)
    chosen = jnp.bitwise_and(lanes, 1) == pair
    a_t = chosen.astype(F32)
    a_u = (jnp.bitwise_and(iota((length, 1), 0), 1) == pair).astype(F32)
    if h > 0:
        s1 = dot_nt(k, q)
    s2 = dot_nt(kc, q) + jnp.where(chosen, 0.0, NEG)
    if h == 0:
        waits[1].wait()
    vc = dot_nn(pick, vf_ref[:, cols]).astype(BF16)
    yield
    m = jnp.maximum(jnp.max(s1, axis=0, keepdims=True), jnp.max(s2, axis=0, keepdims=True))
    m = m * (scale * LOG2E)
    if h > 0:
        dp1 = dot_nt(v, g)
    dp2 = dot_nt(vc, g)
    yield
    e1 = jnp.exp2(s1 * (scale * LOG2E) - m) * (1.0 + a_t * a_u)
    e2 = jnp.exp2(s2 * (scale * LOG2E) - m)
    total = jnp.sum(e1, axis=0, keepdims=True) + jnp.sum(e2, axis=0, keepdims=True)
    part = jnp.sum(e1 * dp1, axis=0, keepdims=True) + jnp.sum(e2 * dp2, axis=0, keepdims=True)
    yield
    inverse = jnp.where(lanes == wide, 0.0, 1.0 / total)
    delta = part * inverse
    p1 = e1 * inverse
    p2 = e2 * inverse
    ds1 = (scale * p1 * (dp1 - delta)).astype(BF16)
    ds2 = (scale * p2 * (dp2 - delta)).astype(BF16)
    p1 = p1.astype(BF16)
    p2 = p2.astype(BF16)
    yield
    dk_ref[:, cols] = dot_nn(ds1, q)
    dv_ref[:, cols] = dot_nn(p1, g)
    ret_ref[:half, cols] = dot_nn(ds2, q).astype(BF16)
    ret_ref[half:, cols] = dot_nn(p2, g).astype(BF16)
    dq_ref[:, cols] = (dot_tn(k, ds1) + dot_tn(kc, ds2)).T.astype(BF16)
    send(h)
    yield


def row_terms(heads, scores, products, weight, keys):
    masked = jnp.where(weight > 0.0, scores, NEG)
    peak = jnp.max(masked, axis=1, keepdims=True)
    e = jnp.exp2(masked - peak) * weight
    parts = []
    for x in (e * products, e):
        high = x.astype(BF16)
        parts += [high, (x - high.astype(F32)).astype(BF16)]
    sums = dot_nn(jnp.concatenate(parts, axis=0), keys)
    first = own_columns(sums[0:16, :] + sums[16:32, :], heads)
    second = own_columns(sums[32:48, :] + sums[48:64, :], heads)
    return first, second, peak


def main_kernel(
    heads, off_hbm, s_hbm, dp_hbm, vf_hbm, own_ref, weight_ref, q_ref, k_ref, v_ref, g_ref, kf_ref,
    dq_hbm, dk_hbm, dv_hbm, ret_hbm, terms_hbm, blocks_hbm,
    off_ref, s_ref, dp_ref, vf_ref, dq_ref, dk_ref, dv_ref, ret_ref, terms, blocks,
    off_sem, in_sem, row_sems, terms_sem, block_sem, out_sems,
):
    offsets = pltpu.make_async_copy(off_hbm, off_ref, off_sem)
    offsets.start()
    values = pltpu.make_async_copy(vf_hbm, vf_ref, in_sem)
    values.start()
    stats = [
        pltpu.make_async_copy(s_hbm, s_ref, row_sems.at[0]),
        pltpu.make_async_copy(dp_hbm, dp_ref, row_sems.at[1]),
    ]
    for copy in stats:
        copy.start()
    dh = q_ref.shape[1] // heads
    near = (dq_ref, dk_ref, dv_ref, ret_ref)
    writes = []

    def send(h):
        base = pl.multiple_of(jnp.bitwise_and(off_ref[1, h], ~15), 16)
        blocks[h] = dq_ref[pl.ds(base, 16), h * dh : (h + 1) * dh]
        if h == heads - 1:
            copy = pltpu.make_async_copy(blocks, blocks_hbm, block_sem)
            copy.start()
            writes.append(copy)
        if h % 2 == 1:
            cols = slice((h - 1) * dh, (h + 1) * dh)
            for i, (a, b) in enumerate(zip(near, (dq_hbm, dk_hbm, dv_hbm, ret_hbm))):
                sem = out_sems.at[h // 2, i]
                copy = pltpu.make_async_copy(a.at[:, cols], b.at[:, cols], sem)
                copy.start()
                writes.append(copy)

    inputs = (q_ref, k_ref, v_ref, g_ref, kf_ref, vf_ref)
    work = [near_head(off_ref, h, inputs, near, (offsets, values), send) for h in range(heads)]
    steps, lag = 6, 2
    for turn in range(steps + lag * (heads - 1)):
        for h in reversed(range(heads)):
            if 0 <= turn - lag * h < steps:
                next(work[h])
        if turn == steps:
            own = own_ref[...].astype(F32)
            queries, grads = block_rows(own[:16, :], heads), block_rows(own[16:, :], heads)
            far_s = dot_nt(queries, kf_ref[...]) * (dh**-0.5 * LOG2E)
            far_dp = dot_nt(grads, vf_ref[...])
            for copy in stats:
                copy.wait()
            weight = weight_ref[0:16, :]
            met = (weight > 1.0).astype(F32)
            near_row = row_terms(heads, s_ref[0:16, :], dp_ref[0:16, :], weight, k_ref[...])
            far_row = row_terms(heads, far_s, far_dp, met, kf_ref[...])
            lane = iota((16, dh), 1)
            peaks = jnp.where(lane == 0, near_row[2], jnp.where(lane == 1, far_row[2], 0.0))
            for i, term in enumerate(near_row[:2] + far_row[:2] + (peaks,)):
                terms[16 * i : 16 * i + 16, :] = term
            copy = pltpu.make_async_copy(terms, terms_hbm, terms_sem)
            copy.start()
            writes.append(copy)
    for copy in writes:
        copy.wait()


def wide_kernel(
    heads, span, recv_ref, mine_ref, theirs_ref, flat
):
    part, slots, dh = heads // 2, recv_ref.shape[0] // span, recv_ref.shape[1]
    scale = dh**-0.5
    me = lax.rem(lax.axis_index("ctx"), span)
    mate = jnp.bitwise_xor(me, 1)
    first = jnp.bitwise_and(me, 1) == 0
    flat[...] = recv_ref[...].astype(F32)

    def gathered(slot):
        return flat[pl.ds(slot, span, stride=slots), :]

    even = jnp.bitwise_and(iota((8, 128), 1), 1) == 0

    def stat(index):
        x = gathered(4 * part + index)
        x = x + pltpu.roll(x, 96, 1) + pltpu.roll(x, 64, 1)
        if span < 128:
            x = jnp.concatenate([x, jnp.zeros((128 - span, 128), F32)], axis=0)
        x = x.T
        near = jnp.where(first, x[0:8, :], x[part : part + 8, :])
        other = jnp.where(first, x[16:24, :], x[16 + part : 24 + part, :])
        other = jnp.where(even, pltpu.roll(other, 127, 1), pltpu.roll(other, 1, 1))
        return near[:, :span], other[:, :span]

    (m_a, m_b), (t_a, t_b), (d_a, d_b) = stat(0), stat(1), stat(2)
    row = iota((16, span), 0)
    device = iota((span, 1), 0)
    k_w, v_w, q_w, g_w = [
        [gathered(i * part + j).astype(BF16) for j in range(part)] for i in range(4)
    ]
    m_c, t_c, d_c = [jnp.zeros((8, span), F32) for _ in range(3)]
    s_key, dp_key, s_row, dp_row = [jnp.zeros((16, span), F32) for _ in range(4)]

    def two_rows(x, j, table):
        for index, device_of in enumerate((me, mate)):
            one = jnp.sum(jnp.where(device == device_of, x, 0.0), axis=0, keepdims=True)
            table = jnp.where(row == 8 * index + j, one, table)
        return table

    for j in range(part):
        s = dot_nt(k_w[j], q_w[j]) * (scale * LOG2E)
        dp = dot_nt(v_w[j], g_w[j])
        m = jnp.max(s, axis=0, keepdims=True)
        e = jnp.exp2(s - m)
        here = row[:8] == j
        m_c = jnp.where(here, m, m_c)
        t_c = jnp.where(here, jnp.sum(e, axis=0, keepdims=True), t_c)
        d_c = jnp.where(here, jnp.sum(e * dp, axis=0, keepdims=True), d_c)
        s_key = two_rows(s, j, s_key)
        dp_key = two_rows(dp, j, dp_key)
        s_row = two_rows(dot_nt(q_w[j], k_w[j]) * (scale * LOG2E), j, s_row)
        dp_row = two_rows(dot_nt(g_w[j], v_w[j]), j, dp_row)
    m_all = jnp.maximum(jnp.maximum(m_a, m_b), m_c)
    w_a, w_b, w_c = jnp.exp2(m_a - m_all), jnp.exp2(m_b - m_all), jnp.exp2(m_c - m_all)
    inverse = 1.0 / (t_a * w_a + t_b * w_b + t_c * w_c)
    delta = (d_a * w_a + d_b * w_b + d_c * w_c) * inverse

    def twice(x):
        return jnp.concatenate([x, x], axis=0)

    def column(x, index):
        return jnp.sum(jnp.where(iota((8, span), 1) == index, x, 0.0), axis=1, keepdims=True)

    p_key = jnp.exp2(s_key - twice(m_all)) * twice(inverse)
    ds_key = scale * p_key * (dp_key - twice(delta))
    of_me = [column(x, me) for x in (m_all, inverse, delta)]
    of_mate = [column(x, mate) for x in (m_all, inverse, delta)]
    m_r, i_r, d_r = [jnp.concatenate(pair, axis=0) for pair in zip(of_me, of_mate)]
    ds_row = scale * (jnp.exp2(s_row - m_r) * i_r) * (dp_row - d_r)

    def times(left, right):
        index = jnp.bitwise_and(row, 7)
        return sum(
            dot_nn(jnp.where(index == j, left, 0.0).astype(BF16), right[j]) for j in range(part)
        )

    terms = (times(ds_row, k_w), times(ds_key, q_w), times(p_key, g_w))
    lane = iota((8, dh), 1)
    for ref, base, columns in ((mine_ref, 0, of_me + of_mate), (theirs_ref, 8, of_mate + of_me)):
        for i, term in enumerate(terms):
            ref[8 * i : 8 * i + 8, :] = term[base : base + 8, :]
        table = jnp.zeros((8, dh), F32)
        for i, value in enumerate(columns):
            table = jnp.where(lane == i, value, table)
        ref[24:32, :] = table


def final_kernel(
    heads, off_hbm, mine_ref, got_ref, own_ref, far_ref, spot_ref, weight_ref, s_ref, dp_ref,
    terms_ref, dki, dvi, blocks_in, ret, dq_in, dq_ref, dk_ref, dv_ref,
    off_ref, full, blocks, dko, dvo, off_sem, block_sems, write_sems,
):
    offsets = pltpu.make_async_copy(off_hbm, off_ref, off_sem)
    offsets.start()
    length, dh = dki.shape[0], own_ref.shape[1]
    half, part = length // 2, heads // 2
    scale = dh**-0.5

    def place(ref, h):
        base = pl.multiple_of(jnp.bitwise_and(off_ref[1, h], ~15), 16)
        return ref.at[pl.ds(base, 16), pl.ds(h * dh, dh)]

    chunks = [slice(2 * j * dh, 2 * (j + 1) * dh) for j in range(part)]
    own, far = own_ref[...].astype(F32), far_ref[...].astype(F32)
    first = jnp.bitwise_and(lax.axis_index("ctx"), 1) == 0
    mine, got = mine_ref[...], got_ref[...]
    low, high = jnp.where(first, mine, got), jnp.where(first, got, mine)
    full[...] = jnp.zeros_like(full)
    for i in range(4):
        full[16 * i : 16 * i + part, :] = low[8 * i : 8 * i + part, :]
        full[16 * i + part : 16 * i + heads, :] = high[8 * i : 8 * i + part, :]
    dq_wide, dk_rows, dv_rows, table = [full[16 * i : 16 * i + 16, :] for i in range(4)]
    m_me, i_me, d_me = [table[:, i : i + 1] for i in range(3)]
    m_two, i_two, d_two = [
        jnp.concatenate([table[:, i : i + 1], table[:, i + 3 : i + 4]], axis=0) for i in range(3)
    ]
    weight = weight_ref[...]
    p_two = jnp.exp2(jnp.where(weight > 0.0, s_ref[...] - m_two, NEG)) * weight * i_two
    ds_two = scale * p_two * (dp_ref[...] - d_two)
    terms = [terms_ref[16 * i : 16 * i + 16, :] for i in range(5)]
    dq_rows = dq_wide
    for i in range(2):
        share = scale * jnp.exp2(terms[4][:, i : i + 1] - m_me) * i_me
        dq_rows += share * (terms[2 * i] - d_me * terms[2 * i + 1])
    spot = spot_ref[...]
    offsets.wait()
    writes = []

    def spread(left, array, rows):
        near = own[16 * array : 16 * array + 16, :]
        high = rows.astype(BF16).astype(F32)
        left = jnp.concatenate([left, spot], axis=0).T.astype(BF16)
        parts = (near, far[16 * array : 16 * array + 16, :], high, rows - high)
        return left, jnp.concatenate([block_rows(part, heads) for part in parts], axis=0)

    for index, (base, out, out_ref, left, right) in enumerate(
        (
            (dki, dko, dk_ref) + spread(ds_two, 0, dk_rows),
            (dvi, dvo, dv_ref) + spread(p_two, 1, dv_rows),
        )
    ):
        back = slice(index * half, (index + 1) * half)
        for j, chunk in enumerate(chunks):
            for h in (2 * j, 2 * j + 1):
                cols = slice(h * dh, (h + 1) * dh)
                pick = iota((length, half), 0) == 2 * iota((length, half), 1) + off_ref[0, h]
                added = dot_nn(left, right[:, cols]) + dot_nn(pick.astype(BF16), ret[back, cols])
                out[:, cols] = (base[:, cols] + added).astype(BF16)
            sem = write_sems.at[index, j]
            copy = pltpu.make_async_copy(out.at[:, chunk], out_ref.at[:, chunk], sem)
            copy.start()
            writes.append(copy)
    for h in range(heads):
        here = iota((16, dh), 0) == jnp.bitwise_and(off_ref[1, h], 15)
        block = jnp.where(here, dq_rows[h : h + 1, :], blocks_in[h].astype(F32))
        blocks[h] = block.astype(BF16)
        copy = pltpu.make_async_copy(blocks.at[h], place(dq_ref, h), block_sems.at[h])
        copy.start()
        writes.append(copy)
    for copy in writes:
        copy.wait()


def on_device(query, key, value, grad_out, offsets):
    length, width = query.shape
    heads = offsets.shape[1]
    dh = width // heads
    size = lax.axis_size("ctx")
    span = min(size, 128)
    slots = 2 * heads + STAT_ROWS
    mates = [(i, i ^ 1) for i in range(size)]
    vmem = pl.BlockSpec(memory_space=pltpu.VMEM)
    smem = pl.BlockSpec(memory_space=pltpu.SMEM)
    hbm = pl.BlockSpec(memory_space=pltpu.HBM)
    params = pltpu.CompilerParams(vmem_limit_bytes=VMEM_LIMIT)
    small = pl.CostEstimate(flops=1000, bytes_accessed=1000, transcendentals=0)
    large = pl.CostEstimate(flops=7 * 10**9, bytes_accessed=1000, transcendentals=0)

    def call(kernel, name, out_shape, in_specs, out_specs, scratch, cost=small, **kwargs):
        return pl.pallas_call(
            kernel,
            out_shape=out_shape,
            in_specs=in_specs,
            out_specs=out_specs,
            scratch_shapes=scratch,
            compiler_params=params,
            cost_estimate=cost,
            name=name,
            **kwargs,
        )

    def far_memory(*arrays):
        return [pltpu.with_memory_space_constraint(array, pltpu.HBM) for array in arrays]

    def near_memory(*arrays):
        return [pltpu.with_memory_space_constraint(array, pltpu.VMEM) for array in arrays]

    query_far = lax.ppermute(query, "ctx", mates)
    grad_far = lax.ppermute(grad_out, "ctx", mates)
    table = pltpu.VMEM((32, length), F32)
    own, spot, weight = call(
        functools.partial(pack_kernel, heads),
        "pack_rows",
        (pltpu.VMEM((32, dh), BF16), table, table),
        [smem] + [hbm] * 2,
        (vmem,) * 3,
        [
            pltpu.VMEM((2 * heads, 16, dh), BF16),
            pltpu.VMEM((32, dh), F32),
            pltpu.SemaphoreType.DMA((2 * heads,)),
        ],
        cost=large,
    )(*far_memory(offsets, query, grad_out))
    key_later, value_later, own = lax.optimization_barrier((key, value, own))
    key_far = lax.ppermute(key_later, "ctx", mates)
    value_far = lax.ppermute(value_later, "ctx", mates)
    repeat = min(span, 32)
    load, s_rows, dp_rows, far = call(
        functools.partial(stats_kernel, heads, span),
        "row_stats",
        (
            pltpu.HBM((span * slots, dh), BF16),
            pltpu.HBM((32, length), F32),
            pltpu.HBM((32, length), F32),
            pltpu.HBM((32, dh), BF16),
        ),
        [vmem] * 7,
        (hbm,) * 4,
        [
            table,
            table,
            pltpu.VMEM((32, dh), BF16),
            pltpu.VMEM((2 * slots, dh), F32),
            pltpu.VMEM((repeat * slots, dh), BF16),
            pltpu.SemaphoreType.DMA((span // repeat,)),
            pltpu.SemaphoreType.DMA((3,)),
        ],
    )(*near_memory(own, spot, weight, query_far, grad_far, key, value))
    groups = None
    if size > span:
        groups = [list(range(base, base + span)) for base in range(0, size, span)]
    received = lax.all_to_all(load, "ctx", 0, 0, axis_index_groups=groups, tiled=True)
    whole = pltpu.VMEM((length, width), BF16)
    wide = pltpu.VMEM((length, width), F32)
    rows = pltpu.VMEM((32, dh), F32)
    dq, dk, dv, partial, terms, blocks = call(
        functools.partial(main_kernel, heads),
        "near_levels",
        (
            pltpu.HBM((length, width), BF16),
            pltpu.HBM((length, width), F32),
            pltpu.HBM((length, width), F32),
            pltpu.HBM((length, width), BF16),
            pltpu.HBM((80, dh), F32),
            pltpu.HBM((heads, 16, dh), BF16),
        ),
        [hbm] * 4 + [vmem] * 7,
        (hbm,) * 6,
        [
            pltpu.SMEM(offsets.shape, jnp.int32),
            table,
            table,
            whole,
            whole,
            wide,
            wide,
            whole,
            pltpu.VMEM((80, dh), F32),
            pltpu.VMEM((heads, 16, dh), BF16),
            pltpu.SemaphoreType.DMA,
            pltpu.SemaphoreType.DMA,
            pltpu.SemaphoreType.DMA((2,)),
            pltpu.SemaphoreType.DMA,
            pltpu.SemaphoreType.DMA,
            pltpu.SemaphoreType.DMA((heads // 2, 4)),
        ],
        cost=large,
    )(
        *far_memory(offsets, s_rows, dp_rows, value_far),
        *near_memory(own, weight, query, key, value, grad_out, key_far),
    )
    returned = lax.ppermute(partial, "ctx", mates)
    mine, theirs = call(
        functools.partial(wide_kernel, heads, span),
        "third_level",
        (rows, rows),
        [vmem],
        (vmem,) * 2,
        [pltpu.VMEM((span * slots, dh), F32)],
        cost=large,
    )(*near_memory(received))
    got = lax.ppermute(theirs, "ctx", mates)
    return call(
        functools.partial(final_kernel, heads),
        "join",
        (pltpu.HBM((length, width), BF16),) * 3,
        [hbm] + [vmem] * 13 + [hbm],
        (hbm,) * 3,
        [
            pltpu.SMEM(offsets.shape, jnp.int32),
            pltpu.VMEM((64, dh), F32),
            pltpu.VMEM((heads, 16, dh), BF16),
            whole,
            whole,
            pltpu.SemaphoreType.DMA,
            pltpu.SemaphoreType.DMA((heads,)),
            pltpu.SemaphoreType.DMA((2, heads // 2)),
        ],
        input_output_aliases={14: 0},
    )(
        *far_memory(offsets),
        *near_memory(mine, got, own, far, spot, weight, s_rows, dp_rows, terms),
        *near_memory(dk, dv, blocks, returned),
        *far_memory(dq),
    )


def solution(mesh):
    placed = (P("ctx", None), P("ctx", None), P("ctx", None), P("ctx", None), P())
    return jax.shard_map(
        on_device,
        mesh=mesh,
        in_specs=placed,
        out_specs=(P("ctx", None), P("ctx", None), P("ctx", None)),
        check_vma=False,
    )
```

```python
import functools

import jax
import jax.numpy as jnp
from jax import lax
from jax.experimental import pallas as pl
from jax.experimental.pallas import tpu as pltpu
from jax.sharding import PartitionSpec as P

NEG = -1e30
F32 = jnp.float32
BF16 = jnp.bfloat16
STAT_ROWS = 4
VMEM_LIMIT = 16 * 1024 * 1024
LOG2E = 1.4426950408889634


def iota(shape, dim):
    return lax.broadcasted_iota(jnp.int32, shape, dim)


def dot_nt(a, b):
    return lax.dot_general(a, b, (((1,), (1,)), ((), ())), preferred_element_type=F32)


def dot_tn(a, b):
    return lax.dot_general(a, b, (((0,), (0,)), ((), ())), preferred_element_type=F32)


def dot_nn(a, b):
    return lax.dot_general(a, b, (((1,), (0,)), ((), ())), preferred_element_type=F32)


def block_rows(rows, heads):
    row = iota(rows.shape, 0)
    return jnp.concatenate(
        [jnp.where(row == h, rows, 0.0).astype(BF16) for h in range(heads)], axis=1
    )


def own_columns(wide_rows, heads):
    dh = wide_rows.shape[1] // heads
    row = iota((16, dh), 0)
    return sum(
        jnp.where(row == h, wide_rows[:, h * dh : (h + 1) * dh], 0.0) for h in range(heads)
    )


def offset_column(off_ref, level, heads, rows):
    row = jnp.bitwise_and(iota((rows, 1), 0), 15)
    column = jnp.zeros((rows, 1), jnp.int32)
    for h in range(heads):
        column = jnp.where(row == h, off_ref[level, h], column)
    return column


def level_one_keys(off_ref, heads, rows, length):
    pair = offset_column(off_ref, 0, heads, rows)
    wide = offset_column(off_ref, 1, heads, rows)
    lane = iota((rows, length), 1)
    chosen = jnp.bitwise_and(wide, 1) == pair
    return jnp.logical_and(jnp.bitwise_and(lane, 1) == pair, chosen)


def row_weights(off_ref, heads, length):
    both = level_one_keys(off_ref, heads, 32, length).astype(F32)
    return jnp.where(iota((32, length), 0) < 16, 1.0 + both, both)


def pack_kernel(
    heads, off_ref, q_ref, g_ref, out_ref, spot_ref, weight_ref, buf, acc, sems
):
    length, dh = q_ref.shape[0], out_ref.shape[1]
    copies = []
    for s, ref in enumerate((q_ref, g_ref)):
        for h in range(heads):
            base = pl.multiple_of(jnp.bitwise_and(off_ref[1, h], ~15), 16)
            slot = s * heads + h
            copy = pltpu.make_async_copy(
                ref.at[pl.ds(base, 16), pl.ds(h * dh, dh)], buf.at[slot], sems.at[slot]
            )
            copy.start()
            copies.append(copy)
    wide = offset_column(off_ref, 1, heads, 32)
    spot_ref[...] = (iota((32, length), 1) == wide).astype(F32)
    weight_ref[...] = row_weights(off_ref, heads, length)
    acc[...] = jnp.zeros_like(acc)
    row = iota((16, dh), 0)
    for s in range(2):
        for h in range(heads):
            slot = s * heads + h
            copies[slot].wait()
            own = row == jnp.bitwise_and(off_ref[1, h], 15)
            block = jnp.where(own, buf[slot].astype(F32), 0.0)
            acc[16 * s + h : 16 * s + h + 1, :] = jnp.sum(block, axis=0, keepdims=True)
    out_ref[...] = acc[...].astype(BF16)


def stats_kernel(
    heads, span, own_ref, spot_ref, weight_ref, qf_ref, gf_ref, k_ref, v_ref,
    load_ref, s_hbm, dp_hbm, far_hbm, s_ref, dp_ref, far_ref, acc, load, sems, row_sems,
):
    dh = own_ref.shape[1]
    part, slots = heads // 2, load_ref.shape[0] // span
    own = own_ref[...].astype(F32)
    spot = spot_ref[0:16, :].astype(BF16)

    def both_rows(whole, first):
        picked = dot_nn(spot, whole)
        far_ref[first : first + 16, :] = own_columns(picked, heads).astype(BF16)
        diagonal = iota(picked.shape, 1) // dh == iota(picked.shape, 0)
        far = jnp.where(diagonal, picked, 0.0).astype(BF16)
        return jnp.concatenate([block_rows(own[first : first + 16, :], heads), far], axis=0)

    queries, grads = both_rows(qf_ref[...], 0), both_rows(gf_ref[...], 16)
    s = dot_nt(queries, k_ref[...]) * (dh**-0.5 * LOG2E)
    dp = dot_nt(grads, v_ref[...])
    s_ref[...] = s
    dp_ref[...] = dp
    early = []
    for i, (near, away) in enumerate(((s_ref, s_hbm), (dp_ref, dp_hbm), (far_ref, far_hbm))):
        copy = pltpu.make_async_copy(near, away, row_sems.at[i])
        copy.start()
        early.append(copy)
    rows = [own_columns(dot_nn(spot, ref[...]), heads) for ref in (k_ref, v_ref)]
    rows += [own[0:16, :], own[16:32, :]]
    for i in range(4):
        for c in range(2):
            slot = c * slots + i * part
            acc[slot : slot + part, :] = rows[i][c * part : (c + 1) * part, :]
    weight = weight_ref[...]
    masked = jnp.where(weight > 0.0, s, NEG)
    m = jnp.max(masked, axis=1, keepdims=True)
    e = jnp.exp2(masked - m) * weight
    t = jnp.sum(e, axis=1, keepdims=True)
    d = jnp.sum(e * dp, axis=1, keepdims=True)
    lane = iota((32, 128), 1)
    table = jnp.where(lane == 0, m, jnp.where(lane == 1, t, jnp.where(lane == 2, d, 0.0)))
    table = jnp.concatenate([table, jnp.zeros((96, 128), F32)], axis=0).T[0:STAT_ROWS, :]
    high = table.astype(BF16).astype(F32)
    rest = table - high
    middle = rest.astype(BF16).astype(F32)
    low = (rest - middle).astype(BF16).astype(F32)
    table = high + pltpu.roll(middle, 32, 1) + pltpu.roll(low, 64, 1)
    for c in range(2):
        acc[c * slots + 4 * part : (c + 1) * slots, :] = table
    halves = acc[...].astype(BF16)
    stride = load.shape[0]
    for i in range(stride // (2 * slots)):
        load[2 * i * slots : 2 * (i + 1) * slots, :] = halves
    copies = [
        pltpu.make_async_copy(load, load_ref.at[pl.ds(i * stride, stride), :], sems.at[i])
        for i in range(span * slots // stride)
    ]
    for copy in copies:
        copy.start()
    for copy in copies + early:
        copy.wait()


def near_head(off_ref, h, inputs, outputs, waits, send):
    q_ref, k_ref, v_ref, g_ref, kf_ref, vf_ref = inputs
    dq_ref, dk_ref, dv_ref, ret_ref = outputs
    length, dh = q_ref.shape[0], q_ref.shape[1] // off_ref.shape[1]
    half = length // 2
    scale = dh**-0.5
    cols = slice(h * dh, (h + 1) * dh)
    q, k, v, g = q_ref[:, cols], k_ref[:, cols], v_ref[:, cols], g_ref[:, cols]
    if h == 0:
        s1, dp1 = dot_nt(k, q), dot_nt(v, g)
        waits[0].wait()
    pair, wide = off_ref[0, h], off_ref[1, h]
    pick = (iota((half, length), 1) == 2 * iota((half, length), 0) + pair).astype(BF16)
    kc = dot_nn(pick, kf_ref[:, cols]).astype(BF16)
    yield
    lanes = iota((1, length), 1)
    chosen = jnp.bitwise_and(lanes, 1) == pair
    a_t = chosen.astype(F32)
    a_u = (jnp.bitwise_and(iota((length, 1), 0), 1) == pair).astype(F32)
    if h > 0:
        s1 = dot_nt(k, q)
    s2 = dot_nt(kc, q) + jnp.where(chosen, 0.0, NEG)
    if h == 0:
        waits[1].wait()
    vc = dot_nn(pick, vf_ref[:, cols]).astype(BF16)
    yield
    m = jnp.maximum(jnp.max(s1, axis=0, keepdims=True), jnp.max(s2, axis=0, keepdims=True))
    m = m * (scale * LOG2E)
    if h > 0:
        dp1 = dot_nt(v, g)
    dp2 = dot_nt(vc, g)
    yield
    e1 = jnp.exp2(s1 * (scale * LOG2E) - m) * (1.0 + a_t * a_u)
    e2 = jnp.exp2(s2 * (scale * LOG2E) - m)
    total = jnp.sum(e1, axis=0, keepdims=True) + jnp.sum(e2, axis=0, keepdims=True)
    part = jnp.sum(e1 * dp1, axis=0, keepdims=True) + jnp.sum(e2 * dp2, axis=0, keepdims=True)
    yield
    inverse = jnp.where(lanes == wide, 0.0, 1.0 / total)
    delta = part * inverse
    p1 = e1 * inverse
    p2 = e2 * inverse
    ds1 = (scale * p1 * (dp1 - delta)).astype(BF16)
    ds2 = (scale * p2 * (dp2 - delta)).astype(BF16)
    p1 = p1.astype(BF16)
    p2 = p2.astype(BF16)
    yield
    dk_ref[:, cols] = dot_nn(ds1, q)
    dv_ref[:, cols] = dot_nn(p1, g)
    ret_ref[:half, cols] = dot_nn(ds2, q).astype(BF16)
    ret_ref[half:, cols] = dot_nn(p2, g).astype(BF16)
    dq_ref[:, cols] = (dot_tn(k, ds1) + dot_tn(kc, ds2)).T.astype(BF16)
    send(h)
    yield


def row_terms(heads, scores, products, weight, keys):
    masked = jnp.where(weight > 0.0, scores, NEG)
    peak = jnp.max(masked, axis=1, keepdims=True)
    e = jnp.exp2(masked - peak) * weight
    parts = []
    for x in (e * products, e):
        high = x.astype(BF16)
        parts += [high, (x - high.astype(F32)).astype(BF16)]
    sums = dot_nn(jnp.concatenate(parts, axis=0), keys)
    first = own_columns(sums[0:16, :] + sums[16:32, :], heads)
    second = own_columns(sums[32:48, :] + sums[48:64, :], heads)
    return first, second, peak


def main_kernel(
    heads, off_hbm, s_hbm, dp_hbm, vf_hbm, own_ref, weight_ref, q_ref, k_ref, v_ref, g_ref, kf_ref,
    dq_hbm, dk_hbm, dv_hbm, ret_hbm, terms_hbm, blocks_hbm,
    off_ref, s_ref, dp_ref, vf_ref, dq_ref, dk_ref, dv_ref, ret_ref, terms, blocks,
    off_sem, in_sem, row_sems, terms_sem, block_sem, out_sems,
):
    offsets = pltpu.make_async_copy(off_hbm, off_ref, off_sem)
    offsets.start()
    values = pltpu.make_async_copy(vf_hbm, vf_ref, in_sem)
    values.start()
    stats = [
        pltpu.make_async_copy(s_hbm, s_ref, row_sems.at[0]),
        pltpu.make_async_copy(dp_hbm, dp_ref, row_sems.at[1]),
    ]
    for copy in stats:
        copy.start()
    dh = q_ref.shape[1] // heads
    near = (dq_ref, dk_ref, dv_ref, ret_ref)
    writes = []

    def send(h):
        base = pl.multiple_of(jnp.bitwise_and(off_ref[1, h], ~15), 16)
        blocks[h] = dq_ref[pl.ds(base, 16), h * dh : (h + 1) * dh]
        if h == heads - 1:
            copy = pltpu.make_async_copy(blocks, blocks_hbm, block_sem)
            copy.start()
            writes.append(copy)
        if h % 2 == 1:
            cols = slice((h - 1) * dh, (h + 1) * dh)
            for i, (a, b) in enumerate(zip(near, (dq_hbm, dk_hbm, dv_hbm, ret_hbm))):
                sem = out_sems.at[h // 2, i]
                copy = pltpu.make_async_copy(a.at[:, cols], b.at[:, cols], sem)
                copy.start()
                writes.append(copy)

    inputs = (q_ref, k_ref, v_ref, g_ref, kf_ref, vf_ref)
    work = [near_head(off_ref, h, inputs, near, (offsets, values), send) for h in range(heads)]
    steps, lag = 6, 2
    for turn in range(steps + lag * (heads - 1)):
        for h in reversed(range(heads)):
            if 0 <= turn - lag * h < steps:
                next(work[h])
        if turn == steps:
            own = own_ref[...].astype(F32)
            queries, grads = block_rows(own[:16, :], heads), block_rows(own[16:, :], heads)
            far_s = dot_nt(queries, kf_ref[...]) * (dh**-0.5 * LOG2E)
            far_dp = dot_nt(grads, vf_ref[...])
            for copy in stats:
                copy.wait()
            weight = weight_ref[0:16, :]
            met = (weight > 1.0).astype(F32)
            near_row = row_terms(heads, s_ref[0:16, :], dp_ref[0:16, :], weight, k_ref[...])
            far_row = row_terms(heads, far_s, far_dp, met, kf_ref[...])
            lane = iota((16, dh), 1)
            peaks = jnp.where(lane == 0, near_row[2], jnp.where(lane == 1, far_row[2], 0.0))
            for i, term in enumerate(near_row[:2] + far_row[:2] + (peaks,)):
                terms[16 * i : 16 * i + 16, :] = term
            copy = pltpu.make_async_copy(terms, terms_hbm, terms_sem)
            copy.start()
            writes.append(copy)
    for copy in writes:
        copy.wait()


def wide_kernel(
    heads, span, recv_ref, mine_ref, theirs_ref, flat
):
    part, slots, dh = heads // 2, recv_ref.shape[0] // span, recv_ref.shape[1]
    scale = dh**-0.5
    me = lax.rem(lax.axis_index("ctx"), span)
    mate = jnp.bitwise_xor(me, 1)
    first = jnp.bitwise_and(me, 1) == 0
    flat[...] = recv_ref[...].astype(F32)

    def gathered(slot):
        return flat[pl.ds(slot, span, stride=slots), :]

    even = jnp.bitwise_and(iota((8, 128), 1), 1) == 0

    def stat(index):
        x = gathered(4 * part + index)
        x = x + pltpu.roll(x, 96, 1) + pltpu.roll(x, 64, 1)
        if span < 128:
            x = jnp.concatenate([x, jnp.zeros((128 - span, 128), F32)], axis=0)
        x = x.T
        near = jnp.where(first, x[0:8, :], x[part : part + 8, :])
        other = jnp.where(first, x[16:24, :], x[16 + part : 24 + part, :])
        other = jnp.where(even, pltpu.roll(other, 127, 1), pltpu.roll(other, 1, 1))
        return near[:, :span], other[:, :span]

    (m_a, m_b), (t_a, t_b), (d_a, d_b) = stat(0), stat(1), stat(2)
    row = iota((16, span), 0)
    device = iota((span, 1), 0)
    k_w, v_w, q_w, g_w = [
        [gathered(i * part + j).astype(BF16) for j in range(part)] for i in range(4)
    ]
    m_c, t_c, d_c = [jnp.zeros((8, span), F32) for _ in range(3)]
    s_key, dp_key, s_row, dp_row = [jnp.zeros((16, span), F32) for _ in range(4)]

    def two_rows(x, j, table):
        for index, device_of in enumerate((me, mate)):
            one = jnp.sum(jnp.where(device == device_of, x, 0.0), axis=0, keepdims=True)
            table = jnp.where(row == 8 * index + j, one, table)
        return table

    for j in range(part):
        s = dot_nt(k_w[j], q_w[j]) * (scale * LOG2E)
        dp = dot_nt(v_w[j], g_w[j])
        m = jnp.max(s, axis=0, keepdims=True)
        e = jnp.exp2(s - m)
        here = row[:8] == j
        m_c = jnp.where(here, m, m_c)
        t_c = jnp.where(here, jnp.sum(e, axis=0, keepdims=True), t_c)
        d_c = jnp.where(here, jnp.sum(e * dp, axis=0, keepdims=True), d_c)
        s_key = two_rows(s, j, s_key)
        dp_key = two_rows(dp, j, dp_key)
        s_row = two_rows(dot_nt(q_w[j], k_w[j]) * (scale * LOG2E), j, s_row)
        dp_row = two_rows(dot_nt(g_w[j], v_w[j]), j, dp_row)
    m_all = jnp.maximum(jnp.maximum(m_a, m_b), m_c)
    w_a, w_b, w_c = jnp.exp2(m_a - m_all), jnp.exp2(m_b - m_all), jnp.exp2(m_c - m_all)
    inverse = 1.0 / (t_a * w_a + t_b * w_b + t_c * w_c)
    delta = (d_a * w_a + d_b * w_b + d_c * w_c) * inverse

    def twice(x):
        return jnp.concatenate([x, x], axis=0)

    def column(x, index):
        return jnp.sum(jnp.where(iota((8, span), 1) == index, x, 0.0), axis=1, keepdims=True)

    p_key = jnp.exp2(s_key - twice(m_all)) * twice(inverse)
    ds_key = scale * p_key * (dp_key - twice(delta))
    of_me = [column(x, me) for x in (m_all, inverse, delta)]
    of_mate = [column(x, mate) for x in (m_all, inverse, delta)]
    m_r, i_r, d_r = [jnp.concatenate(pair, axis=0) for pair in zip(of_me, of_mate)]
    ds_row = scale * (jnp.exp2(s_row - m_r) * i_r) * (dp_row - d_r)

    def times(left, right):
        index = jnp.bitwise_and(row, 7)
        return sum(
            dot_nn(jnp.where(index == j, left, 0.0).astype(BF16), right[j]) for j in range(part)
        )

    terms = (times(ds_row, k_w), times(ds_key, q_w), times(p_key, g_w))
    lane = iota((8, dh), 1)
    for ref, base, columns in ((mine_ref, 0, of_me + of_mate), (theirs_ref, 8, of_mate + of_me)):
        for i, term in enumerate(terms):
            ref[8 * i : 8 * i + 8, :] = term[base : base + 8, :]
        table = jnp.zeros((8, dh), F32)
        for i, value in enumerate(columns):
            table = jnp.where(lane == i, value, table)
        ref[24:32, :] = table


def final_kernel(
    heads, off_hbm, mine_ref, got_ref, own_ref, far_ref, spot_ref, weight_ref, s_ref, dp_ref,
    terms_ref, dki, dvi, blocks_in, ret, dq_in, dq_ref, dk_ref, dv_ref,
    off_ref, full, blocks, dko, dvo, off_sem, block_sems, write_sems,
):
    offsets = pltpu.make_async_copy(off_hbm, off_ref, off_sem)
    offsets.start()
    length, dh = dki.shape[0], own_ref.shape[1]
    half, part = length // 2, heads // 2
    scale = dh**-0.5

    def place(ref, h):
        base = pl.multiple_of(jnp.bitwise_and(off_ref[1, h], ~15), 16)
        return ref.at[pl.ds(base, 16), pl.ds(h * dh, dh)]

    chunks = [slice(2 * j * dh, 2 * (j + 1) * dh) for j in range(part)]
    own, far = own_ref[...].astype(F32), far_ref[...].astype(F32)
    first = jnp.bitwise_and(lax.axis_index("ctx"), 1) == 0
    mine, got = mine_ref[...], got_ref[...]
    low, high = jnp.where(first, mine, got), jnp.where(first, got, mine)
    full[...] = jnp.zeros_like(full)
    for i in range(4):
        full[16 * i : 16 * i + part, :] = low[8 * i : 8 * i + part, :]
        full[16 * i + part : 16 * i + heads, :] = high[8 * i : 8 * i + part, :]
    dq_wide, dk_rows, dv_rows, table = [full[16 * i : 16 * i + 16, :] for i in range(4)]
    m_me, i_me, d_me = [table[:, i : i + 1] for i in range(3)]
    m_two, i_two, d_two = [
        jnp.concatenate([table[:, i : i + 1], table[:, i + 3 : i + 4]], axis=0) for i in range(3)
    ]
    weight = weight_ref[...]
    p_two = jnp.exp2(jnp.where(weight > 0.0, s_ref[...] - m_two, NEG)) * weight * i_two
    ds_two = scale * p_two * (dp_ref[...] - d_two)
    terms = [terms_ref[16 * i : 16 * i + 16, :] for i in range(5)]
    dq_rows = dq_wide
    for i in range(2):
        share = scale * jnp.exp2(terms[4][:, i : i + 1] - m_me) * i_me
        dq_rows += share * (terms[2 * i] - d_me * terms[2 * i + 1])
    spot = spot_ref[...]
    offsets.wait()
    writes = []

    def spread(left, array, rows):
        near = own[16 * array : 16 * array + 16, :]
        high = rows.astype(BF16).astype(F32)
        left = jnp.concatenate([left, spot], axis=0).T.astype(BF16)
        parts = (near, far[16 * array : 16 * array + 16, :], high, rows - high)
        return left, jnp.concatenate([block_rows(part, heads) for part in parts], axis=0)

    for index, (base, out, out_ref, left, right) in enumerate(
        (
            (dki, dko, dk_ref) + spread(ds_two, 0, dk_rows),
            (dvi, dvo, dv_ref) + spread(p_two, 1, dv_rows),
        )
    ):
        back = slice(index * half, (index + 1) * half)
        for j, chunk in enumerate(chunks):
            added = base[:, chunk] + dot_nn(left, right[:, chunk])
            for h in (2 * j, 2 * j + 1):
                cols = slice(h * dh, (h + 1) * dh)
                mine_part = slice((h - 2 * j) * dh, (h - 2 * j + 1) * dh)
                pick = iota((length, half), 0) == 2 * iota((length, half), 1) + off_ref[0, h]
                back_part = dot_nn(pick.astype(BF16), ret[back, cols])
                out[:, cols] = (added[:, mine_part] + back_part).astype(BF16)
            sem = write_sems.at[index, j]
            copy = pltpu.make_async_copy(out.at[:, chunk], out_ref.at[:, chunk], sem)
            copy.start()
            writes.append(copy)
    for h in range(heads):
        here = iota((16, dh), 0) == jnp.bitwise_and(off_ref[1, h], 15)
        block = jnp.where(here, dq_rows[h : h + 1, :], blocks_in[h].astype(F32))
        blocks[h] = block.astype(BF16)
        copy = pltpu.make_async_copy(blocks.at[h], place(dq_ref, h), block_sems.at[h])
        copy.start()
        writes.append(copy)
    for copy in writes:
        copy.wait()


def on_device(query, key, value, grad_out, offsets):
    length, width = query.shape
    heads = offsets.shape[1]
    dh = width // heads
    size = lax.axis_size("ctx")
    span = min(size, 128)
    slots = 2 * heads + STAT_ROWS
    mates = [(i, i ^ 1) for i in range(size)]
    vmem = pl.BlockSpec(memory_space=pltpu.VMEM)
    smem = pl.BlockSpec(memory_space=pltpu.SMEM)
    hbm = pl.BlockSpec(memory_space=pltpu.HBM)
    params = pltpu.CompilerParams(vmem_limit_bytes=VMEM_LIMIT)
    small = pl.CostEstimate(flops=1000, bytes_accessed=1000, transcendentals=0)
    large = pl.CostEstimate(flops=7 * 10**9, bytes_accessed=1000, transcendentals=0)

    def call(kernel, name, out_shape, in_specs, out_specs, scratch, cost=small, **kwargs):
        return pl.pallas_call(
            kernel,
            out_shape=out_shape,
            in_specs=in_specs,
            out_specs=out_specs,
            scratch_shapes=scratch,
            compiler_params=params,
            cost_estimate=cost,
            name=name,
            **kwargs,
        )

    def far_memory(*arrays):
        return [pltpu.with_memory_space_constraint(array, pltpu.HBM) for array in arrays]

    def near_memory(*arrays):
        return [pltpu.with_memory_space_constraint(array, pltpu.VMEM) for array in arrays]

    query_far = lax.ppermute(query, "ctx", mates)
    grad_far = lax.ppermute(grad_out, "ctx", mates)
    table = pltpu.VMEM((32, length), F32)
    own, spot, weight = call(
        functools.partial(pack_kernel, heads),
        "pack_rows",
        (pltpu.VMEM((32, dh), BF16), table, table),
        [smem] + [hbm] * 2,
        (vmem,) * 3,
        [
            pltpu.VMEM((2 * heads, 16, dh), BF16),
            pltpu.VMEM((32, dh), F32),
            pltpu.SemaphoreType.DMA((2 * heads,)),
        ],
        cost=large,
    )(*far_memory(offsets, query, grad_out))
    key_later, value_later, own = lax.optimization_barrier((key, value, own))
    key_far = lax.ppermute(key_later, "ctx", mates)
    value_far = lax.ppermute(value_later, "ctx", mates)
    repeat = min(span, 32)
    load, s_rows, dp_rows, far = call(
        functools.partial(stats_kernel, heads, span),
        "row_stats",
        (
            pltpu.HBM((span * slots, dh), BF16),
            pltpu.HBM((32, length), F32),
            pltpu.HBM((32, length), F32),
            pltpu.HBM((32, dh), BF16),
        ),
        [vmem] * 7,
        (hbm,) * 4,
        [
            table,
            table,
            pltpu.VMEM((32, dh), BF16),
            pltpu.VMEM((2 * slots, dh), F32),
            pltpu.VMEM((repeat * slots, dh), BF16),
            pltpu.SemaphoreType.DMA((span // repeat,)),
            pltpu.SemaphoreType.DMA((3,)),
        ],
    )(*near_memory(own, spot, weight, query_far, grad_far, key, value))
    groups = None
    if size > span:
        groups = [list(range(base, base + span)) for base in range(0, size, span)]
    received = lax.all_to_all(load, "ctx", 0, 0, axis_index_groups=groups, tiled=True)
    whole = pltpu.VMEM((length, width), BF16)
    wide = pltpu.VMEM((length, width), F32)
    rows = pltpu.VMEM((32, dh), F32)
    dq, dk, dv, partial, terms, blocks = call(
        functools.partial(main_kernel, heads),
        "near_levels",
        (
            pltpu.HBM((length, width), BF16),
            pltpu.HBM((length, width), F32),
            pltpu.HBM((length, width), F32),
            pltpu.HBM((length, width), BF16),
            pltpu.HBM((80, dh), F32),
            pltpu.HBM((heads, 16, dh), BF16),
        ),
        [hbm] * 4 + [vmem] * 7,
        (hbm,) * 6,
        [
            pltpu.SMEM(offsets.shape, jnp.int32),
            table,
            table,
            whole,
            whole,
            wide,
            wide,
            whole,
            pltpu.VMEM((80, dh), F32),
            pltpu.VMEM((heads, 16, dh), BF16),
            pltpu.SemaphoreType.DMA,
            pltpu.SemaphoreType.DMA,
            pltpu.SemaphoreType.DMA((2,)),
            pltpu.SemaphoreType.DMA,
            pltpu.SemaphoreType.DMA,
            pltpu.SemaphoreType.DMA((heads // 2, 4)),
        ],
        cost=large,
    )(
        *far_memory(offsets, s_rows, dp_rows, value_far),
        *near_memory(own, weight, query, key, value, grad_out, key_far),
    )
    returned = lax.ppermute(partial, "ctx", mates)
    mine, theirs = call(
        functools.partial(wide_kernel, heads, span),
        "third_level",
        (rows, rows),
        [vmem],
        (vmem,) * 2,
        [pltpu.VMEM((span * slots, dh), F32)],
        cost=large,
    )(*near_memory(received))
    got = lax.ppermute(theirs, "ctx", mates)
    return call(
        functools.partial(final_kernel, heads),
        "join",
        (pltpu.HBM((length, width), BF16),) * 3,
        [hbm] + [vmem] * 13 + [hbm],
        (hbm,) * 3,
        [
            pltpu.SMEM(offsets.shape, jnp.int32),
            pltpu.VMEM((64, dh), F32),
            pltpu.VMEM((heads, 16, dh), BF16),
            whole,
            whole,
            pltpu.SemaphoreType.DMA,
            pltpu.SemaphoreType.DMA((heads,)),
            pltpu.SemaphoreType.DMA((2, heads // 2)),
        ],
        input_output_aliases={14: 0},
    )(
        *far_memory(offsets),
        *near_memory(mine, got, own, far, spot, weight, s_rows, dp_rows, terms),
        *near_memory(dk, dv, blocks, returned),
        *far_memory(dq),
    )


def solution(mesh):
    placed = (P("ctx", None), P("ctx", None), P("ctx", None), P("ctx", None), P())
    return jax.shard_map(
        on_device,
        mesh=mesh,
        in_specs=placed,
        out_specs=(P("ctx", None), P("ctx", None), P("ctx", None)),
        check_vma=False,
    )
```
